32 devices in a mesh: grp: 2 (over y), gx: 8 (over z, x), gy: 2 (over core).
Axes of the slice: x: 2, y: 2, z: 4, core: 2. Of those that a mesh axis runs over, the one named last changes fastest.
Arguments:
- misfit: float32 [2, 256, 1536], P(None, ('grp', 'gx'), 'gy'), parts along dimension 1
- velocity: float32 [2, 256, 1536], P(None, ('grp', 'gx'), 'gy'), parts along dimension 1
- viscosity: float32 [256, 1536], P(('grp', 'gx'), 'gy'), parts along dimension 0, may hold values from 0.2 to 2
- friction: float32 [256, 1536], P(('grp', 'gx'), 'gy'), parts along dimension 0, may hold values from 0.2 to 4
- ice: int32 [256, 1536], P(('grp', 'gx'), 'gy'), parts along dimension 0, may hold values 0 or 1
- grounded: int32 [256, 1536], P(('grp', 'gx'), 'gy'), parts along dimension 0, may hold values 0 or 1
- bounds: float32 [8], P('grp'), parts along dimension 0, may hold values from 2.1 to 32, as said below
Outputs:
- multiplier: float32 [2, 256, 1536], P(None, ('grp', 'gx'), 'gy'), parts along dimension 1
- scaled_gradient: float32 [256, 1536], P(('grp', 'gx'), 'gy'), parts along dimension 0
- residual_norm: float32 [2], P('grp'), parts along dimension 0
The draws below stay inside these ranges and needn't reach their ends.
There are 2 independent parts, one for each index of `grp`. The reference program is written for one: setup_inputs(seed, part) draws one part's arguments, and reference() takes and returns one part's arrays. A program takes and returns all parts, laid end to end along the dimension named above; each array names one. Nothing has to cross between parts.
Inputs may be any that keep to these rules, and one draw needn't show every extreme that they name: bounds holds a lower and an upper bound for the fine grid, then for the coarse grid; each lower bound is under its upper bound.
All inputs are finite; a program needn't handle non-finite values. No bound on the sum of `ice` or of `grounded` on one device may be relied on, other than what follows from the above.
Results may differ from the reference program's by a relative error of at most 0.0003.
Values sent between devices are 32-bit elements; how exact they have to be, the bound alone decides.
No kernel may reach another device: no remote copies, remote signals or barrier semaphores. Data moves between devices by JAX's collectives and lax.ppermute only.
A program may use at most 64 MiB of HBM per device.

```python
import math
import jax
import jax.numpy as jnp
from jax import lax

DEG = 4
NX = 128
NY = 1536


def rising(count):
    return 1.0 + 2.0 * jnp.arange(count, dtype=jnp.float32) / max(count - 1, 1)


def draw_misfit(key, part):
    key = jax.random.fold_in(key, 11)
    ramp = rising(NX)[None, :, None]
    return jax.random.normal(key, (2, NX, NY), jnp.float32) * ramp


def draw_velocity(key, part):
    key = jax.random.fold_in(key, 12)
    ramp = rising(NX)[None, :, None]
    return jax.random.normal(key, (2, NX, NY), jnp.float32) * ramp


def draw_bounds(key, part):
    key = jax.random.fold_in(key, 13)
    keys = jax.random.split(key, 4)
    fine_top = jax.random.uniform(keys[0], (), jnp.float32, 14.0, 18.0)
    fine_low = fine_top * jax.random.uniform(keys[1], (), jnp.float32, 0.15, 0.3)
    coarse_top = jax.random.uniform(keys[2], (), jnp.float32, 24.0, 32.0)
    coarse_low = coarse_top * jax.random.uniform(keys[3], (), jnp.float32, 0.1, 0.2)
    return jnp.stack([fine_low, fine_top, coarse_low, coarse_top])


def with_ends(array, stream_key, smallest, top_value):
    longest = array.shape.index(max(array.shape))
    spots = []
    for shift in (0, 1):
        where = [jax.random.randint(jax.random.fold_in(stream_key, axis), (), 0, length) for axis, length in enumerate(array.shape)]
        where[longest] = (where[longest] + shift) % array.shape[longest]
        spots.append(tuple(where))
    return array.at[spots[0]].set(smallest).at[spots[1]].set(top_value)


def block_levels(key, shape, cuts, least, high):
    factor_of, own = 1.0, jax.random.fold_in(key, 6)
    for axis_at, parts in cuts:
        draws = jnp.exp(jax.random.uniform(jax.random.fold_in(own, axis_at), (parts,), jnp.float32, least / len(cuts), high / len(cuts)))
        factor_of = factor_of * jnp.repeat(draws, shape[axis_at] // parts).reshape([-1 if axis == axis_at else 1 for axis in range(len(shape))])
    return factor_of


def setup_inputs(seed: int = 0, part: int = 0) -> dict:
    key_list = jax.random.split(jax.random.key(seed), 8)
    own_keys = jax.random.split(jax.random.fold_in(key_list[7], part), 8)
    return {
        "misfit": draw_misfit(jax.random.fold_in(jax.random.fold_in(key_list[7], part), 71), part),
        "velocity": draw_velocity(jax.random.fold_in(jax.random.fold_in(key_list[7], part), 71), part),
        "viscosity": jnp.clip(jnp.exp(math.log(2.0) - 2.3025851 * jax.random.uniform(own_keys[2], (NX, NY), jnp.float32) ** block_levels(own_keys[2], (NX, NY), ((0, 8), (1, 2)), -0.2, 0.2)), 0.2, 2.0),
        "friction": jnp.clip(jnp.exp(math.log(4.0) - 2.9957323 * jax.random.uniform(own_keys[3], (NX, NY), jnp.float32) ** block_levels(own_keys[3], (NX, NY), ((0, 8), (1, 2)), -0.2, 0.2)), 0.2, 4.0),
        "ice": with_ends((jax.random.randint(own_keys[4], (NX, NY), 0, 10) < 9).astype(jnp.int32), jax.random.fold_in(own_keys[4], 1), 0, 1),
        "grounded": with_ends((jax.random.randint(own_keys[5], (NX, NY), 0, 2) < 1).astype(jnp.int32), jax.random.fold_in(own_keys[5], 1), 0, 1),
        "bounds": draw_bounds(jax.random.fold_in(jax.random.fold_in(key_list[7], part), 71), part),
    }


def apply_stencil(bordered, border_visc, beta):
    stiffness = 0.25 * (border_visc[:-1, :-1] + border_visc[1:, :-1] + border_visc[:-1, 1:] + border_visc[1:, 1:])
    low_low = bordered[:, :-1, :-1]
    high_low = bordered[:, 1:, :-1]
    low_high = bordered[:, :-1, 1:]
    high_high = bordered[:, 1:, 1:]
    along_x = 0.5 * (high_low + high_high - low_low - low_high)
    along_y = 0.5 * (low_high + high_high - low_low - high_low)
    normal_x = stiffness * (4.0 * along_x[0] + 2.0 * along_y[1])
    normal_y = stiffness * (4.0 * along_y[1] + 2.0 * along_x[0])
    shear_term = stiffness * (along_y[0] + along_x[1])
    force_x = jnp.stack([normal_x, shear_term])
    force_y = jnp.stack([shear_term, normal_y])
    corner_a = -0.5 * (force_x + force_y)
    corner_b = 0.5 * (force_x - force_y)
    corner_c = 0.5 * (force_y - force_x)
    corner_d = 0.5 * (force_x + force_y)
    centre = bordered[:, 1:-1, 1:-1]
    total = corner_a[:, 1:, 1:] + corner_b[:, :-1, 1:] + corner_c[:, 1:, :-1] + corner_d[:, :-1, :-1]
    return total + beta * centre

def chebyshev(source, operator, lower, upper, inside, final):
    middle = 0.5 * (upper + lower)
    half_width = 0.5 * (upper - lower)
    spread = middle / half_width
    factor = 1.0 / spread
    update = source / middle * inside
    iterate = update
    for step in range(DEG - 1):
        remaining = source - operator(iterate)
        factor_next = 1.0 / (2.0 * spread - factor)
        update = (factor_next * factor * update + 2.0 * factor_next / half_width * remaining) * inside
        iterate = iterate + update
        factor = factor_next
    if final:
        return (iterate, source - operator(iterate))
    return (iterate, iterate)

def reference(misfit, velocity, viscosity, friction, ice, grounded, bounds):
    visc_eff = viscosity * ice.astype(jnp.float32)
    beta_eff = friction * grounded.astype(jnp.float32)
    pad_visc = jnp.pad(visc_eff, 1)

    def fine_apply(iterate):
        return apply_stencil(jnp.pad(iterate, ((0, 0), (1, 1), (1, 1))), pad_visc, beta_eff)
    fine_x, residual = chebyshev(misfit, fine_apply, bounds[0], bounds[1], 1.0, True)
    coarse_source = residual.reshape(2, NX // 2, 2, NY // 2, 2).sum(axis=(2, 4))
    coarse_visc = 0.25 * visc_eff.reshape(NX // 2, 2, NY // 2, 2).sum(axis=(1, 3))
    coarse_beta = beta_eff.reshape(NX // 2, 2, NY // 2, 2).sum(axis=(1, 3))
    coarse_pad = jnp.pad(coarse_visc, 1)

    def coarse_apply(iterate):
        return apply_stencil(jnp.pad(iterate, ((0, 0), (1, 1), (1, 1))), coarse_pad, coarse_beta)
    correction, unused = chebyshev(coarse_source, coarse_apply, bounds[2], bounds[3], 1.0, False)
    multiplier = fine_x + jnp.repeat(jnp.repeat(correction, 2, axis=1), 2, axis=2)
    gradient = -beta_eff * lax.optimization_barrier(jnp.sum(velocity * multiplier, axis=0))
    grad_scale = jnp.sqrt(jnp.sum(gradient * gradient) / (NX * NY) + 1e-06)
    norm_value = jnp.sqrt(jnp.sum(residual * residual) / (2 * NX * NY)).reshape(1)
    return (multiplier, gradient / grad_scale, norm_value)
```

```python
import functools

import jax
import jax.numpy as jnp
from jax import lax
from jax.experimental import pallas as pl
from jax.experimental.pallas import tpu as pltpu
from jax.sharding import PartitionSpec as P

DEG = 4
LANES = 128
SEGS = 8
RIM = 10
EDGE = 16
F32 = jnp.float32
AXES = ("gx", "gy")


def lane_ids():
    return lax.broadcasted_iota(jnp.int32, (8, LANES), 1)


def pack_kernel(misfit, visc, friction, ice, grounded, kb, down_send, up_send, side_send):
    rows, cols = visc.shape
    left = lax.axis_index("gy") == 0
    kb[0] = visc[...] * ice[...].astype(F32)
    kb[1] = friction[...] * grounded[...].astype(F32)
    fields = (misfit.at[0], misfit.at[1], kb.at[0], kb.at[1])
    for n, field in enumerate(fields):
        down_send[8 * n : 8 * n + 8, :] = field[rows - 8 :, :]
        down_send[32 + 2 * n : 34 + 2 * n, :] = field[rows - 10 : rows - 8, :]
        up_send[8 * n : 8 * n + 8, :] = field[:8, :]
        up_send[32 + 2 * n : 34 + 2 * n, :] = field[8:10, :]
        side_send[rows * n : rows * n + rows, :] = jnp.where(
            left, field[:, cols - LANES :], field[:, :LANES]
        )


def spread_rows(blocks, store):
    lanes = lax.broadcasted_iota(jnp.int32, blocks[1].shape, 1)
    for s in range(SEGS):
        start = 96 * s - EDGE
        first = start // LANES
        offset = start - LANES * first
        merged = jnp.where(lanes >= offset, blocks[first + 1], blocks[first + 2])
        store(s, pltpu.roll(merged, LANES - offset, 1))


def main_kernel(
    bounds, misfit, kb, velocity, from_up, from_down, side, side_up, side_down,
    multiplier, gradient, sums,
    fu, fv, kk, bb, cell, xu, xv, du, dv, ru, rv, cfu, cfv, ckk, cbb, ccell, cxu, cxv, cdu, cdv, mu, mv,
):
    rows, cols = gradient.shape
    total = rows + 2 * RIM
    column_blocks = cols // LANES
    gx_at, gx_size = lax.axis_index("gx"), lax.axis_size("gx")
    left = lax.axis_index("gy") == 0

    def spread(ref, base, height, side_block, target, first_row):
        blocks = [ref[base : base + height, LANES * j : LANES * j + LANES] for j in range(column_blocks)]
        zero = jnp.zeros_like(side_block)
        blocks = [jnp.where(left, zero, side_block)] + blocks + [jnp.where(left, side_block, zero)]

        def store(s, value):
            target[pl.ds(first_row * 8 + s, height, stride=8), :] = value

        spread_rows(blocks, store)

    targets = (fu, fv, kk, bb)
    own = (misfit.at[0], misfit.at[1], kb.at[0], kb.at[1])
    for n in range(4):
        for h in range(0, rows, 8):
            spread(own[n], h, 8, side[rows * n + h : rows * n + h + 8, :], targets[n], RIM + h)
    for received, partner, near, far in (
        (from_up, side_up, RIM - 8, 0),
        (from_down, side_down, RIM + rows, RIM + rows + 8),
    ):
        edge = jnp.where(left, partner[:, :LANES], partner[:, cols - LANES :])
        for n in range(4):
            spread(received, 8 * n, 8, edge[8 * n : 8 * n + 8], targets[n], near)
            spread(received, 32 + 2 * n, 2, edge[32 + 2 * n : 34 + 2 * n], targets[n], far)

    lanes = lane_ids()
    column = 96 * lax.broadcasted_iota(jnp.int32, (8, LANES), 0) + lanes - EDGE
    inside = jnp.where(left, (column >= 0).astype(F32), (column < cols).astype(F32))
    above = inside * jnp.where(gx_at > 0, 1.0, 0.0)
    below = inside * jnp.where(gx_at < gx_size - 1, 1.0, 0.0)
    mine = ((lanes >= EDGE) & (lanes < LANES - EDGE)).astype(F32)
    even = lanes % 2 == 0

    def at(ref, row):
        return ref[8 * row : 8 * row + 8, :]

    def put(ref, row, value):
        ref[8 * row : 8 * row + 8, :] = value

    def stiffness(visc, target, count, shift):
        paired = None
        for row in range(count):
            k = at(visc, row)
            now = k + pltpu.roll(k, LANES - shift, 1)
            if row:
                put(target, row - 1, 0.125 * (paired + now))
            paired = now

    def residual(x_u, x_v, f_u, f_v, beta, stiff, low, high, shift, use):
        def gradients(row):
            u, v = at(x_u, row), at(x_v, row)
            ru_, rv_ = pltpu.roll(u, LANES - shift, 1), pltpu.roll(v, LANES - shift, 1)
            return u, v, u + ru_, v + rv_, ru_ - u, rv_ - v

        def forces(row, one, two):
            a, b = two[2] - one[2], two[5] + one[5]
            c, d = two[4] + one[4], two[3] - one[3]
            s = at(stiff, row)
            both = a + b
            return s * (both + a), s * (both + b), (0.5 * s) * (c + d)

        before = gradients(low - 1)
        here = gradients(low)
        cell_before = forces(low - 1, before, here)
        for row in range(low, high):
            after = gradients(row + 1)
            cell_here = forces(row, here, after)
            shear = cell_before[2] + cell_here[2]
            shear_step = cell_before[2] - cell_here[2]
            px, qy = cell_before[0] - cell_here[0], cell_before[1] + cell_here[1]
            au = (px - shear) + pltpu.roll(px + shear, shift, 1)
            av = (shear_step - qy) + pltpu.roll(shear_step + qy, shift, 1)
            u, v = here[0], here[1]
            b = at(beta, row)
            use(row, u, v, at(f_u, row) - au - b * u, at(f_v, row) - av - b * v)
            here, cell_before = after, cell_here

    def sweep(x_u, x_v, d_u, d_v, f_u, f_v, beta, stiff, lower, upper, count, rim, shift):
        lower, upper = jnp.full((8, LANES), lower), jnp.full((8, LANES), upper)
        middle = 0.5 * (upper + lower)
        half = 0.5 * (upper - lower)
        spread_ = middle / half
        factor = 1.0 / spread_
        inverse = 1.0 / middle
        for row in range(count):
            put(x_u, row, at(f_u, row) * inverse)
            put(x_v, row, at(f_v, row) * inverse)
        for step in range(DEG - 1):
            factor_next = 1.0 / (2.0 * spread_ - factor)
            keep = factor_next * factor
            gain = 2.0 * factor_next / half
            gains = (gain * above, gain * inside, gain * below)
            first = step == 0

            def use(row, u, v, gu, gv):
                part = gains[0 if row < rim else 2 if row >= count - rim else 1]
                old_u = u if first else at(d_u, row)
                old_v = v if first else at(d_v, row)
                new_u = keep * old_u + part * gu
                new_v = keep * old_v + part * gv
                put(d_u, row, new_u)
                put(d_v, row, new_v)
                put(x_u, row, u + new_u)
                put(x_v, row, v + new_v)

            residual(x_u, x_v, f_u, f_v, beta, stiff, step + 1, count - step - 1, shift, use)
            factor = factor_next

    stiffness(kk, cell, total, 1)
    sweep(xu, xv, du, dv, fu, fv, bb, cell, bounds[0], bounds[1], total, RIM, 1)

    squares = [jnp.zeros((8, LANES), F32)]

    def keep_residual(row, u, v, gu, gv):
        part = above if row < RIM else below if row >= RIM + rows else inside
        gu, gv = gu * part, gv * part
        put(ru, row, gu)
        put(rv, row, gv)
        if RIM <= row < RIM + rows:
            squares[0] = squares[0] + (gu * gu + gv * gv)

    residual(xu, xv, fu, fv, bb, cell, DEG, total - DEG, 1, keep_residual)

    coarse_rim = (RIM - DEG) // 2
    coarse_rows = rows // 2 + 2 * coarse_rim
    for i in range(coarse_rows):
        row = DEG + 2 * i
        for source, target, scale in ((ru, cfu, None), (rv, cfv, None), (kk, ckk, 0.25), (bb, cbb, None)):
            pair = at(source, row) + at(source, row + 1)
            pair = pair + pltpu.roll(pair, LANES - 1, 1)
            put(target, i, pair if scale is None else scale * pair)
    stiffness(ckk, ccell, coarse_rows, 2)
    sweep(cxu, cxv, cdu, cdv, cfu, cfv, cbb, ccell, bounds[2], bounds[3], coarse_rows, coarse_rim, 2)

    for i in range(rows // 2):
        for fine, coarse, target in ((xu, cxu, mu), (xv, cxv, mv)):
            correction = at(coarse, coarse_rim + i)
            correction = jnp.where(even, correction, pltpu.roll(correction, 1, 1))
            for row in (2 * i, 2 * i + 1):
                put(target, row, at(fine, RIM + row) + correction)

    gradient_squares = jnp.zeros((8, LANES), F32)
    for h in range(0, rows, 8):
        for j in range(column_blocks):
            s = (LANES * j) // 96
            shift = LANES * j - 96 * s + EDGE
            border = 96 * (s + 1) - LANES * j
            columns = slice(LANES * j, LANES * j + LANES)
            product = None
            for n, source in enumerate((mu, mv)):
                one = source[pl.ds(8 * h + s, 8, stride=8), :]
                two = source[pl.ds(8 * h + s + 1, 8, stride=8), :]
                value = jnp.where(
                    lanes < border, pltpu.roll(one, LANES - shift, 1), pltpu.roll(two, (96 - shift) % LANES, 1)
                )
                multiplier[n, h : h + 8, columns] = value
                term = velocity[n, h : h + 8, columns] * value
                product = term if product is None else product + term
            value = -kb[1, h : h + 8, columns] * product
            gradient[h : h + 8, columns] = value
            gradient_squares = gradient_squares + value * value
    residual_squares = jnp.sum(squares[0] * mine, axis=0, keepdims=True)
    gradient_squares = jnp.sum(gradient_squares, axis=0, keepdims=True)
    pair = jnp.concatenate([residual_squares, gradient_squares], axis=1)
    sums[...] = jnp.broadcast_to(pair, sums.shape)


def scale_kernel(nodes, gathered, gradient, scaled, norm):
    residual_total = jnp.sum(gathered[:, :LANES], keepdims=True)
    gradient_total = jnp.sum(gathered[:, LANES:], keepdims=True)
    scaled[...] = gradient[...] / jnp.sqrt(gradient_total / nodes + 1e-06)
    norm[...] = jnp.sqrt(residual_total / (2 * nodes))


def body(misfit, velocity, viscosity, friction, ice, grounded, bounds):
    rows, cols = viscosity.shape
    gx_size, gy_size = lax.axis_size("gx"), lax.axis_size("gy")
    assert gy_size == 2 and cols == 96 * SEGS and rows == 16
    peers = gx_size * gy_size
    nodes = rows * cols * peers
    total = rows + 2 * RIM
    shaped = jax.ShapeDtypeStruct
    whole = pl.BlockSpec(memory_space=pltpu.VMEM)
    params = pltpu.CompilerParams(vmem_limit_bytes=32 * 1024 * 1024)

    kb, down_send, up_send, side_send = pl.pallas_call(
        pack_kernel,
        out_shape=(
            shaped((2, rows, cols), F32),
            shaped((4 * RIM, cols), F32),
            shaped((4 * RIM, cols), F32),
            shaped((4 * rows, LANES), F32),
        ),
        in_specs=[whole] * 5,
        out_specs=[whole] * 4,
        compiler_params=params,
        name="pack",
    )(misfit, viscosity, friction, ice, grounded)

    down = [(i, i + 1) for i in range(gx_size - 1)]
    up = [(j, i) for i, j in down]
    swap = [(0, 1), (1, 0)]
    from_up = lax.ppermute(down_send, "gx", down)
    from_down = lax.ppermute(up_send, "gx", up)
    side = lax.ppermute(side_send, "gy", swap)
    side_up = lax.ppermute(from_up, "gy", swap)
    side_down = lax.ppermute(from_down, "gy", swap)

    fine = pltpu.VMEM((8 * total, LANES), F32)
    coarse = pltpu.VMEM((4 * total, LANES), F32)
    owned = pltpu.VMEM((8 * rows, LANES), F32)
    multiplier, gradient, sums = pl.pallas_call(
        main_kernel,
        out_shape=(
            shaped((2, rows, cols), F32),
            shaped((rows, cols), F32),
            shaped((peers, 2 * LANES), F32),
        ),
        in_specs=[pl.BlockSpec(memory_space=pltpu.SMEM)] + [whole] * 8,
        out_specs=[whole] * 3,
        scratch_shapes=[fine] * 11 + [coarse] * 9 + [owned] * 2,
        compiler_params=params,
        name="leg",
    )(bounds, misfit, kb, velocity, from_up, from_down, side, side_up, side_down)

    gathered = lax.all_to_all(sums, AXES, 0, 0, tiled=True)
    scaled, norm = pl.pallas_call(
        functools.partial(scale_kernel, nodes),
        out_shape=(shaped((rows, cols), F32), shaped((1, 1), F32)),
        in_specs=[whole] * 2,
        out_specs=[whole] * 2,
        compiler_params=params,
        name="scale",
    )(gathered, gradient)
    return multiplier, scaled, norm.reshape(1)


def solution(mesh):
    tile = P(("grp", "gx"), "gy")
    pair = P(None, ("grp", "gx"), "gy")
    return jax.shard_map(
        body,
        mesh=mesh,
        in_specs=(pair, pair, tile, tile, tile, tile, P("grp")),
        out_specs=(pair, tile, P("grp")),
        check_vma=False,
    )
```

```python
import functools

import jax
import jax.numpy as jnp
from jax import lax
from jax.experimental import pallas as pl
from jax.experimental.pallas import tpu as pltpu
from jax.sharding import PartitionSpec as P

DEG = 4
LANES = 128
SEGS = 8
RIM = 10
EDGE = 16
F32 = jnp.float32
AXES = ("gx", "gy")


def lane_ids():
    return lax.broadcasted_iota(jnp.int32, (8, LANES), 1)


def pack_kernel(
    bounds, misfit, visc, friction, ice, grounded,
    fields, coefficients, x_send, z_send, side_send,
    levels, visc_in, friction_in, ice_in, grounded_in, sems,
):
    copies = [
        pltpu.make_async_copy(source, target, sems.at[n])
        for n, (source, target) in enumerate((
            (misfit, fields.at[pl.ds(0, 2)]),
            (visc, visc_in),
            (ice, ice_in),
            (friction, friction_in),
            (grounded, grounded_in),
            (bounds, levels),
        ))
    ]
    for copy in copies:
        copy.start()
    rows, cols = visc.shape
    left = lax.axis_index("gy") == 0
    low_half = lax.axis_index("gx") % 2 == 0
    for copy in copies[:5]:
        copy.wait()
    fields[2] = visc_in[...] * ice_in[...].astype(F32)
    fields[3] = friction_in[...] * grounded_in[...].astype(F32)
    for n in range(4):
        last, first = fields[n, rows - 8 :, :], fields[n, :8, :]
        x_send[8 * n : 8 * n + 8, :] = jnp.where(low_half, last, first)
        z_send[8 * n : 8 * n + 8, :] = jnp.where(low_half, first, last)
        last, first = fields[n, rows - 10 : rows - 8, :], fields[n, 8:10, :]
        x_send[32 + 2 * n : 34 + 2 * n, :] = jnp.where(low_half, last, first)
        z_send[32 + 2 * n : 34 + 2 * n, :] = jnp.where(low_half, first, last)
        side_send[rows * n : rows * n + rows, :] = jnp.where(
            left, fields[n, :, cols - LANES :], fields[n, :, :LANES]
        )
    copies[5].wait()
    for sweep in range(2):
        lower = jnp.full((8, LANES), levels[2 * sweep])
        upper = jnp.full((8, LANES), levels[2 * sweep + 1])
        middle = 0.5 * (upper + lower)
        half = 0.5 * (upper - lower)
        spread = middle / half
        factor = 1.0 / spread
        values = [1.0 / middle]
        for step in range(DEG - 1):
            factor_next = 1.0 / (2.0 * spread - factor)
            values += [factor_next * factor, 2.0 * factor_next / half]
            factor = factor_next
        for n, value in enumerate(values):
            row = 8 * (sweep * (2 * DEG - 1) + n)
            coefficients[row : row + 8, :] = value


def spread_rows(blocks, store):
    lanes = lax.broadcasted_iota(jnp.int32, blocks[1].shape, 1)
    for s in range(SEGS):
        start = 96 * s - EDGE
        first = start // LANES
        offset = start - LANES * first
        merged = jnp.where(lanes >= offset, blocks[first + 1], blocks[first + 2])
        store(s, pltpu.roll(merged, LANES - offset, 1))


def main_kernel(
    coefficients, fields, velocity, from_x, from_z, side, side_x, side_z,
    multiplier, gradient, sums,
    fu, fv, kk, bb, cell, xu, xv, du, dv, ru, rv, cfu, cfv, ckk, cbb, ccell, cxu, cxv, cdu, cdv, mu, mv,
):
    rows, cols = gradient.shape
    total = rows + 2 * RIM
    column_blocks = cols // LANES
    gx_at, gx_size = lax.axis_index("gx"), lax.axis_size("gx")
    low_half = gx_at % 2 == 0
    left = lax.axis_index("gy") == 0

    def spread(ref, base, height, side_block, target, first_row):
        blocks = [ref[base : base + height, LANES * j : LANES * j + LANES] for j in range(column_blocks)]
        zero = jnp.zeros_like(side_block)
        blocks = [jnp.where(left, zero, side_block)] + blocks + [jnp.where(left, side_block, zero)]

        def store(s, value):
            target[pl.ds(first_row * 8 + s, height, stride=8), :] = value

        spread_rows(blocks, store)

    targets = (fu, fv, kk, bb)
    for n in range(4):
        for h in range(0, rows, 8):
            spread(fields.at[n], h, 8, side[rows * n + h : rows * n + h + 8, :], targets[n], RIM + h)
    for received, partner, is_above in ((from_x, side_x, jnp.logical_not(low_half)), (from_z, side_z, low_half)):
        near = jnp.where(is_above, RIM - 8, RIM + rows)
        far = jnp.where(is_above, 0, RIM + rows + 8)
        edge = jnp.where(left, partner[:, :LANES], partner[:, cols - LANES :])
        for n in range(4):
            spread(received, 8 * n, 8, edge[8 * n : 8 * n + 8], targets[n], near)
            spread(received, 32 + 2 * n, 2, edge[32 + 2 * n : 34 + 2 * n], targets[n], far)

    lanes = lane_ids()
    column = 96 * lax.broadcasted_iota(jnp.int32, (8, LANES), 0) + lanes - EDGE
    inside = jnp.where(left, (column >= 0).astype(F32), (column < cols).astype(F32))
    above = inside * jnp.where(gx_at > 0, 1.0, 0.0)
    below = inside * jnp.where(gx_at < gx_size - 1, 1.0, 0.0)
    mine = ((lanes >= EDGE) & (lanes < LANES - EDGE)).astype(F32)
    even = lanes % 2 == 0

    def at(ref, row):
        return ref[8 * row : 8 * row + 8, :]

    def put(ref, row, value):
        ref[8 * row : 8 * row + 8, :] = value

    def stiffness(visc, target, count, shift):
        paired = None
        for row in range(count):
            k = at(visc, row)
            now = k + pltpu.roll(k, LANES - shift, 1)
            if row:
                put(target, row - 1, 0.125 * (paired + now))
            paired = now

    def residual(x_u, x_v, f_u, f_v, beta, stiff, low, high, shift, use):
        def gradients(row):
            u, v = at(x_u, row), at(x_v, row)
            ru_, rv_ = pltpu.roll(u, LANES - shift, 1), pltpu.roll(v, LANES - shift, 1)
            return u, v, u + ru_, v + rv_, ru_ - u, rv_ - v

        def forces(row, one, two):
            a, b = two[2] - one[2], two[5] + one[5]
            c, d = two[4] + one[4], two[3] - one[3]
            s = at(stiff, row)
            both = a + b
            return s * (both + a), s * (both + b), (0.5 * s) * (c + d)

        before = gradients(low - 1)
        here = gradients(low)
        cell_before = forces(low - 1, before, here)
        for row in range(low, high):
            after = gradients(row + 1)
            cell_here = forces(row, here, after)
            shear = cell_before[2] + cell_here[2]
            shear_step = cell_before[2] - cell_here[2]
            px, qy = cell_before[0] - cell_here[0], cell_before[1] + cell_here[1]
            au = (px - shear) + pltpu.roll(px + shear, shift, 1)
            av = (shear_step - qy) + pltpu.roll(shear_step + qy, shift, 1)
            u, v = here[0], here[1]
            b = at(beta, row)
            use(row, u, v, at(f_u, row) - au - b * u, at(f_v, row) - av - b * v)
            here, cell_before = after, cell_here

    def sweep(x_u, x_v, d_u, d_v, f_u, f_v, beta, stiff, table, count, rim, shift):
        inverse = at(coefficients, table)
        for row in range(count):
            put(x_u, row, at(f_u, row) * inverse)
            put(x_v, row, at(f_v, row) * inverse)
        for step in range(DEG - 1):
            keep = at(coefficients, table + 1 + 2 * step)
            gain = at(coefficients, table + 2 + 2 * step)
            gains = (gain * above, gain * inside, gain * below)
            first = step == 0

            def use(row, u, v, gu, gv):
                part = gains[0 if row < rim else 2 if row >= count - rim else 1]
                old_u = u if first else at(d_u, row)
                old_v = v if first else at(d_v, row)
                new_u = keep * old_u + part * gu
                new_v = keep * old_v + part * gv
                put(d_u, row, new_u)
                put(d_v, row, new_v)
                put(x_u, row, u + new_u)
                put(x_v, row, v + new_v)

            residual(x_u, x_v, f_u, f_v, beta, stiff, step + 1, count - step - 1, shift, use)

    stiffness(kk, cell, total, 1)
    sweep(xu, xv, du, dv, fu, fv, bb, cell, 0, total, RIM, 1)

    squares = [jnp.zeros((8, LANES), F32)]

    def keep_residual(row, u, v, gu, gv):
        part = above if row < RIM else below if row >= RIM + rows else inside
        gu, gv = gu * part, gv * part
        put(ru, row, gu)
        put(rv, row, gv)
        if RIM <= row < RIM + rows:
            squares[0] = squares[0] + (gu * gu + gv * gv)

    residual(xu, xv, fu, fv, bb, cell, DEG, total - DEG, 1, keep_residual)

    coarse_rim = (RIM - DEG) // 2
    coarse_rows = rows // 2 + 2 * coarse_rim
    for i in range(coarse_rows):
        row = DEG + 2 * i
        for source, target, scale in ((ru, cfu, None), (rv, cfv, None), (kk, ckk, 0.25), (bb, cbb, None)):
            pair = at(source, row) + at(source, row + 1)
            pair = pair + pltpu.roll(pair, LANES - 1, 1)
            put(target, i, pair if scale is None else scale * pair)
    stiffness(ckk, ccell, coarse_rows, 2)
    sweep(cxu, cxv, cdu, cdv, cfu, cfv, cbb, ccell, 2 * DEG - 1, coarse_rows, coarse_rim, 2)

    for i in range(rows // 2):
        for fine, coarse, target in ((xu, cxu, mu), (xv, cxv, mv)):
            correction = at(coarse, coarse_rim + i)
            correction = jnp.where(even, correction, pltpu.roll(correction, 1, 1))
            for row in (2 * i, 2 * i + 1):
                put(target, row, at(fine, RIM + row) + correction)

    gradient_squares = jnp.zeros((8, LANES), F32)
    for h in range(0, rows, 8):
        for j in range(column_blocks):
            s = (LANES * j) // 96
            shift = LANES * j - 96 * s + EDGE
            border = 96 * (s + 1) - LANES * j
            columns = slice(LANES * j, LANES * j + LANES)
            product = None
            for n, source in enumerate((mu, mv)):
                one = source[pl.ds(8 * h + s, 8, stride=8), :]
                two = source[pl.ds(8 * h + s + 1, 8, stride=8), :]
                value = jnp.where(
                    lanes < border, pltpu.roll(one, LANES - shift, 1), pltpu.roll(two, (96 - shift) % LANES, 1)
                )
                multiplier[n, h : h + 8, columns] = value
                term = velocity[n, h : h + 8, columns] * value
                product = term if product is None else product + term
            value = -fields[3, h : h + 8, columns] * product
            gradient[h : h + 8, columns] = value
            gradient_squares = gradient_squares + value * value
    residual_squares = jnp.sum(squares[0] * mine, axis=0, keepdims=True)
    gradient_squares = jnp.sum(gradient_squares, axis=0, keepdims=True)
    pair = jnp.concatenate([residual_squares, gradient_squares], axis=1)
    sums[...] = jnp.broadcast_to(pair, sums.shape)


def scale_kernel(nodes, gathered, gradient, scaled, norm):
    residual_total = jnp.sum(gathered[:, :LANES], keepdims=True)
    gradient_total = jnp.sum(gathered[:, LANES:], keepdims=True)
    scaled[...] = gradient[...] / jnp.sqrt(gradient_total / nodes + 1e-06)
    norm[...] = jnp.sqrt(residual_total / (2 * nodes))


def body(misfit, velocity, viscosity, friction, ice, grounded, bounds):
    rows, cols = viscosity.shape
    gx_size, gy_size = lax.axis_size("gx"), lax.axis_size("gy")
    assert gy_size == 2 and cols == 96 * SEGS and rows == 16
    peers = gx_size * gy_size
    nodes = rows * cols * peers
    total = rows + 2 * RIM
    shaped = jax.ShapeDtypeStruct
    whole = pl.BlockSpec(memory_space=pltpu.VMEM)
    params = pltpu.CompilerParams(vmem_limit_bytes=32 * 1024 * 1024)

    held = pl.BlockSpec(memory_space=pltpu.HBM)
    fields, coefficients, x_send, z_send, side_send = pl.pallas_call(
        pack_kernel,
        out_shape=(
            shaped((4, rows, cols), F32),
            shaped((16 * (2 * DEG - 1), LANES), F32),
            shaped((4 * RIM, cols), F32),
            shaped((4 * RIM, cols), F32),
            shaped((4 * rows, LANES), F32),
        ),
        in_specs=[held] * 6,
        out_specs=[whole] * 5,
        scratch_shapes=[
            pltpu.SMEM((4,), F32),
            pltpu.VMEM((rows, cols), F32),
            pltpu.VMEM((rows, cols), F32),
            pltpu.VMEM((rows, cols), jnp.int32),
            pltpu.VMEM((rows, cols), jnp.int32),
            pltpu.SemaphoreType.DMA((6,)),
        ],
        compiler_params=params,
        name="pack",
    )(*(pltpu.with_memory_space_constraint(x, pltpu.HBM) for x in (bounds, misfit, viscosity, friction, ice, grounded)))

    x_pairs = [(i, i ^ 1) for i in range(gx_size) if i ^ 1 < gx_size]
    z_pairs = [(i, j) for i in range(1, gx_size - 1, 2) for j in (i + 1,)]
    z_pairs += [(j, i) for i, j in z_pairs]
    swap = [(0, 1), (1, 0)]
    from_x = lax.ppermute(x_send, "gx", x_pairs)
    from_z = lax.ppermute(z_send, "gx", z_pairs)
    side = lax.ppermute(side_send, "gy", swap)
    side_x = lax.ppermute(from_x, "gy", swap)
    side_z = lax.ppermute(from_z, "gy", swap)

    fine = pltpu.VMEM((8 * total, LANES), F32)
    coarse = pltpu.VMEM((4 * total, LANES), F32)
    owned = pltpu.VMEM((8 * rows, LANES), F32)
    multiplier, gradient, sums = pl.pallas_call(
        main_kernel,
        out_shape=(
            shaped((2, rows, cols), F32),
            shaped((rows, cols), F32),
            shaped((peers, 2 * LANES), F32),
        ),
        in_specs=[whole] * 8,
        out_specs=[whole] * 3,
        scratch_shapes=[fine] * 11 + [coarse] * 9 + [owned] * 2,
        compiler_params=params,
        name="leg",
    )(coefficients, fields, velocity, from_x, from_z, side, side_x, side_z)

    gathered = lax.all_to_all(sums, AXES, 0, 0, tiled=True)
    scaled, norm = pl.pallas_call(
        functools.partial(scale_kernel, nodes),
        out_shape=(shaped((rows, cols), F32), shaped((1, 1), F32)),
        in_specs=[whole] * 2,
        out_specs=[whole] * 2,
        compiler_params=params,
        name="scale",
    )(gathered, gradient)
    return multiplier, scaled, norm.reshape(1)


def solution(mesh):
    tile = P(("grp", "gx"), "gy")
    pair = P(None, ("grp", "gx"), "gy")
    return jax.shard_map(
        body,
        mesh=mesh,
        in_specs=(pair, pair, tile, tile, tile, tile, P("grp")),
        out_specs=(pair, tile, P("grp")),
        check_vma=False,
    )
```

```python
import functools

import jax
import jax.numpy as jnp
from jax import lax
from jax.experimental import pallas as pl
from jax.experimental.pallas import tpu as pltpu
from jax.sharding import PartitionSpec as P

DEG = 4
LANES = 128
SEGS = 8
RIM = 10
EDGE = 16
F32 = jnp.float32
AXES = ("gx", "gy")


def lane_ids():
    return lax.broadcasted_iota(jnp.int32, (8, LANES), 1)


def pack_kernel(
    bounds, misfit, visc, friction, ice, grounded,
    fields, coefficients, x_send, z_send, side_send,
    levels, visc_in, friction_in, ice_in, grounded_in, sems,
):
    copies = [
        pltpu.make_async_copy(source, target, sems.at[n])
        for n, (source, target) in enumerate((
            (misfit, fields.at[pl.ds(0, 2)]),
            (visc, visc_in),
            (ice, ice_in),
            (friction, friction_in),
            (grounded, grounded_in),
            (bounds, levels),
        ))
    ]
    for copy in copies:
        copy.start()
    rows, cols = visc.shape
    left = lax.axis_index("gy") == 0
    low_half = lax.axis_index("gx") % 2 == 0
    for copy in copies[:5]:
        copy.wait()
    fields[2] = visc_in[...] * ice_in[...].astype(F32)
    fields[3] = friction_in[...] * grounded_in[...].astype(F32)
    for n in range(4):
        last, first = fields[n, rows - 8 :, :], fields[n, :8, :]
        x_send[8 * n : 8 * n + 8, :] = jnp.where(low_half, last, first)
        z_send[8 * n : 8 * n + 8, :] = jnp.where(low_half, first, last)
        last, first = fields[n, rows - 10 : rows - 8, :], fields[n, 8:10, :]
        x_send[32 + 2 * n : 34 + 2 * n, :] = jnp.where(low_half, last, first)
        z_send[32 + 2 * n : 34 + 2 * n, :] = jnp.where(low_half, first, last)
        side_send[rows * n : rows * n + rows, :] = jnp.where(
            left, fields[n, :, cols - LANES :], fields[n, :, :LANES]
        )
    copies[5].wait()
    for sweep in range(2):
        lower = jnp.full((8, LANES), levels[2 * sweep])
        upper = jnp.full((8, LANES), levels[2 * sweep + 1])
        middle = 0.5 * (upper + lower)
        half = 0.5 * (upper - lower)
        spread = middle / half
        factor = 1.0 / spread
        values = [1.0 / middle]
        for step in range(DEG - 1):
            factor_next = 1.0 / (2.0 * spread - factor)
            values += [factor_next * factor, 2.0 * factor_next / half]
            factor = factor_next
        for n, value in enumerate(values):
            row = 8 * (sweep * (2 * DEG - 1) + n)
            coefficients[row : row + 8, :] = value


def spread_rows(blocks, store):
    lanes = lax.broadcasted_iota(jnp.int32, blocks[1].shape, 1)
    for s in range(SEGS):
        start = 96 * s - EDGE
        first = start // LANES
        offset = start - LANES * first
        merged = jnp.where(lanes >= offset, blocks[first + 1], blocks[first + 2])
        store(s, pltpu.roll(merged, LANES - offset, 1))


def main_kernel(
    coefficients, fields, velocity, from_x, from_z, side, side_x, side_z,
    multiplier, gradient, sums,
    fu, fv, kk, bb, cell, xu, xv, du, dv, ru, rv, cfu, cfv, ckk, cbb, ccell, cxu, cxv, cdu, cdv, mu, mv,
    nxu, nxv, nu, nv, tu, tv,
):
    rows, cols = gradient.shape
    total = rows + 2 * RIM
    column_blocks = cols // LANES
    gx_at, gx_size = lax.axis_index("gx"), lax.axis_size("gx")
    low_half = gx_at % 2 == 0
    left = lax.axis_index("gy") == 0

    next_, here_part, shifted_part = (nxu, nxv), (nu, nv), (tu, tv)

    def spread(ref, base, height, side_block, target, first_row):
        blocks = [ref[base : base + height, LANES * j : LANES * j + LANES] for j in range(column_blocks)]
        zero = jnp.zeros_like(side_block)
        blocks = [jnp.where(left, zero, side_block)] + blocks + [jnp.where(left, side_block, zero)]

        def store(s, value):
            target[pl.ds(first_row * 8 + s, height, stride=8), :] = value

        spread_rows(blocks, store)

    targets = (fu, fv, kk, bb)
    for n in range(4):
        for h in range(0, rows, 8):
            spread(fields.at[n], h, 8, side[rows * n + h : rows * n + h + 8, :], targets[n], RIM + h)
    for received, partner, is_above in ((from_x, side_x, jnp.logical_not(low_half)), (from_z, side_z, low_half)):
        near = jnp.where(is_above, RIM - 8, RIM + rows)
        far = jnp.where(is_above, 0, RIM + rows + 8)
        edge = jnp.where(left, partner[:, :LANES], partner[:, cols - LANES :])
        for n in range(4):
            spread(received, 8 * n, 8, edge[8 * n : 8 * n + 8], targets[n], near)
            spread(received, 32 + 2 * n, 2, edge[32 + 2 * n : 34 + 2 * n], targets[n], far)

    lanes = lane_ids()
    column = 96 * lax.broadcasted_iota(jnp.int32, (8, LANES), 0) + lanes - EDGE
    inside = jnp.where(left, (column >= 0).astype(F32), (column < cols).astype(F32))
    above = inside * jnp.where(gx_at > 0, 1.0, 0.0)
    below = inside * jnp.where(gx_at < gx_size - 1, 1.0, 0.0)
    mine = ((lanes >= EDGE) & (lanes < LANES - EDGE)).astype(F32)
    even = lanes % 2 == 0

    def at(ref, row):
        return ref[8 * row : 8 * row + 8, :]

    def put(ref, row, value):
        ref[8 * row : 8 * row + 8, :] = value

    def stiffness(visc, target, count, shift):
        paired = None
        for row in range(count):
            k = at(visc, row)
            now = k + pltpu.roll(k, LANES - shift, 1)
            if row:
                put(target, row - 1, 0.125 * (paired + now))
            paired = now

    def shifted(value, shift):
        return pltpu.roll(value, LANES - shift, 1)

    def forces(x, stiff, low, high, shift):
        def gradients(row):
            u, v = at(x[0], row), at(x[1], row)
            next_u, next_v = at(next_[0], row), at(next_[1], row)
            return u + next_u, v + next_v, next_u - u, next_v - v

        def cells(row, one, two):
            a, b = two[0] - one[0], two[3] + one[3]
            c, d = two[2] + one[2], two[1] - one[1]
            s = at(stiff, row)
            both = a + b
            return s * (both + a), s * (both + b), (0.5 * s) * (c + d)

        here = gradients(low)
        before = cells(low - 1, gradients(low - 1), here)
        for row in range(low, high):
            after = gradients(row + 1)
            now = cells(row, here, after)
            shear, shear_step = before[2] + now[2], before[2] - now[2]
            normal_step, normal = before[0] - now[0], before[1] + now[1]
            put(here_part[0], row, normal_step - shear)
            put(here_part[1], row, shear_step - normal)
            put(shifted_part[0], row, pltpu.roll(normal_step + shear, shift, 1))
            put(shifted_part[1], row, pltpu.roll(shear_step + normal, shift, 1))
            here, before = after, now

    def remaining(n, x_row, f, beta, row):
        return (at(f[n], row) - at(beta, row) * x_row) - (at(here_part[n], row) + at(shifted_part[n], row))

    def sweep(x, old, f, beta, stiff, table, count, rim, shift):
        inverse = at(coefficients, table)
        for row in range(count):
            for n in range(2):
                value = at(f[n], row) * inverse
                put(x[n], row, value)
                put(next_[n], row, shifted(value, shift))
        for step in range(DEG - 1):
            keep = at(coefficients, table + 1 + 2 * step)
            gain = at(coefficients, table + 2 + 2 * step)
            gains = (gain * above, gain * inside, gain * below)
            low, high = step + 1, count - step - 1
            forces(x, stiff, low, high, shift)
            for row in range(low, high):
                part = gains[0 if row < rim else 2 if row >= count - rim else 1]
                for n in range(2):
                    value = at(x[n], row)
                    change = value if step == 0 else value - at(old[n], row)
                    value = value + keep * change + part * remaining(n, value, f, beta, row)
                    put(old[n], row, value)
                    put(next_[n], row, shifted(value, shift))
            x, old = old, x
        return x

    stiffness(kk, cell, total, 1)
    x = sweep((xu, xv), (du, dv), (fu, fv), bb, cell, 0, total, RIM, 1)
    forces(x, cell, DEG, total - DEG, 1)
    squares = jnp.zeros((8, LANES), F32)
    for row in range(DEG, total - DEG):
        part = above if row < RIM else below if row >= RIM + rows else inside
        for n in range(2):
            value = part * remaining(n, at(x[n], row), (fu, fv), bb, row)
            put((ru, rv)[n], row, value)
            if RIM <= row < RIM + rows:
                squares = squares + value * value

    coarse_rim = (RIM - DEG) // 2
    coarse_rows = rows // 2 + 2 * coarse_rim
    for i in range(coarse_rows):
        row = DEG + 2 * i
        for source, target, scale in ((ru, cfu, None), (rv, cfv, None), (kk, ckk, 0.25), (bb, cbb, None)):
            pair = at(source, row) + at(source, row + 1)
            pair = pair + pltpu.roll(pair, LANES - 1, 1)
            put(target, i, pair if scale is None else scale * pair)
    stiffness(ckk, ccell, coarse_rows, 2)
    coarse_x = sweep((cxu, cxv), (cdu, cdv), (cfu, cfv), cbb, ccell, 2 * DEG - 1, coarse_rows, coarse_rim, 2)

    for i in range(rows // 2):
        for fine, coarse, target in zip(x, coarse_x, (mu, mv)):
            correction = at(coarse, coarse_rim + i)
            correction = jnp.where(even, correction, pltpu.roll(correction, 1, 1))
            for row in (2 * i, 2 * i + 1):
                put(target, row, at(fine, RIM + row) + correction)

    gradient_squares = jnp.zeros((8, LANES), F32)
    for h in range(0, rows, 8):
        for j in range(column_blocks):
            s = (LANES * j) // 96
            shift = LANES * j - 96 * s + EDGE
            border = 96 * (s + 1) - LANES * j
            columns = slice(LANES * j, LANES * j + LANES)
            product = None
            for n, source in enumerate((mu, mv)):
                one = source[pl.ds(8 * h + s, 8, stride=8), :]
                two = source[pl.ds(8 * h + s + 1, 8, stride=8), :]
                value = jnp.where(
                    lanes < border, pltpu.roll(one, LANES - shift, 1), pltpu.roll(two, (96 - shift) % LANES, 1)
                )
                multiplier[n, h : h + 8, columns] = value
                term = velocity[n, h : h + 8, columns] * value
                product = term if product is None else product + term
            value = -fields[3, h : h + 8, columns] * product
            gradient[h : h + 8, columns] = value
            gradient_squares = gradient_squares + value * value
    residual_squares = jnp.sum(squares * mine, axis=0, keepdims=True)
    gradient_squares = jnp.sum(gradient_squares, axis=0, keepdims=True)
    pair = jnp.concatenate([residual_squares, gradient_squares], axis=1)
    sums[...] = jnp.broadcast_to(pair, sums.shape)


def scale_kernel(nodes, gathered, gradient, scaled, norm):
    residual_total = jnp.sum(gathered[:, :LANES], keepdims=True)
    gradient_total = jnp.sum(gathered[:, LANES:], keepdims=True)
    scaled[...] = gradient[...] / jnp.sqrt(gradient_total / nodes + 1e-06)
    norm[...] = jnp.sqrt(residual_total / (2 * nodes))


def body(misfit, velocity, viscosity, friction, ice, grounded, bounds):
    rows, cols = viscosity.shape
    gx_size, gy_size = lax.axis_size("gx"), lax.axis_size("gy")
    assert gy_size == 2 and cols == 96 * SEGS and rows == 16
    peers = gx_size * gy_size
    nodes = rows * cols * peers
    total = rows + 2 * RIM
    shaped = jax.ShapeDtypeStruct
    whole = pl.BlockSpec(memory_space=pltpu.VMEM)
    params = pltpu.CompilerParams(vmem_limit_bytes=32 * 1024 * 1024)

    held = pl.BlockSpec(memory_space=pltpu.HBM)
    fields, coefficients, x_send, z_send, side_send = pl.pallas_call(
        pack_kernel,
        out_shape=(
            shaped((4, rows, cols), F32),
            shaped((16 * (2 * DEG - 1), LANES), F32),
            shaped((4 * RIM, cols), F32),
            shaped((4 * RIM, cols), F32),
            shaped((4 * rows, LANES), F32),
        ),
        in_specs=[held] * 6,
        out_specs=[whole] * 5,
        scratch_shapes=[
            pltpu.SMEM((4,), F32),
            pltpu.VMEM((rows, cols), F32),
            pltpu.VMEM((rows, cols), F32),
            pltpu.VMEM((rows, cols), jnp.int32),
            pltpu.VMEM((rows, cols), jnp.int32),
            pltpu.SemaphoreType.DMA((6,)),
        ],
        compiler_params=params,
        name="pack",
    )(*(pltpu.with_memory_space_constraint(x, pltpu.HBM) for x in (bounds, misfit, viscosity, friction, ice, grounded)))

    x_pairs = [(i, i ^ 1) for i in range(gx_size) if i ^ 1 < gx_size]
    z_pairs = [(i, j) for i in range(1, gx_size - 1, 2) for j in (i + 1,)]
    z_pairs += [(j, i) for i, j in z_pairs]
    swap = [(0, 1), (1, 0)]
    from_x = lax.ppermute(x_send, "gx", x_pairs)
    from_z = lax.ppermute(z_send, "gx", z_pairs)
    side = lax.ppermute(side_send, "gy", swap)
    side_x = lax.ppermute(from_x, "gy", swap)
    side_z = lax.ppermute(from_z, "gy", swap)

    fine = pltpu.VMEM((8 * total, LANES), F32)
    coarse = pltpu.VMEM((4 * total, LANES), F32)
    owned = pltpu.VMEM((8 * rows, LANES), F32)
    multiplier, gradient, sums = pl.pallas_call(
        main_kernel,
        out_shape=(
            shaped((2, rows, cols), F32),
            shaped((rows, cols), F32),
            shaped((peers, 2 * LANES), F32),
        ),
        in_specs=[whole] * 8,
        out_specs=[whole] * 3,
        scratch_shapes=[fine] * 11 + [coarse] * 9 + [owned] * 2 + [fine] * 6,
        compiler_params=params,
        name="leg",
    )(coefficients, fields, velocity, from_x, from_z, side, side_x, side_z)

    gathered = lax.all_to_all(sums, AXES, 0, 0, tiled=True)
    scaled, norm = pl.pallas_call(
        functools.partial(scale_kernel, nodes),
        out_shape=(shaped((rows, cols), F32), shaped((1, 1), F32)),
        in_specs=[whole] * 2,
        out_specs=[whole] * 2,
        compiler_params=params,
        name="scale",
    )(gathered, gradient)
    return multiplier, scaled, norm.reshape(1)


def solution(mesh):
    tile = P(("grp", "gx"), "gy")
    pair = P(None, ("grp", "gx"), "gy")
    return jax.shard_map(
        body,
        mesh=mesh,
        in_specs=(pair, pair, tile, tile, tile, tile, P("grp")),
        out_specs=(pair, tile, P("grp")),
        check_vma=False,
    )
```

```python
import functools

import jax
import jax.numpy as jnp
from jax import lax
from jax.experimental import pallas as pl
from jax.experimental.pallas import tpu as pltpu
from jax.sharding import PartitionSpec as P

DEG = 4
LANES = 128
SEGS = 8
RIM = 10
EDGE = 16
F32 = jnp.float32
AXES = ("gx", "gy")


def lane_ids():
    return lax.broadcasted_iota(jnp.int32, (8, LANES), 1)


def pack_kernel(
    bounds, misfit, visc, friction, ice, grounded,
    fields, coefficients, x_send, z_send, side_send,
    levels, visc_in, friction_in, ice_in, grounded_in, sems,
):
    copies = [
        pltpu.make_async_copy(source, target, sems.at[n])
        for n, (source, target) in enumerate((
            (misfit, fields.at[pl.ds(0, 2)]),
            (visc, visc_in),
            (ice, ice_in),
            (friction, friction_in),
            (grounded, grounded_in),
            (bounds, levels),
        ))
    ]
    for copy in copies:
        copy.start()
    rows, cols = visc.shape
    left = lax.axis_index("gy") == 0
    at, last_at = lax.axis_index("gx"), lax.axis_size("gx") - 1
    low_half = at % 2 == 0
    at_end = (at == 0) | (at == last_at)
    for copy in copies[:5]:
        copy.wait()
    fields[2] = visc_in[...] * ice_in[...].astype(F32)
    fields[3] = friction_in[...] * grounded_in[...].astype(F32)
    for n in range(4):
        last, first = fields[n, rows - 8 :, :], fields[n, :8, :]
        x_send[8 * n : 8 * n + 8, :] = jnp.where(low_half, last, first)
        z_send[8 * n : 8 * n + 8, :] = jnp.where(at_end, 0.0, jnp.where(low_half, first, last))
        last, first = fields[n, rows - 10 : rows - 8, :], fields[n, 8:10, :]
        x_send[32 + 2 * n : 34 + 2 * n, :] = jnp.where(low_half, last, first)
        z_send[32 + 2 * n : 34 + 2 * n, :] = jnp.where(at_end, 0.0, jnp.where(low_half, first, last))
        side_send[rows * n : rows * n + rows, :] = jnp.where(
            left, fields[n, :, cols - LANES :], fields[n, :, :LANES]
        )
    copies[5].wait()
    for sweep in range(2):
        lower = jnp.full((8, LANES), levels[2 * sweep])
        upper = jnp.full((8, LANES), levels[2 * sweep + 1])
        middle = 0.5 * (upper + lower)
        half = 0.5 * (upper - lower)
        spread = middle / half
        factor = 1.0 / spread
        values = [1.0 / middle]
        for step in range(DEG - 1):
            factor_next = 1.0 / (2.0 * spread - factor)
            values += [factor_next * factor, 2.0 * factor_next / half]
            factor = factor_next
        for n, value in enumerate(values):
            row = 8 * (sweep * (2 * DEG - 1) + n)
            coefficients[row : row + 8, :] = value


def spread_rows(blocks, store):
    lanes = lax.broadcasted_iota(jnp.int32, blocks[1].shape, 1)
    for s in range(SEGS):
        start = 96 * s - EDGE
        first = start // LANES
        offset = start - LANES * first
        merged = jnp.where(lanes >= offset, blocks[first + 1], blocks[first + 2])
        store(s, pltpu.roll(merged, LANES - offset, 1))


def main_kernel(
    coefficients, fields, velocity, from_x, from_z, side, side_x, side_z,
    multiplier, gradient, sums,
    fu, fv, kk, bb, cell, xu, xv, du, dv, ru, rv, cfu, cfv, ckk, cbb, ccell, cxu, cxv, cdu, cdv, mu, mv,
    nxu, nxv, nu, nv, tu, tv,
):
    rows, cols = gradient.shape
    total = rows + 2 * RIM
    column_blocks = cols // LANES
    gx_at, gx_size = lax.axis_index("gx"), lax.axis_size("gx")
    low_half = gx_at % 2 == 0
    left = lax.axis_index("gy") == 0

    next_, here_part, shifted_part = (nxu, nxv), (nu, nv), (tu, tv)

    def spread(ref, base, height, side_block, target, first_row):
        blocks = [ref[base : base + height, LANES * j : LANES * j + LANES] for j in range(column_blocks)]
        zero = jnp.zeros_like(side_block)
        blocks = [jnp.where(left, zero, side_block)] + blocks + [jnp.where(left, side_block, zero)]

        def store(s, value):
            target[pl.ds(first_row * 8 + s, height, stride=8), :] = value

        spread_rows(blocks, store)

    targets = (fu, fv, kk, bb)
    for n in range(4):
        for h in range(0, rows, 8):
            spread(fields.at[n], h, 8, side[rows * n + h : rows * n + h + 8, :], targets[n], RIM + h)
    for received, partner, is_above in ((from_x, side_x, jnp.logical_not(low_half)), (from_z, side_z, low_half)):
        near = jnp.where(is_above, RIM - 8, RIM + rows)
        far = jnp.where(is_above, 0, RIM + rows + 8)
        edge = jnp.where(left, partner[:, :LANES], partner[:, cols - LANES :])
        for n in range(4):
            spread(received, 8 * n, 8, edge[8 * n : 8 * n + 8], targets[n], near)
            spread(received, 32 + 2 * n, 2, edge[32 + 2 * n : 34 + 2 * n], targets[n], far)

    lanes = lane_ids()
    column = 96 * lax.broadcasted_iota(jnp.int32, (8, LANES), 0) + lanes - EDGE
    inside = jnp.where(left, (column >= 0).astype(F32), (column < cols).astype(F32))
    above = inside * jnp.where(gx_at > 0, 1.0, 0.0)
    below = inside * jnp.where(gx_at < gx_size - 1, 1.0, 0.0)
    mine = ((lanes >= EDGE) & (lanes < LANES - EDGE)).astype(F32)
    even = lanes % 2 == 0

    def at(ref, row):
        return ref[8 * row : 8 * row + 8, :]

    def put(ref, row, value):
        ref[8 * row : 8 * row + 8, :] = value

    def stiffness(visc, target, count, shift):
        paired = None
        for row in range(count):
            k = at(visc, row)
            now = k + pltpu.roll(k, LANES - shift, 1)
            if row:
                put(target, row - 1, 0.125 * (paired + now))
            paired = now

    def shifted(value, shift):
        return pltpu.roll(value, LANES - shift, 1)

    def forces(x, stiff, low, high, shift):
        def gradients(row):
            u, v = at(x[0], row), at(x[1], row)
            next_u, next_v = at(next_[0], row), at(next_[1], row)
            return u + next_u, v + next_v, next_u - u, next_v - v

        def cells(row, one, two):
            a, b = two[0] - one[0], two[3] + one[3]
            c, d = two[2] + one[2], two[1] - one[1]
            s = at(stiff, row)
            both = a + b
            return s * (both + a), s * (both + b), (0.5 * s) * (c + d)

        here = gradients(low)
        before = cells(low - 1, gradients(low - 1), here)
        for row in range(low, high):
            after = gradients(row + 1)
            now = cells(row, here, after)
            shear, shear_step = before[2] + now[2], before[2] - now[2]
            normal_step, normal = before[0] - now[0], before[1] + now[1]
            put(here_part[0], row, normal_step - shear)
            put(here_part[1], row, shear_step - normal)
            put(shifted_part[0], row, pltpu.roll(normal_step + shear, shift, 1))
            put(shifted_part[1], row, pltpu.roll(shear_step + normal, shift, 1))
            here, before = after, now

    def remaining(n, x_row, f, beta, row):
        return (at(f[n], row) - at(beta, row) * x_row) - (at(here_part[n], row) + at(shifted_part[n], row))

    def sweep(x, old, f, beta, stiff, table, count, rim, shift):
        inverse = at(coefficients, table)
        for row in range(count):
            for n in range(2):
                value = at(f[n], row) * inverse
                put(x[n], row, value)
                put(next_[n], row, shifted(value, shift))
        for step in range(DEG - 1):
            keep = at(coefficients, table + 1 + 2 * step)
            gain = at(coefficients, table + 2 + 2 * step)
            gains = (gain * above, gain * inside, gain * below)
            low, high = step + 1, count - step - 1
            forces(x, stiff, low, high, shift)
            for row in range(low, high):
                part = gains[0 if row < rim else 2 if row >= count - rim else 1]
                for n in range(2):
                    value = at(x[n], row)
                    change = value if step == 0 else value - at(old[n], row)
                    value = value + keep * change + part * remaining(n, value, f, beta, row)
                    put(old[n], row, value)
                    put(next_[n], row, shifted(value, shift))
            x, old = old, x
        return x

    stiffness(kk, cell, total, 1)
    x = sweep((xu, xv), (du, dv), (fu, fv), bb, cell, 0, total, RIM, 1)
    forces(x, cell, DEG, total - DEG, 1)
    squares = jnp.zeros((8, LANES), F32)
    for row in range(DEG, total - DEG):
        part = above if row < RIM else below if row >= RIM + rows else inside
        for n in range(2):
            value = part * remaining(n, at(x[n], row), (fu, fv), bb, row)
            put((ru, rv)[n], row, value)
            if RIM <= row < RIM + rows:
                squares = squares + value * value

    coarse_rim = (RIM - DEG) // 2
    coarse_rows = rows // 2 + 2 * coarse_rim
    for i in range(coarse_rows):
        row = DEG + 2 * i
        for source, target, scale in ((ru, cfu, None), (rv, cfv, None), (kk, ckk, 0.25), (bb, cbb, None)):
            pair = at(source, row) + at(source, row + 1)
            pair = pair + pltpu.roll(pair, LANES - 1, 1)
            put(target, i, pair if scale is None else scale * pair)
    stiffness(ckk, ccell, coarse_rows, 2)
    coarse_x = sweep((cxu, cxv), (cdu, cdv), (cfu, cfv), cbb, ccell, 2 * DEG - 1, coarse_rows, coarse_rim, 2)

    for i in range(rows // 2):
        for fine, coarse, target in zip(x, coarse_x, (mu, mv)):
            correction = at(coarse, coarse_rim + i)
            correction = jnp.where(even, correction, pltpu.roll(correction, 1, 1))
            for row in (2 * i, 2 * i + 1):
                put(target, row, at(fine, RIM + row) + correction)

    gradient_squares = jnp.zeros((8, LANES), F32)
    for h in range(0, rows, 8):
        for j in range(column_blocks):
            s = (LANES * j) // 96
            shift = LANES * j - 96 * s + EDGE
            border = 96 * (s + 1) - LANES * j
            columns = slice(LANES * j, LANES * j + LANES)
            product = None
            for n, source in enumerate((mu, mv)):
                one = source[pl.ds(8 * h + s, 8, stride=8), :]
                two = source[pl.ds(8 * h + s + 1, 8, stride=8), :]
                value = jnp.where(
                    lanes < border, pltpu.roll(one, LANES - shift, 1), pltpu.roll(two, (96 - shift) % LANES, 1)
                )
                multiplier[n, h : h + 8, columns] = value
                term = velocity[n, h : h + 8, columns] * value
                product = term if product is None else product + term
            value = -fields[3, h : h + 8, columns] * product
            gradient[h : h + 8, columns] = value
            gradient_squares = gradient_squares + value * value
    residual_squares = jnp.sum(squares * mine, axis=0, keepdims=True)
    gradient_squares = jnp.sum(gradient_squares, axis=0, keepdims=True)
    pair = jnp.concatenate([residual_squares, gradient_squares], axis=1)
    sums[...] = jnp.broadcast_to(pair, sums.shape)


def scale_kernel(nodes, gathered, gradient, held_multiplier, scaled, norm, multiplier, scaled_out, norm_out, sems):
    copies = [
        pltpu.make_async_copy(source, target, sems.at[n])
        for n, (source, target) in enumerate(((held_multiplier, multiplier), (norm_out, norm), (scaled_out, scaled)))
    ]
    copies[0].start()
    residual_total = jnp.sum(gathered[:, :LANES], keepdims=True)
    gradient_total = jnp.sum(gathered[:, LANES:], keepdims=True)
    norm_out[...] = jnp.sqrt(residual_total / (2 * nodes))
    copies[1].start()
    scaled_out[...] = gradient[...] / jnp.sqrt(gradient_total / nodes + 1e-06)
    copies[2].start()
    for copy in copies:
        copy.wait()


def body(misfit, velocity, viscosity, friction, ice, grounded, bounds):
    rows, cols = viscosity.shape
    gx_size, gy_size = lax.axis_size("gx"), lax.axis_size("gy")
    assert gy_size == 2 and gx_size % 2 == 0 and cols == 96 * SEGS and rows == 16
    peers = gx_size * gy_size
    nodes = rows * cols * peers
    total = rows + 2 * RIM
    shaped = jax.ShapeDtypeStruct
    whole = pl.BlockSpec(memory_space=pltpu.VMEM)
    params = pltpu.CompilerParams(vmem_limit_bytes=32 * 1024 * 1024)

    held = pl.BlockSpec(memory_space=pltpu.HBM)
    fields, coefficients, x_send, z_send, side_send = pl.pallas_call(
        pack_kernel,
        out_shape=(
            shaped((4, rows, cols), F32),
            shaped((16 * (2 * DEG - 1), LANES), F32),
            shaped((4 * RIM, cols), F32),
            shaped((4 * RIM, cols), F32),
            shaped((4 * rows, LANES), F32),
        ),
        in_specs=[held] * 6,
        out_specs=[whole] * 5,
        scratch_shapes=[
            pltpu.SMEM((4,), F32),
            pltpu.VMEM((rows, cols), F32),
            pltpu.VMEM((rows, cols), F32),
            pltpu.VMEM((rows, cols), jnp.int32),
            pltpu.VMEM((rows, cols), jnp.int32),
            pltpu.SemaphoreType.DMA((6,)),
        ],
        compiler_params=params,
        name="pack",
    )(*(pltpu.with_memory_space_constraint(x, pltpu.HBM) for x in (bounds, misfit, viscosity, friction, ice, grounded)))

    x_pairs = [(i, i ^ 1) for i in range(gx_size)]
    z_pairs = [(2 * i + c, 2 * j + c) for i in range(1, gx_size - 1) for j in (i + 1 if i % 2 else i - 1,) for c in (0, 1)]
    z_pairs += [(2 * i + c, 2 * i + 1 - c) for i in (0, gx_size - 1) for c in (0, 1)]
    swap = [(0, 1), (1, 0)]
    from_x = lax.ppermute(x_send, "gx", x_pairs)
    from_z = lax.ppermute(z_send, AXES, z_pairs)
    side = lax.ppermute(side_send, "gy", swap)
    from_x, from_z, side = lax.optimization_barrier((from_x, from_z, side))
    side_x = lax.ppermute(from_x, "gy", swap)
    side_z = lax.ppermute(from_z, "gy", swap)

    fine = pltpu.VMEM((8 * total, LANES), F32)
    coarse = pltpu.VMEM((4 * total, LANES), F32)
    owned = pltpu.VMEM((8 * rows, LANES), F32)
    held_multiplier, gradient, sums = pl.pallas_call(
        main_kernel,
        out_shape=(
            pltpu.VMEM((2, rows, cols), F32),
            pltpu.VMEM((rows, cols), F32),
            shaped((peers, 2 * LANES), F32),
        ),
        in_specs=[whole] * 8,
        out_specs=[whole] * 3,
        scratch_shapes=[fine] * 11 + [coarse] * 9 + [owned] * 2 + [fine] * 6,
        compiler_params=params,
        name="leg",
    )(coefficients, fields, velocity, from_x, from_z, side, side_x, side_z)

    gathered = lax.all_to_all(sums, AXES, 0, 0, tiled=True)
    scaled, norm, multiplier = pl.pallas_call(
        functools.partial(scale_kernel, nodes),
        out_shape=(
            pltpu.HBM((rows, cols), F32),
            pltpu.HBM((1, 1), F32),
            pltpu.HBM((2, rows, cols), F32),
        ),
        in_specs=[whole] * 3,
        out_specs=[held] * 3,
        scratch_shapes=[
            pltpu.VMEM((rows, cols), F32),
            pltpu.VMEM((1, 1), F32),
            pltpu.SemaphoreType.DMA((3,)),
        ],
        compiler_params=params,
        name="scale",
    )(gathered, gradient, held_multiplier)
    return multiplier, scaled, norm.reshape(1)


def solution(mesh):
    tile = P(("grp", "gx"), "gy")
    pair = P(None, ("grp", "gx"), "gy")
    return jax.shard_map(
        body,
        mesh=mesh,
        in_specs=(pair, pair, tile, tile, tile, tile, P("grp")),
        out_specs=(pair, tile, P("grp")),
        check_vma=False,
    )
```

```python
import functools

import jax
import jax.numpy as jnp
from jax import lax
from jax.experimental import pallas as pl
from jax.experimental.pallas import tpu as pltpu
from jax.sharding import PartitionSpec as P

DEG = 4
LANES = 128
SEGS = 8
RIM = 10
EDGE = 16
F32 = jnp.float32
AXES = ("gx", "gy")


def lane_ids():
    return lax.broadcasted_iota(jnp.int32, (8, LANES), 1)


def pack_kernel(
    bounds, misfit, visc, friction, ice, grounded,
    fields, coefficients, x_send, z_send, side_send, x_corner, z_corner,
    levels, visc_in, friction_in, ice_in, grounded_in, sems,
):
    copies = [
        pltpu.make_async_copy(source, target, sems.at[n])
        for n, (source, target) in enumerate((
            (misfit, fields.at[pl.ds(0, 2)]),
            (visc, visc_in),
            (ice, ice_in),
            (friction, friction_in),
            (grounded, grounded_in),
            (bounds, levels),
        ))
    ]
    for copy in copies:
        copy.start()
    rows, cols = visc.shape
    left = lax.axis_index("gy") == 0
    at, last_at = lax.axis_index("gx"), lax.axis_size("gx") - 1
    low_half = at % 2 == 0
    at_end = (at == 0) | (at == last_at)
    for copy in copies[:5]:
        copy.wait()
    fields[2] = visc_in[...] * ice_in[...].astype(F32)
    fields[3] = friction_in[...] * grounded_in[...].astype(F32)
    for n in range(4):
        last, first = fields[n, rows - 8 :, :], fields[n, :8, :]
        x_send[8 * n : 8 * n + 8, :] = jnp.where(low_half, last, first)
        z_send[8 * n : 8 * n + 8, :] = jnp.where(at_end, 0.0, jnp.where(low_half, first, last))
        last, first = fields[n, rows - 10 : rows - 8, :], fields[n, 8:10, :]
        x_send[32 + 2 * n : 34 + 2 * n, :] = jnp.where(low_half, last, first)
        z_send[32 + 2 * n : 34 + 2 * n, :] = jnp.where(at_end, 0.0, jnp.where(low_half, first, last))
        side_send[rows * n : rows * n + rows, :] = jnp.where(
            left, fields[n, :, cols - LANES :], fields[n, :, :LANES]
        )
    for source, target in ((x_send, x_corner), (z_send, z_corner)):
        target[...] = jnp.where(left, source[:, cols - LANES :], source[:, :LANES])
    copies[5].wait()
    for sweep in range(2):
        lower = jnp.full((8, LANES), levels[2 * sweep])
        upper = jnp.full((8, LANES), levels[2 * sweep + 1])
        middle = 0.5 * (upper + lower)
        half = 0.5 * (upper - lower)
        spread = middle / half
        factor = 1.0 / spread
        values = [1.0 / middle]
        for step in range(DEG - 1):
            factor_next = 1.0 / (2.0 * spread - factor)
            values += [factor_next * factor, 2.0 * factor_next / half]
            factor = factor_next
        for n, value in enumerate(values):
            row = 8 * (sweep * (2 * DEG - 1) + n)
            coefficients[row : row + 8, :] = value


def spread_rows(blocks, store):
    lanes = lax.broadcasted_iota(jnp.int32, blocks[1].shape, 1)
    for s in range(SEGS):
        start = 96 * s - EDGE
        first = start // LANES
        offset = start - LANES * first
        merged = jnp.where(lanes >= offset, blocks[first + 1], blocks[first + 2])
        store(s, pltpu.roll(merged, LANES - offset, 1))


def main_kernel(
    coefficients, fields, velocity, from_x, from_z, side, side_x, side_z,
    multiplier, gradient, sums,
    fu, fv, kk, bb, cell, xu, xv, du, dv, ru, rv, cfu, cfv, ckk, cbb, ccell, cxu, cxv, cdu, cdv, mu, mv,
    nxu, nxv, nu, nv, tu, tv,
):
    rows, cols = gradient.shape
    total = rows + 2 * RIM
    column_blocks = cols // LANES
    gx_at, gx_size = lax.axis_index("gx"), lax.axis_size("gx")
    low_half = gx_at % 2 == 0
    left = lax.axis_index("gy") == 0

    next_, here_part, shifted_part = (nxu, nxv), (nu, nv), (tu, tv)

    def spread(ref, base, height, side_block, target, first_row):
        blocks = [ref[base : base + height, LANES * j : LANES * j + LANES] for j in range(column_blocks)]
        zero = jnp.zeros_like(side_block)
        blocks = [jnp.where(left, zero, side_block)] + blocks + [jnp.where(left, side_block, zero)]

        def store(s, value):
            target[pl.ds(first_row * 8 + s, height, stride=8), :] = value

        spread_rows(blocks, store)

    targets = (fu, fv, kk, bb)
    for n in range(4):
        for h in range(0, rows, 8):
            spread(fields.at[n], h, 8, side[rows * n + h : rows * n + h + 8, :], targets[n], RIM + h)
    for received, partner, is_above in ((from_x, side_x, jnp.logical_not(low_half)), (from_z, side_z, low_half)):
        near = jnp.where(is_above, RIM - 8, RIM + rows)
        far = jnp.where(is_above, 0, RIM + rows + 8)
        edge = partner[...]
        for n in range(4):
            spread(received, 8 * n, 8, edge[8 * n : 8 * n + 8], targets[n], near)
            spread(received, 32 + 2 * n, 2, edge[32 + 2 * n : 34 + 2 * n], targets[n], far)

    lanes = lane_ids()
    column = 96 * lax.broadcasted_iota(jnp.int32, (8, LANES), 0) + lanes - EDGE
    inside = jnp.where(left, (column >= 0).astype(F32), (column < cols).astype(F32))
    above = inside * jnp.where(gx_at > 0, 1.0, 0.0)
    below = inside * jnp.where(gx_at < gx_size - 1, 1.0, 0.0)
    mine = ((lanes >= EDGE) & (lanes < LANES - EDGE)).astype(F32)
    even = lanes % 2 == 0

    def at(ref, row):
        return ref[8 * row : 8 * row + 8, :]

    def put(ref, row, value):
        ref[8 * row : 8 * row + 8, :] = value

    def stiffness(visc, target, count, shift):
        paired = None
        for row in range(count):
            k = at(visc, row)
            now = k + pltpu.roll(k, LANES - shift, 1)
            if row:
                put(target, row - 1, 0.125 * (paired + now))
            paired = now

    def shifted(value, shift):
        return pltpu.roll(value, LANES - shift, 1)

    def forces(x, stiff, low, high, shift):
        def gradients(row):
            u, v = at(x[0], row), at(x[1], row)
            next_u, next_v = at(next_[0], row), at(next_[1], row)
            return u + next_u, v + next_v, next_u - u, next_v - v

        def cells(row, one, two):
            a, b = two[0] - one[0], two[3] + one[3]
            c, d = two[2] + one[2], two[1] - one[1]
            s = at(stiff, row)
            both = a + b
            return s * (both + a), s * (both + b), (0.5 * s) * (c + d)

        here = gradients(low)
        before = cells(low - 1, gradients(low - 1), here)
        for row in range(low, high):
            after = gradients(row + 1)
            now = cells(row, here, after)
            shear, shear_step = before[2] + now[2], before[2] - now[2]
            normal_step, normal = before[0] - now[0], before[1] + now[1]
            put(here_part[0], row, normal_step - shear)
            put(here_part[1], row, shear_step - normal)
            put(shifted_part[0], row, pltpu.roll(normal_step + shear, shift, 1))
            put(shifted_part[1], row, pltpu.roll(shear_step + normal, shift, 1))
            here, before = after, now

    def remaining(n, x_row, f, beta, row):
        return (at(f[n], row) - at(beta, row) * x_row) - (at(here_part[n], row) + at(shifted_part[n], row))

    def sweep(x, old, f, beta, stiff, table, count, rim, shift):
        inverse = at(coefficients, table)
        for row in range(count):
            for n in range(2):
                value = at(f[n], row) * inverse
                put(x[n], row, value)
                put(next_[n], row, shifted(value, shift))
        for step in range(DEG - 1):
            keep = at(coefficients, table + 1 + 2 * step)
            gain = at(coefficients, table + 2 + 2 * step)
            gains = (gain * above, gain * inside, gain * below)
            low, high = step + 1, count - step - 1
            forces(x, stiff, low, high, shift)
            for row in range(low, high):
                part = gains[0 if row < rim else 2 if row >= count - rim else 1]
                for n in range(2):
                    value = at(x[n], row)
                    change = value if step == 0 else value - at(old[n], row)
                    value = value + keep * change + part * remaining(n, value, f, beta, row)
                    put(old[n], row, value)
                    put(next_[n], row, shifted(value, shift))
            x, old = old, x
        return x

    stiffness(kk, cell, total, 1)
    x = sweep((xu, xv), (du, dv), (fu, fv), bb, cell, 0, total, RIM, 1)
    forces(x, cell, DEG, total - DEG, 1)
    squares = jnp.zeros((8, LANES), F32)
    for row in range(DEG, total - DEG):
        part = above if row < RIM else below if row >= RIM + rows else inside
        for n in range(2):
            value = part * remaining(n, at(x[n], row), (fu, fv), bb, row)
            put((ru, rv)[n], row, value)
            if RIM <= row < RIM + rows:
                squares = squares + value * value

    coarse_rim = (RIM - DEG) // 2
    coarse_rows = rows // 2 + 2 * coarse_rim
    for i in range(coarse_rows):
        row = DEG + 2 * i
        for source, target, scale in ((ru, cfu, None), (rv, cfv, None), (kk, ckk, 0.25), (bb, cbb, None)):
            pair = at(source, row) + at(source, row + 1)
            pair = pair + pltpu.roll(pair, LANES - 1, 1)
            put(target, i, pair if scale is None else scale * pair)
    stiffness(ckk, ccell, coarse_rows, 2)
    coarse_x = sweep((cxu, cxv), (cdu, cdv), (cfu, cfv), cbb, ccell, 2 * DEG - 1, coarse_rows, coarse_rim, 2)

    for i in range(rows // 2):
        for fine, coarse, target in zip(x, coarse_x, (mu, mv)):
            correction = at(coarse, coarse_rim + i)
            correction = jnp.where(even, correction, pltpu.roll(correction, 1, 1))
            for row in (2 * i, 2 * i + 1):
                put(target, row, at(fine, RIM + row) + correction)

    gradient_squares = jnp.zeros((8, LANES), F32)
    for h in range(0, rows, 8):
        for j in range(column_blocks):
            s = (LANES * j) // 96
            shift = LANES * j - 96 * s + EDGE
            border = 96 * (s + 1) - LANES * j
            columns = slice(LANES * j, LANES * j + LANES)
            product = None
            for n, source in enumerate((mu, mv)):
                one = source[pl.ds(8 * h + s, 8, stride=8), :]
                two = source[pl.ds(8 * h + s + 1, 8, stride=8), :]
                value = jnp.where(
                    lanes < border, pltpu.roll(one, LANES - shift, 1), pltpu.roll(two, (96 - shift) % LANES, 1)
                )
                multiplier[n, h : h + 8, columns] = value
                term = velocity[n, h : h + 8, columns] * value
                product = term if product is None else product + term
            value = -fields[3, h : h + 8, columns] * product
            gradient[h : h + 8, columns] = value
            gradient_squares = gradient_squares + value * value
    residual_squares = jnp.sum(squares * mine, axis=0, keepdims=True)
    gradient_squares = jnp.sum(gradient_squares, axis=0, keepdims=True)
    pair = jnp.concatenate([residual_squares, gradient_squares], axis=1)
    sums[...] = jnp.broadcast_to(pair, sums.shape)


def scale_kernel(nodes, gathered, gradient, held_multiplier, scaled, norm, multiplier, scaled_out, norm_out, sems):
    copies = [
        pltpu.make_async_copy(source, target, sems.at[n])
        for n, (source, target) in enumerate(((held_multiplier, multiplier), (norm_out, norm), (scaled_out, scaled)))
    ]
    copies[0].start()
    residual_total = jnp.sum(gathered[:, :LANES], keepdims=True)
    gradient_total = jnp.sum(gathered[:, LANES:], keepdims=True)
    norm_out[...] = jnp.sqrt(residual_total / (2 * nodes))
    copies[1].start()
    scaled_out[...] = gradient[...] / jnp.sqrt(gradient_total / nodes + 1e-06)
    copies[2].start()
    for copy in copies:
        copy.wait()


def body(misfit, velocity, viscosity, friction, ice, grounded, bounds):
    rows, cols = viscosity.shape
    gx_size, gy_size = lax.axis_size("gx"), lax.axis_size("gy")
    assert gy_size == 2 and gx_size % 2 == 0 and cols == 96 * SEGS and rows == 16
    peers = gx_size * gy_size
    nodes = rows * cols * peers
    total = rows + 2 * RIM
    shaped = jax.ShapeDtypeStruct
    whole = pl.BlockSpec(memory_space=pltpu.VMEM)
    params = pltpu.CompilerParams(vmem_limit_bytes=32 * 1024 * 1024)

    held = pl.BlockSpec(memory_space=pltpu.HBM)
    fields, coefficients, x_send, z_send, side_send, x_corner, z_corner = pl.pallas_call(
        pack_kernel,
        out_shape=(
            shaped((4, rows, cols), F32),
            shaped((16 * (2 * DEG - 1), LANES), F32),
            shaped((4 * RIM, cols), F32),
            shaped((4 * RIM, cols), F32),
            shaped((4 * rows, LANES), F32),
            shaped((4 * RIM, LANES), F32),
            shaped((4 * RIM, LANES), F32),
        ),
        in_specs=[held] * 6,
        out_specs=[whole] * 7,
        scratch_shapes=[
            pltpu.SMEM((4,), F32),
            pltpu.VMEM((rows, cols), F32),
            pltpu.VMEM((rows, cols), F32),
            pltpu.VMEM((rows, cols), jnp.int32),
            pltpu.VMEM((rows, cols), jnp.int32),
            pltpu.SemaphoreType.DMA((6,)),
        ],
        compiler_params=params,
        name="pack",
    )(*(pltpu.with_memory_space_constraint(x, pltpu.HBM) for x in (bounds, misfit, viscosity, friction, ice, grounded)))

    x_pairs = [(i, i ^ 1) for i in range(gx_size)]
    z_pairs = [(2 * i + c, 2 * j + c) for i in range(1, gx_size - 1) for j in (i + 1 if i % 2 else i - 1,) for c in (0, 1)]
    z_pairs += [(2 * i + c, 2 * i + 1 - c) for i in (0, gx_size - 1) for c in (0, 1)]
    swap = [(0, 1), (1, 0)]
    from_x = lax.ppermute(x_send, "gx", x_pairs)
    from_z = lax.ppermute(z_send, AXES, z_pairs)
    side = lax.ppermute(side_send, "gy", swap)
    side_x = lax.ppermute(x_corner, AXES, [(2 * i + c, 2 * j + 1 - c) for i, j in x_pairs for c in (0, 1)])
    side_z = lax.ppermute(z_corner, AXES, [(i, j ^ 1 if 1 < i < 2 * gx_size - 2 else j) for i, j in z_pairs])

    fine = pltpu.VMEM((8 * total, LANES), F32)
    coarse = pltpu.VMEM((4 * total, LANES), F32)
    owned = pltpu.VMEM((8 * rows, LANES), F32)
    held_multiplier, gradient, sums = pl.pallas_call(
        main_kernel,
        out_shape=(
            pltpu.VMEM((2, rows, cols), F32),
            pltpu.VMEM((rows, cols), F32),
            shaped((peers, 2 * LANES), F32),
        ),
        in_specs=[whole] * 8,
        out_specs=[whole] * 3,
        scratch_shapes=[fine] * 11 + [coarse] * 9 + [owned] * 2 + [fine] * 6,
        compiler_params=params,
        name="leg",
    )(coefficients, fields, velocity, from_x, from_z, side, side_x, side_z)

    gathered = lax.all_to_all(sums, AXES, 0, 0, tiled=True)
    scaled, norm, multiplier = pl.pallas_call(
        functools.partial(scale_kernel, nodes),
        out_shape=(
            pltpu.HBM((rows, cols), F32),
            pltpu.HBM((1, 1), F32),
            pltpu.HBM((2, rows, cols), F32),
        ),
        in_specs=[whole] * 3,
        out_specs=[held] * 3,
        scratch_shapes=[
            pltpu.VMEM((rows, cols), F32),
            pltpu.VMEM((1, 1), F32),
            pltpu.SemaphoreType.DMA((3,)),
        ],
        compiler_params=params,
        name="scale",
    )(gathered, gradient, held_multiplier)
    return multiplier, scaled, norm.reshape(1)


def solution(mesh):
    tile = P(("grp", "gx"), "gy")
    pair = P(None, ("grp", "gx"), "gy")
    return jax.shard_map(
        body,
        mesh=mesh,
        in_specs=(pair, pair, tile, tile, tile, tile, P("grp")),
        out_specs=(pair, tile, P("grp")),
        check_vma=False,
    )
```

```python
import functools

import jax
import jax.numpy as jnp
from jax import lax
from jax.experimental import pallas as pl
from jax.experimental.pallas import tpu as pltpu
from jax.sharding import PartitionSpec as P

DEG = 4
LANES = 128
SEGS = 8
RIM = 10
EDGE = 16
F32 = jnp.float32
AXES = ("gx", "gy")


def lane_ids():
    return lax.broadcasted_iota(jnp.int32, (8, LANES), 1)


def pack_kernel(
    bounds, misfit, visc, friction, ice, grounded,
    fields, coefficients, x_send, z_send, side_send, x_corner, z_corner,
    levels, visc_in, friction_in, ice_in, grounded_in, sems,
):
    copies = [
        pltpu.make_async_copy(source, target, sems.at[n])
        for n, (source, target) in enumerate((
            (misfit, fields.at[pl.ds(0, 2)]),
            (visc, visc_in),
            (ice, ice_in),
            (friction, friction_in),
            (grounded, grounded_in),
            (bounds, levels),
        ))
    ]
    for copy in copies:
        copy.start()
    rows, cols = visc.shape
    left = lax.axis_index("gy") == 0
    at, last_at = lax.axis_index("gx"), lax.axis_size("gx") - 1
    low_half = at % 2 == 0
    at_end = (at == 0) | (at == last_at)
    for copy in copies[:5]:
        copy.wait()
    fields[2] = visc_in[...] * ice_in[...].astype(F32)
    fields[3] = friction_in[...] * grounded_in[...].astype(F32)
    for n in range(4):
        last, first = fields[n, rows - 8 :, :], fields[n, :8, :]
        x_send[8 * n : 8 * n + 8, :] = jnp.where(low_half, last, first)
        z_send[8 * n : 8 * n + 8, :] = jnp.where(at_end, 0.0, jnp.where(low_half, first, last))
        last, first = fields[n, rows - 10 : rows - 8, :], fields[n, 8:10, :]
        x_send[32 + 2 * n : 34 + 2 * n, :] = jnp.where(low_half, last, first)
        z_send[32 + 2 * n : 34 + 2 * n, :] = jnp.where(at_end, 0.0, jnp.where(low_half, first, last))
        side_send[rows * n : rows * n + rows, :] = jnp.where(
            left, fields[n, :, cols - LANES :], fields[n, :, :LANES]
        )
    own_columns = lane_ids() // EDGE == lax.broadcasted_iota(jnp.int32, (8, LANES), 0)
    for source, target in ((x_send, x_corner), (z_send, z_corner)):
        for q in range(RIM // 2):
            last, first = source[8 * q : 8 * q + 8, cols - LANES :], source[8 * q : 8 * q + 8, :LANES]
            columns = jnp.where(
                left,
                pltpu.roll(last, EDGE, 1, stride=EDGE, stride_axis=0),
                pltpu.roll(first, 0, 1, stride=EDGE, stride_axis=0),
            )
            target[q : q + 1, :] = jnp.sum(jnp.where(own_columns, columns, 0.0), axis=0, keepdims=True)
        target[RIM // 2 :, :] = jnp.zeros((8 - RIM // 2, LANES), F32)
    copies[5].wait()
    for sweep in range(2):
        lower = jnp.full((8, LANES), levels[2 * sweep])
        upper = jnp.full((8, LANES), levels[2 * sweep + 1])
        middle = 0.5 * (upper + lower)
        half = 0.5 * (upper - lower)
        spread = middle / half
        factor = 1.0 / spread
        values = [1.0 / middle]
        for step in range(DEG - 1):
            factor_next = 1.0 / (2.0 * spread - factor)
            values += [factor_next * factor, 2.0 * factor_next / half]
            factor = factor_next
        for n, value in enumerate(values):
            row = 8 * (sweep * (2 * DEG - 1) + n)
            coefficients[row : row + 8, :] = value


def spread_rows(blocks, store):
    lanes = lax.broadcasted_iota(jnp.int32, blocks[1].shape, 1)
    for s in range(SEGS):
        start = 96 * s - EDGE
        first = start // LANES
        offset = start - LANES * first
        merged = jnp.where(lanes >= offset, blocks[first + 1], blocks[first + 2])
        store(s, pltpu.roll(merged, LANES - offset, 1))


def main_kernel(
    coefficients, fields, velocity, from_x, from_z, side, side_x, side_z,
    multiplier, gradient, sums,
    fu, fv, kk, bb, cell, xu, xv, du, dv, ru, rv, cfu, cfv, ckk, cbb, ccell, cxu, cxv, cdu, cdv, mu, mv,
    nxu, nxv, nu, nv, tu, tv, cell_before, corner,
):
    rows, cols = gradient.shape
    total = rows + 2 * RIM
    column_blocks = cols // LANES
    gx_at, gx_size = lax.axis_index("gx"), lax.axis_size("gx")
    low_half = gx_at % 2 == 0
    left = lax.axis_index("gy") == 0

    next_, here_part, shifted_part = (nxu, nxv), (nu, nv), (tu, tv)
    previous = here_part

    def spread(ref, base, height, side_block, target, first_row):
        blocks = [ref[base : base + height, LANES * j : LANES * j + LANES] for j in range(column_blocks)]
        zero = jnp.zeros_like(side_block)
        blocks = [jnp.where(left, zero, side_block)] + blocks + [jnp.where(left, side_block, zero)]

        def store(s, value):
            target[pl.ds(first_row * 8 + s, height, stride=8), :] = value

        spread_rows(blocks, store)

    targets = (fu, fv, kk, bb)
    for n in range(4):
        for h in range(0, rows, 8):
            spread(fields.at[n], h, 8, side[rows * n + h : rows * n + h + 8, :], targets[n], RIM + h)
    for received, partner, is_above in ((from_x, side_x, jnp.logical_not(low_half)), (from_z, side_z, low_half)):
        near = jnp.where(is_above, RIM - 8, RIM + rows)
        far = jnp.where(is_above, 0, RIM + rows + 8)
        rolled = [pltpu.roll(partner[...], (LANES - EDGE * i) % LANES, 1) if i else partner[...] for i in range(8)]
        for i in range(8):
            columns = jnp.where(left, rolled[i], rolled[(i + 1) % 8])
            corner[pl.ds(i, RIM // 2, stride=8), :] = columns[: RIM // 2]
        edge = corner
        for n in range(4):
            spread(received, 8 * n, 8, edge[8 * n : 8 * n + 8, :], targets[n], near)
            spread(received, 32 + 2 * n, 2, edge[32 + 2 * n : 34 + 2 * n, :], targets[n], far)

    lanes = lane_ids()
    column = 96 * lax.broadcasted_iota(jnp.int32, (8, LANES), 0) + lanes - EDGE
    inside = jnp.where(left, (column >= 0).astype(F32), (column < cols).astype(F32))
    above = inside * jnp.where(gx_at > 0, 1.0, 0.0)
    below = inside * jnp.where(gx_at < gx_size - 1, 1.0, 0.0)
    mine = ((lanes >= EDGE) & (lanes < LANES - EDGE)).astype(F32)
    even = lanes % 2 == 0

    def at(ref, row):
        return ref[8 * row : 8 * row + 8, :]

    def put(ref, row, value):
        ref[8 * row : 8 * row + 8, :] = value

    def stiffness(visc, target, count, shift):
        paired = None
        for row in range(count):
            k = at(visc, row)
            now = k + pltpu.roll(k, LANES - shift, 1)
            if row:
                put(target, row - 1, 0.125 * (paired + now))
            paired = now

    def shifted(value, shift):
        return pltpu.roll(value, LANES - shift, 1)

    def forces(x, stiff, low, high, shift):
        def gradients(row):
            u, v = at(x[0], row), at(x[1], row)
            next_u, next_v = at(next_[0], row), at(next_[1], row)
            return u + next_u, v + next_v, next_u - u, next_v - v

        def cells(row, one, two):
            a, b = two[0] - one[0], two[3] + one[3]
            c, d = two[2] + one[2], two[1] - one[1]
            s = at(stiff, row)
            both = a + b
            return s * (both + a), s * (both + b), (0.5 * s) * (c + d)

        here = gradients(low)
        before = cells(low - 1, gradients(low - 1), here)
        for row in range(low, high):
            after = gradients(row + 1)
            now = cells(row, here, after)
            shear, shear_step = before[2] + now[2], before[2] - now[2]
            normal_step, normal = before[0] - now[0], before[1] + now[1]
            put(here_part[0], row, normal_step - shear)
            put(here_part[1], row, shear_step - normal)
            put(shifted_part[0], row, pltpu.roll(normal_step + shear, shift, 1))
            put(shifted_part[1], row, pltpu.roll(shear_step + normal, shift, 1))
            here, before = after, now

    def remaining(n, x_row, f, beta, row):
        return (at(f[n], row) - at(beta, row) * x_row) - (at(here_part[n], row) + at(shifted_part[n], row))

    def sweep(x, old, f, beta, stiff, table, count, rim, shift):
        inverse = at(coefficients, table)
        for row in range(count):
            for n in range(2):
                value = at(f[n], row) * inverse
                put(x[n], row, value)
                put(next_[n], row, shifted(value, shift))
        for step in range(DEG - 1):
            keep = at(coefficients, table + 1 + 2 * step)
            gain = at(coefficients, table + 2 + 2 * step)
            gains = (gain * above, gain * inside, gain * below)
            low, high = step + 1, count - step - 1
            forces(x, stiff, low, high, shift)
            for row in range(low, high):
                part = gains[0 if row < rim else 2 if row >= count - rim else 1]
                for n in range(2):
                    value = at(x[n], row)
                    change = value if step == 0 else value - at(old[n], row)
                    value = value + keep * change + part * remaining(n, value, f, beta, row)
                    put(old[n], row, value)
                    put(next_[n], row, shifted(value, shift))
            x, old = old, x
        return x

    def short_sweep(x, old, f, beta, stiff, table, count, rim, shift):
        for row in range(count - 1):
            put(cell_before, row, pltpu.roll(at(stiff, row), shift, 1))

        def keep_both(n, row, value):
            put(next_[n], row, shifted(value, shift))
            put(previous[n], row, pltpu.roll(value, shift, 1))

        def gradients(row):
            u, v = at(x[0], row), at(x[1], row)
            next_u, next_v = at(next_[0], row), at(next_[1], row)
            last_u, last_v = at(previous[0], row), at(previous[1], row)
            return (
                (u + next_u, v + next_v, next_u - u, next_v - v),
                (u + last_u, v + last_v, u - last_u, v - last_v),
            )

        def cells(row, one, two):
            values = []
            for stiff_, one_, two_ in zip((stiff, cell_before), one, two):
                a, b = two_[0] - one_[0], two_[3] + one_[3]
                c, d = two_[2] + one_[2], two_[1] - one_[1]
                s = at(stiff_, row)
                both = a + b
                values.append((s * (both + a), s * (both + b), (0.5 * s) * (c + d)))
            return values

        inverse = at(coefficients, table)
        for row in range(count):
            for n in range(2):
                value = at(f[n], row) * inverse
                put(x[n], row, value)
                keep_both(n, row, value)
        for step in range(DEG - 1):
            keep = at(coefficients, table + 1 + 2 * step)
            gain = at(coefficients, table + 2 + 2 * step)
            gains = (gain * above, gain * inside, gain * below)
            low, high = step + 1, count - step - 1
            here = gradients(low)
            before = cells(low - 1, gradients(low - 1), here)
            for row in range(low, high):
                after = gradients(row + 1)
                now = cells(row, here, after)
                (xx0, yy0, xy0), (xx1, yy1, xy1) = (
                    (p[0] - q[0], p[1] + q[1], (p[2] + q[2], p[2] - q[2])) for p, q in zip(before, now)
                )
                applied = ((xx0 - xy0[0]) + (xx1 + xy1[0]), (xy0[1] - yy0) + (xy1[1] + yy1))
                part = gains[0 if row < rim else 2 if row >= count - rim else 1]
                for n in range(2):
                    value = at(x[n], row)
                    change = value if step == 0 else value - at(old[n], row)
                    left_over = (at(f[n], row) - at(beta, row) * value) - applied[n]
                    value = value + keep * change + part * left_over
                    put(old[n], row, value)
                    if step < DEG - 2:
                        keep_both(n, row, value)
                here, before = after, now
            x, old = old, x
        return x

    stiffness(kk, cell, total, 1)
    x = sweep((xu, xv), (du, dv), (fu, fv), bb, cell, 0, total, RIM, 1)
    forces(x, cell, DEG, total - DEG, 1)
    squares = jnp.zeros((8, LANES), F32)
    for row in range(DEG, total - DEG):
        part = above if row < RIM else below if row >= RIM + rows else inside
        for n in range(2):
            value = part * remaining(n, at(x[n], row), (fu, fv), bb, row)
            put((ru, rv)[n], row, value)
            if RIM <= row < RIM + rows:
                squares = squares + value * value

    coarse_rim = (RIM - DEG) // 2
    coarse_rows = rows // 2 + 2 * coarse_rim
    for i in range(coarse_rows):
        row = DEG + 2 * i
        for source, target, scale in ((ru, cfu, None), (rv, cfv, None), (kk, ckk, 0.25), (bb, cbb, None)):
            pair = at(source, row) + at(source, row + 1)
            pair = pair + pltpu.roll(pair, LANES - 1, 1)
            put(target, i, pair if scale is None else scale * pair)
    stiffness(ckk, ccell, coarse_rows, 2)
    coarse_x = short_sweep((cxu, cxv), (cdu, cdv), (cfu, cfv), cbb, ccell, 2 * DEG - 1, coarse_rows, coarse_rim, 2)

    for i in range(rows // 2):
        for fine, coarse, target in zip(x, coarse_x, (mu, mv)):
            correction = at(coarse, coarse_rim + i)
            correction = jnp.where(even, correction, pltpu.roll(correction, 1, 1))
            for row in (2 * i, 2 * i + 1):
                put(target, row, at(fine, RIM + row) + correction)

    gradient_squares = jnp.zeros((8, LANES), F32)
    for h in range(0, rows, 8):
        for j in range(column_blocks):
            s = (LANES * j) // 96
            shift = LANES * j - 96 * s + EDGE
            border = 96 * (s + 1) - LANES * j
            columns = slice(LANES * j, LANES * j + LANES)
            product = None
            for n, source in enumerate((mu, mv)):
                one = source[pl.ds(8 * h + s, 8, stride=8), :]
                two = source[pl.ds(8 * h + s + 1, 8, stride=8), :]
                value = jnp.where(
                    lanes < border, pltpu.roll(one, LANES - shift, 1), pltpu.roll(two, (96 - shift) % LANES, 1)
                )
                multiplier[n, h : h + 8, columns] = value
                term = velocity[n, h : h + 8, columns] * value
                product = term if product is None else product + term
            value = -fields[3, h : h + 8, columns] * product
            gradient[h : h + 8, columns] = value
            gradient_squares = gradient_squares + value * value
    residual_squares = jnp.sum(squares * mine, axis=0, keepdims=True)
    gradient_squares = jnp.sum(gradient_squares, axis=0, keepdims=True)
    pair = jnp.concatenate([residual_squares, gradient_squares], axis=1)
    sums[...] = jnp.broadcast_to(pair, sums.shape)


def scale_kernel(nodes, gathered, gradient, held_multiplier, scaled, norm, multiplier, scaled_out, norm_out, sems):
    copies = [
        pltpu.make_async_copy(source, target, sems.at[n])
        for n, (source, target) in enumerate(((held_multiplier, multiplier), (norm_out, norm), (scaled_out, scaled)))
    ]
    copies[0].start()
    residual_total = jnp.sum(gathered[:, :LANES], keepdims=True)
    gradient_total = jnp.sum(gathered[:, LANES:], keepdims=True)
    norm_out[...] = jnp.sqrt(residual_total / (2 * nodes))
    copies[1].start()
    scaled_out[...] = gradient[...] / jnp.sqrt(gradient_total / nodes + 1e-06)
    copies[2].start()
    for copy in copies:
        copy.wait()


def body(misfit, velocity, viscosity, friction, ice, grounded, bounds):
    rows, cols = viscosity.shape
    gx_size, gy_size = lax.axis_size("gx"), lax.axis_size("gy")
    assert gy_size == 2 and gx_size % 2 == 0 and cols == 96 * SEGS and rows == 16
    peers = gx_size * gy_size
    nodes = rows * cols * peers
    total = rows + 2 * RIM
    shaped = jax.ShapeDtypeStruct
    whole = pl.BlockSpec(memory_space=pltpu.VMEM)
    params = pltpu.CompilerParams(vmem_limit_bytes=32 * 1024 * 1024)

    held = pl.BlockSpec(memory_space=pltpu.HBM)
    fields, coefficients, x_send, z_send, side_send, x_corner, z_corner = pl.pallas_call(
        pack_kernel,
        out_shape=(
            shaped((4, rows, cols), F32),
            shaped((16 * (2 * DEG - 1), LANES), F32),
            shaped((4 * RIM, cols), F32),
            shaped((4 * RIM, cols), F32),
            shaped((4 * rows, LANES), F32),
            shaped((8, LANES), F32),
            shaped((8, LANES), F32),
        ),
        in_specs=[held] * 6,
        out_specs=[whole] * 7,
        scratch_shapes=[
            pltpu.SMEM((4,), F32),
            pltpu.VMEM((rows, cols), F32),
            pltpu.VMEM((rows, cols), F32),
            pltpu.VMEM((rows, cols), jnp.int32),
            pltpu.VMEM((rows, cols), jnp.int32),
            pltpu.SemaphoreType.DMA((6,)),
        ],
        compiler_params=params,
        name="pack",
    )(*(pltpu.with_memory_space_constraint(x, pltpu.HBM) for x in (bounds, misfit, viscosity, friction, ice, grounded)))

    x_pairs = [(i, i ^ 1) for i in range(gx_size)]
    z_pairs = [(2 * i + c, 2 * j + c) for i in range(1, gx_size - 1) for j in (i + 1 if i % 2 else i - 1,) for c in (0, 1)]
    z_pairs += [(2 * i + c, 2 * i + 1 - c) for i in (0, gx_size - 1) for c in (0, 1)]
    swap = [(0, 1), (1, 0)]
    from_x = lax.ppermute(x_send, "gx", x_pairs)
    from_z = lax.ppermute(z_send, AXES, z_pairs)
    side = lax.ppermute(side_send, "gy", swap)
    side_x = lax.ppermute(x_corner, AXES, [(2 * i + c, 2 * j + 1 - c) for i, j in x_pairs for c in (0, 1)])
    side_z = lax.ppermute(z_corner, AXES, [(i, j ^ 1 if 1 < i < 2 * gx_size - 2 else j) for i, j in z_pairs])

    fine = pltpu.VMEM((8 * total, LANES), F32)
    coarse = pltpu.VMEM((4 * total, LANES), F32)
    owned = pltpu.VMEM((8 * rows, LANES), F32)
    held_multiplier, gradient, sums = pl.pallas_call(
        main_kernel,
        out_shape=(
            pltpu.VMEM((2, rows, cols), F32),
            pltpu.VMEM((rows, cols), F32),
            shaped((peers, 2 * LANES), F32),
        ),
        in_specs=[whole] * 8,
        out_specs=[whole] * 3,
        scratch_shapes=[fine] * 11 + [coarse] * 9 + [owned] * 2 + [fine] * 6 + [coarse, pltpu.VMEM((4 * RIM, LANES), F32)],
        compiler_params=params,
        name="leg",
    )(coefficients, fields, velocity, from_x, from_z, side, side_x, side_z)

    gathered = lax.all_to_all(sums, AXES, 0, 0, tiled=True)
    scaled, norm, multiplier = pl.pallas_call(
        functools.partial(scale_kernel, nodes),
        out_shape=(
            pltpu.HBM((rows, cols), F32),
            pltpu.HBM((1, 1), F32),
            pltpu.HBM((2, rows, cols), F32),
        ),
        in_specs=[whole] * 3,
        out_specs=[held] * 3,
        scratch_shapes=[
            pltpu.VMEM((rows, cols), F32),
            pltpu.VMEM((1, 1), F32),
            pltpu.SemaphoreType.DMA((3,)),
        ],
        compiler_params=params,
        name="scale",
    )(gathered, gradient, held_multiplier)
    return multiplier, scaled, norm.reshape(1)


def solution(mesh):
    tile = P(("grp", "gx"), "gy")
    pair = P(None, ("grp", "gx"), "gy")
    return jax.shard_map(
        body,
        mesh=mesh,
        in_specs=(pair, pair, tile, tile, tile, tile, P("grp")),
        out_specs=(pair, tile, P("grp")),
        check_vma=False,
    )
```

```python
import functools

import jax
import jax.numpy as jnp
from jax import lax
from jax.experimental import pallas as pl
from jax.experimental.pallas import tpu as pltpu
from jax.sharding import PartitionSpec as P

DEG = 4
LANES = 128
SEGS = 8
RIM = 10
EDGE = 16
F32 = jnp.float32
AXES = ("gx", "gy")


def lane_ids():
    return lax.broadcasted_iota(jnp.int32, (8, LANES), 1)


def pack_kernel(
    bounds, misfit, visc, friction, ice, grounded,
    fields, coefficients, x_send, z_send, side_send, x_corner, z_corner,
    levels, visc_in, friction_in, ice_in, grounded_in, sems,
):
    copies = [
        pltpu.make_async_copy(source, target, sems.at[n])
        for n, (source, target) in enumerate((
            (misfit, fields.at[pl.ds(0, 2)]),
            (visc, visc_in),
            (ice, ice_in),
            (friction, friction_in),
            (grounded, grounded_in),
            (bounds, levels),
        ))
    ]
    for copy in copies:
        copy.start()
    rows, cols = visc.shape
    left = lax.axis_index("gy") == 0
    at, last_at = lax.axis_index("gx"), lax.axis_size("gx") - 1
    low_half = at % 2 == 0
    at_end = (at == 0) | (at == last_at)
    for copy in copies[:5]:
        copy.wait()
    fields[2] = visc_in[...] * ice_in[...].astype(F32)
    fields[3] = friction_in[...] * grounded_in[...].astype(F32)
    for n in range(4):
        last, first = fields[n, rows - 8 :, :], fields[n, :8, :]
        x_send[8 * n : 8 * n + 8, :] = jnp.where(low_half, last, first)
        z_send[8 * n : 8 * n + 8, :] = jnp.where(at_end, 0.0, jnp.where(low_half, first, last))
        last, first = fields[n, rows - 10 : rows - 8, :], fields[n, 8:10, :]
        x_send[32 + 2 * n : 34 + 2 * n, :] = jnp.where(low_half, last, first)
        z_send[32 + 2 * n : 34 + 2 * n, :] = jnp.where(at_end, 0.0, jnp.where(low_half, first, last))
        side_send[rows * n : rows * n + rows, :] = jnp.where(
            left, fields[n, :, cols - LANES :], fields[n, :, :LANES]
        )
    own_columns = lane_ids() // EDGE == lax.broadcasted_iota(jnp.int32, (8, LANES), 0)
    for source, target in ((x_send, x_corner), (z_send, z_corner)):
        for q in range(RIM // 2):
            last, first = source[8 * q : 8 * q + 8, cols - LANES :], source[8 * q : 8 * q + 8, :LANES]
            columns = jnp.where(
                left,
                pltpu.roll(last, EDGE, 1, stride=EDGE, stride_axis=0),
                pltpu.roll(first, 0, 1, stride=EDGE, stride_axis=0),
            )
            target[q : q + 1, :] = jnp.sum(jnp.where(own_columns, columns, 0.0), axis=0, keepdims=True)
        target[RIM // 2 :, :] = jnp.zeros((8 - RIM // 2, LANES), F32)
    copies[5].wait()
    for sweep in range(2):
        lower = jnp.full((8, LANES), levels[2 * sweep])
        upper = jnp.full((8, LANES), levels[2 * sweep + 1])
        middle = 0.5 * (upper + lower)
        half = 0.5 * (upper - lower)
        spread = middle / half
        factor = 1.0 / spread
        values = [1.0 / middle]
        for step in range(DEG - 1):
            factor_next = 1.0 / (2.0 * spread - factor)
            values += [factor_next * factor, 2.0 * factor_next / half]
            factor = factor_next
        for n, value in enumerate(values):
            row = 8 * (sweep * (2 * DEG - 1) + n)
            coefficients[row : row + 8, :] = value


class Rows:
    def __init__(self, *pieces):
        self.pieces = pieces

    def place(self, row):
        for first, end, ref, start in self.pieces:
            if first <= row < end:
                return ref, slice(8 * (row - first + start), 8 * (row - first + start) + 8)
        raise IndexError(row)


def at(array, row):
    ref, place = array.place(row)
    return ref[place, :]


def put(array, row, value):
    ref, place = array.place(row)
    ref[place, :] = value


def to_left(value, shift):
    return pltpu.roll(value, LANES - shift, 1)


def to_right(value, shift):
    return pltpu.roll(value, shift, 1)


def spread(ref, base, height, left, side_block, target, first_row):
    blocks = [ref[base : base + height, LANES * j : LANES * j + LANES] for j in range(ref.shape[1] // LANES)]
    zero = jnp.zeros((height, LANES), F32)
    if side_block is None:
        blocks = [zero] + blocks + [zero]
    else:
        blocks = [jnp.where(left, zero, side_block)] + blocks + [jnp.where(left, side_block, zero)]
    lanes = lax.broadcasted_iota(jnp.int32, (height, LANES), 1)
    for s in range(SEGS):
        start = 96 * s - EDGE
        first = start // LANES
        offset = start - LANES * first
        merged = jnp.where(lanes >= offset, blocks[first + 1], blocks[first + 2])
        target[pl.ds(first_row * 8 + s, height, stride=8), :] = to_left(merged, offset)


def inside_columns(left, cols):
    column = 96 * lax.broadcasted_iota(jnp.int32, (8, LANES), 0) + lane_ids() - EDGE
    return jnp.where(left, (column >= 0).astype(F32), (column < cols).astype(F32))


def own_columns():
    lanes = lane_ids()
    return ((lanes >= EDGE) & (lanes < LANES - EDGE)).astype(F32)


def stiffness(visc, target, first, last, shift):
    paired = None
    for row in range(first, last + 1):
        k = at(visc, row)
        now = k + to_left(k, shift)
        if row > first:
            put(target, row - 1, 0.125 * (paired + now))
        paired = now


def edge_gradients(here, there):
    return here[0] + there[0], here[1] + there[1], there[0] - here[0], there[1] - here[1]


def cell_forces(s, one, two):
    a, b = two[0] - one[0], two[3] + one[3]
    c, d = two[2] + one[2], two[1] - one[1]
    both = a + b
    return s * (both + a), s * (both + b), (0.5 * s) * (c + d)


def forces(x, following, stiff, near, far, low, high, shift):
    def gradients(row):
        return edge_gradients([at(part, row) for part in x], [at(part, row) for part in following])

    here = gradients(low)
    before = cell_forces(at(stiff, low - 1), gradients(low - 1), here)
    for row in range(low, high):
        after = gradients(row + 1)
        now = cell_forces(at(stiff, row), here, after)
        shear, shear_step = before[2] + now[2], before[2] - now[2]
        normal_step, normal = before[0] - now[0], before[1] + now[1]
        put(near[0], row, normal_step - shear)
        put(near[1], row, shear_step - normal)
        put(far[0], row, to_right(normal_step + shear, shift))
        put(far[1], row, to_right(shear_step + normal, shift))
        here, before = after, now


def remaining(n, value, f, beta, near, far, row):
    return (at(f[n], row) - at(beta, row) * value) - (at(near[n], row) + at(far[n], row))


def begin(x, following, f, coefficients, rows, shift):
    inverse = coefficients[:8, :]
    for row in rows:
        for n in range(2):
            value = at(f[n], row) * inverse
            put(x[n], row, value)
            put(following[n], row, to_left(value, shift))


def advance(levels, followings, f, beta, stiff, near, far, coefficients, step, spans, mask_of):
    keep = coefficients[8 + 16 * step : 16 + 16 * step, :]
    gain = coefficients[16 + 16 * step : 24 + 16 * step, :]
    gains = {}
    x, new = levels[step], levels[step + 1]
    for low, high in spans:
        forces(x, followings[step], stiff, near, far, low, high, 1)
        for row in range(low, high):
            mask = mask_of(row)
            part = gains.setdefault(id(mask), gain * mask)
            for n in range(2):
                value = at(x[n], row)
                change = value if step == 0 else value - at(levels[step - 1][n], row)
                value = value + keep * change + part * remaining(n, value, f, beta, near, far, row)
                put(new[n], row, value)
                put(followings[step + 1][n], row, to_left(value, 1))


def restrict(source, target, i, scale=None):
    row = DEG + 2 * i
    pair = at(source, row) + at(source, row + 1)
    pair = pair + to_left(pair, 1)
    put(target, i, pair if scale is None else scale * pair)


def pairs_of(refs):
    return [tuple(refs[n : n + 2]) for n in range(0, len(refs), 2)]


def middle_kernel(coefficients, fields, side, *refs):
    rows, cols = fields.shape[1:]
    end = RIM + rows
    left = lax.axis_index("gy") == 0
    outs, scratch = refs[:-4], refs[-4:]
    own, cell_ref, squares_out = outs[:4], outs[4], outs[5]
    level_refs, following_refs = pairs_of(outs[6 : 6 + 2 * DEG]), pairs_of(outs[6 + 2 * DEG : 6 + 4 * DEG])
    residual_refs, coarse_refs = outs[6 + 4 * DEG : 8 + 4 * DEG], outs[8 + 4 * DEG :]
    for n in range(4):
        for h in range(0, rows, 8):
            spread(fields.at[n], h, 8, left, side[rows * n + h : rows * n + h + 8, :], own[n], h)

    def whole_rows(ref):
        return Rows((RIM, end, ref, 0))

    f_u, f_v, visc, beta = (whole_rows(ref) for ref in own)
    f = (f_u, f_v)
    cell = whole_rows(cell_ref)
    levels = [tuple(map(whole_rows, pair)) for pair in level_refs]
    followings = [tuple(map(whole_rows, pair)) for pair in following_refs]
    near, far = (tuple(map(whole_rows, pair)) for pair in pairs_of(scratch))
    inside = inside_columns(left, cols)
    stiffness(visc, cell, RIM, end - 1, 1)
    begin(levels[0], followings[0], f, coefficients, range(RIM, end), 1)
    for step in range(DEG - 1):
        span = (RIM + step + 1, end - step - 1)
        advance(levels, followings, f, beta, cell, near, far, coefficients, step, (span,), lambda row: inside)
    residual = tuple(map(whole_rows, residual_refs))
    low, high = RIM + DEG, end - DEG
    forces(levels[-1], followings[-1], cell, near, far, low, high, 1)
    squares = jnp.zeros((8, LANES), F32)
    for row in range(low, high):
        for n in range(2):
            value = inside * remaining(n, at(levels[-1][n], row), f, beta, near, far, row)
            put(residual[n], row, value)
            squares = squares + value * value
    squares_out[...] = squares
    rim = (RIM - DEG) // 2
    coarse = [Rows((rim, rim + rows // 2, ref, 0)) for ref in coarse_refs]
    for i in range(rim, rim + rows // 2):
        restrict(visc, coarse[0], i, 0.25)
        restrict(beta, coarse[1], i)
        if low <= DEG + 2 * i < high:
            restrict(residual[0], coarse[2], i)
            restrict(residual[1], coarse[3], i)


def main_kernel(coefficients, fields, velocity, from_x, from_z, side_x, side_z, middle, outs, scratch):
    multiplier, gradient, sums = outs
    scratch = list(scratch)
    rows, cols = gradient.shape
    total, end = rows + 2 * RIM, RIM + rows
    gx_at, gx_size = lax.axis_index("gx"), lax.axis_size("gx")
    low_half = gx_at % 2 == 0
    left = lax.axis_index("gy") == 0
    own, cell_ref, squares_ref = middle[:4], middle[4], middle[5]
    level_refs, following_refs = pairs_of(middle[6 : 6 + 2 * DEG]), pairs_of(middle[6 + 2 * DEG : 6 + 4 * DEG])
    residual_refs, coarse_refs = middle[6 + 4 * DEG : 8 + 4 * DEG], middle[8 + 4 * DEG :]

    def take(count):
        taken = scratch[:count]
        del scratch[:count]
        return taken

    rims = take(4)
    joint = [Rows((0, rows, ref, 0)) for ref in take(2)]
    for received, partner, corner, is_above in (
        (from_x, side_x, take(1)[0], jnp.logical_not(low_half)),
        (from_z, side_z, take(1)[0], low_half),
    ):
        near = jnp.where(is_above, RIM - 8, RIM)
        far = jnp.where(is_above, 0, RIM + 8)
        rolled = [to_left(partner[...], EDGE * i) if i else partner[...] for i in range(8)]
        for i in range(8):
            columns = jnp.where(left, rolled[i], rolled[(i + 1) % 8])
            corner[pl.ds(i, RIM // 2, stride=8), :] = columns[: RIM // 2]
        for n in range(4):
            spread(received, 8 * n, 8, left, corner[8 * n : 8 * n + 8, :], rims[n], near)
            spread(received, 32 + 2 * n, 2, left, corner[32 + 2 * n : 34 + 2 * n, :], rims[n], far)

    def joined(full, ref, margin):
        return Rows(
            (0, RIM + margin, full, 0),
            (RIM + margin, end - margin, ref, margin),
            (end - margin, total, full, end - margin),
        )

    f_u, f_v, visc, beta = (
        Rows((0, RIM, rim, 0), (RIM, end, ref, 0), (end, total, rim, RIM)) for rim, ref in zip(rims, own)
    )
    f = (f_u, f_v)
    cell_full = take(1)[0]
    cell = Rows((0, RIM, cell_full, 0), (RIM, end - 1, cell_ref, 0), (end - 1, total, cell_full, end - 1))
    levels = [tuple(joined(take(1)[0], ref, n) for ref in pair) for n, pair in enumerate(level_refs)]
    followings = [tuple(joined(take(1)[0], ref, n) for ref in pair) for n, pair in enumerate(following_refs)]
    residual = tuple(joined(take(1)[0], ref, DEG) for ref in residual_refs)
    near, far = (tuple(Rows((0, total, ref, 0)) for ref in take(2)) for _ in range(2))

    inside = inside_columns(left, cols)
    above = inside * jnp.where(gx_at > 0, 1.0, 0.0)
    below = inside * jnp.where(gx_at < gx_size - 1, 1.0, 0.0)

    def mask_of(row):
        return above if row < RIM else below if row >= end else inside

    stiffness(visc, cell, 0, RIM, 1)
    stiffness(visc, cell, end - 1, total - 1, 1)
    begin(levels[0], followings[0], f, coefficients, [*range(RIM), *range(end, total)], 1)
    for step in range(DEG - 1):
        spans = ((step + 1, RIM + step + 1), (end - step - 1, total - step - 1))
        advance(levels, followings, f, beta, cell, near, far, coefficients, step, spans, mask_of)
    x = levels[-1]
    squares = squares_ref[...]
    for low, high in ((DEG, RIM + DEG), (end - DEG, total - DEG)):
        forces(x, followings[-1], cell, near, far, low, high, 1)
        for row in range(low, high):
            for n in range(2):
                value = mask_of(row) * remaining(n, at(x[n], row), f, beta, near, far, row)
                put(residual[n], row, value)
                if RIM <= row < end:
                    squares = squares + value * value

    coarse_rim = (RIM - DEG) // 2
    count = rows // 2 + 2 * coarse_rim

    def coarse_joined(ref, margin):
        first, last = coarse_rim + margin, count - coarse_rim - margin
        full = take(1)[0]
        return Rows((0, first, full, 0), (first, last, ref, margin), (last, count, full, last))

    margins = (0, 0, DEG // 2, DEG // 2)
    coarse = [coarse_joined(ref, margin) for ref, margin in zip(coarse_refs, margins)]
    for source, target, margin, scale in zip((visc, beta, *residual), coarse, margins, (0.25, None, None, None)):
        for i in [*range(coarse_rim + margin), *range(count - coarse_rim - margin, count)]:
            restrict(source, target, i, scale)

    def plain():
        return Rows((0, count, take(1)[0], 0))

    stiff, stiff_before = plain(), plain()
    stiffness(coarse[0], stiff, 0, count - 1, 2)
    for row in range(count - 1):
        put(stiff_before, row, to_right(at(stiff, row), 2))
    c_beta, c_f = coarse[1], coarse[2:]
    c_x, c_old, following, previous = ((plain(), plain()) for _ in range(4))
    table = 8 * (2 * DEG - 1)

    def keep_both(n, row, value):
        put(following[n], row, to_left(value, 2))
        put(previous[n], row, to_right(value, 2))

    def gradients(row):
        here = [at(part, row) for part in c_x]
        after = [at(part, row) for part in following]
        before = [at(part, row) for part in previous]
        return edge_gradients(here, after), edge_gradients(before, here)

    def cells(row, one, two):
        return [cell_forces(at(s, row), p, q) for s, p, q in zip((stiff, stiff_before), one, two)]

    inverse = coefficients[table : table + 8, :]
    for row in range(count):
        for n in range(2):
            value = at(c_f[n], row) * inverse
            put(c_x[n], row, value)
            keep_both(n, row, value)
    for step in range(DEG - 1):
        keep = coefficients[table + 8 + 16 * step : table + 16 + 16 * step, :]
        gain = coefficients[table + 16 + 16 * step : table + 24 + 16 * step, :]
        gains = (gain * above, gain * inside, gain * below)
        low, high = step + 1, count - step - 1
        here = gradients(low)
        before = cells(low - 1, gradients(low - 1), here)
        for row in range(low, high):
            after = gradients(row + 1)
            now = cells(row, here, after)
            (xx0, yy0, xy0), (xx1, yy1, xy1) = (
                (p[0] - q[0], p[1] + q[1], (p[2] + q[2], p[2] - q[2])) for p, q in zip(before, now)
            )
            applied = ((xx0 - xy0[0]) + (xx1 + xy1[0]), (xy0[1] - yy0) + (xy1[1] + yy1))
            part = gains[0 if row < coarse_rim else 2 if row >= count - coarse_rim else 1]
            for n in range(2):
                value = at(c_x[n], row)
                change = value if step == 0 else value - at(c_old[n], row)
                left_over = (at(c_f[n], row) - at(c_beta, row) * value) - applied[n]
                value = value + keep * change + part * left_over
                put(c_old[n], row, value)
                if step < DEG - 2:
                    keep_both(n, row, value)
            here, before = after, now
        c_x, c_old = c_old, c_x

    lanes = lane_ids()
    for i in range(rows // 2):
        for n in range(2):
            correction = at(c_x[n], coarse_rim + i)
            correction = jnp.where(lanes % 2 == 0, correction, to_right(correction, 1))
            for row in (2 * i, 2 * i + 1):
                put(joint[n], row, at(x[n], RIM + row) + correction)

    gradient_squares = jnp.zeros((8, LANES), F32)
    for h in range(0, rows, 8):
        for j in range(cols // LANES):
            s = (LANES * j) // 96
            shift = LANES * j - 96 * s + EDGE
            border = 96 * (s + 1) - LANES * j
            columns = slice(LANES * j, LANES * j + LANES)
            product = None
            for n in range(2):
                source = joint[n].pieces[0][2]
                one = source[pl.ds(8 * h + s, 8, stride=8), :]
                two = source[pl.ds(8 * h + s + 1, 8, stride=8), :]
                value = jnp.where(lanes < border, to_left(one, shift), to_right(two, (96 - shift) % LANES))
                multiplier[n, h : h + 8, columns] = value
                term = velocity[n, h : h + 8, columns] * value
                product = term if product is None else product + term
            value = -fields[3, h : h + 8, columns] * product
            gradient[h : h + 8, columns] = value
            gradient_squares = gradient_squares + value * value
    pair = [jnp.sum(value, axis=0, keepdims=True) for value in (squares * own_columns(), gradient_squares)]
    sums[...] = jnp.broadcast_to(jnp.concatenate(pair, axis=1), sums.shape)


def scale_kernel(nodes, gathered, gradient, held_multiplier, scaled, norm, multiplier, scaled_out, norm_out, sems):
    copies = [
        pltpu.make_async_copy(source, target, sems.at[n])
        for n, (source, target) in enumerate(((held_multiplier, multiplier), (norm_out, norm), (scaled_out, scaled)))
    ]
    copies[0].start()
    residual_total = jnp.sum(gathered[:, :LANES], keepdims=True)
    gradient_total = jnp.sum(gathered[:, LANES:], keepdims=True)
    norm_out[...] = jnp.sqrt(residual_total / (2 * nodes))
    copies[1].start()
    scaled_out[...] = gradient[...] / jnp.sqrt(gradient_total / nodes + 1e-06)
    copies[2].start()
    for copy in copies:
        copy.wait()


def body(misfit, velocity, viscosity, friction, ice, grounded, bounds):
    rows, cols = viscosity.shape
    gx_size, gy_size = lax.axis_size("gx"), lax.axis_size("gy")
    assert gy_size == 2 and gx_size % 2 == 0 and cols == 96 * SEGS and rows == 16
    peers = gx_size * gy_size
    nodes = rows * cols * peers
    total = rows + 2 * RIM
    shaped = jax.ShapeDtypeStruct
    whole = pl.BlockSpec(memory_space=pltpu.VMEM)
    params = pltpu.CompilerParams(vmem_limit_bytes=32 * 1024 * 1024)

    held = pl.BlockSpec(memory_space=pltpu.HBM)
    fields, coefficients, x_send, z_send, side_send, x_corner, z_corner = pl.pallas_call(
        pack_kernel,
        out_shape=(
            shaped((4, rows, cols), F32),
            shaped((16 * (2 * DEG - 1), LANES), F32),
            shaped((4 * RIM, cols), F32),
            shaped((4 * RIM, cols), F32),
            shaped((4 * rows, LANES), F32),
            shaped((8, LANES), F32),
            shaped((8, LANES), F32),
        ),
        in_specs=[held] * 6,
        out_specs=[whole] * 7,
        scratch_shapes=[
            pltpu.SMEM((4,), F32),
            pltpu.VMEM((rows, cols), F32),
            pltpu.VMEM((rows, cols), F32),
            pltpu.VMEM((rows, cols), jnp.int32),
            pltpu.VMEM((rows, cols), jnp.int32),
            pltpu.SemaphoreType.DMA((6,)),
        ],
        compiler_params=params,
        name="pack",
    )(*(pltpu.with_memory_space_constraint(x, pltpu.HBM) for x in (bounds, misfit, viscosity, friction, ice, grounded)))

    x_pairs = [(i, i ^ 1) for i in range(gx_size)]
    z_pairs = [(2 * i + c, 2 * j + c) for i in range(1, gx_size - 1) for j in (i + 1 if i % 2 else i - 1,) for c in (0, 1)]
    z_pairs += [(2 * i + c, 2 * i + 1 - c) for i in (0, gx_size - 1) for c in (0, 1)]
    swap = [(0, 1), (1, 0)]
    from_x = lax.ppermute(x_send, "gx", x_pairs)
    from_z = lax.ppermute(z_send, AXES, z_pairs)
    side = lax.ppermute(side_send, "gy", swap)
    side_x = lax.ppermute(x_corner, AXES, [(2 * i + c, 2 * j + 1 - c) for i, j in x_pairs for c in (0, 1)])
    side_z = lax.ppermute(z_corner, AXES, [(i, j ^ 1 if 1 < i < 2 * gx_size - 2 else j) for i, j in z_pairs])

    fine = pltpu.VMEM((8 * total, LANES), F32)
    coarse = pltpu.VMEM((4 * total, LANES), F32)
    owned = pltpu.VMEM((8 * rows, LANES), F32)
    halved = pltpu.VMEM((4 * rows, LANES), F32)
    middle = pl.pallas_call(
        middle_kernel,
        out_shape=[owned] * 5 + [pltpu.VMEM((8, LANES), F32)] + [owned] * (4 * DEG + 2) + [halved] * 4,
        in_specs=[whole] * 3,
        out_specs=[whole] * (12 + 4 * DEG),
        scratch_shapes=[owned] * 4,
        compiler_params=params,
        name="middle",
    )(coefficients, fields, side)

    def leg_kernel(coefficients, fields, velocity, from_x, from_z, side_x, side_z, *refs):
        done, refs = refs[: len(middle)], refs[len(middle) :]
        main_kernel(coefficients, fields, velocity, from_x, from_z, side_x, side_z, done, refs[:3], refs[3:])

    rim = pltpu.VMEM((16 * RIM, LANES), F32)
    corner = pltpu.VMEM((4 * RIM, LANES), F32)
    held_multiplier, gradient, sums = pl.pallas_call(
        leg_kernel,
        out_shape=(
            pltpu.VMEM((2, rows, cols), F32),
            pltpu.VMEM((rows, cols), F32),
            shaped((peers, 2 * LANES), F32),
        ),
        in_specs=[whole] * (7 + len(middle)),
        out_specs=[whole] * 3,
        scratch_shapes=[rim] * 4 + [owned] * 2 + [corner] * 2 + [fine] * (7 + 4 * DEG) + [coarse] * 14,
        compiler_params=params,
        name="leg",
    )(coefficients, fields, velocity, from_x, from_z, side_x, side_z, *middle)

    gathered = lax.all_to_all(sums, AXES, 0, 0, tiled=True)
    scaled, norm, multiplier = pl.pallas_call(
        functools.partial(scale_kernel, nodes),
        out_shape=(
            pltpu.HBM((rows, cols), F32),
            pltpu.HBM((1, 1), F32),
            pltpu.HBM((2, rows, cols), F32),
        ),
        in_specs=[whole] * 3,
        out_specs=[held] * 3,
        scratch_shapes=[
            pltpu.VMEM((rows, cols), F32),
            pltpu.VMEM((1, 1), F32),
            pltpu.SemaphoreType.DMA((3,)),
        ],
        compiler_params=params,
        name="scale",
    )(gathered, gradient, held_multiplier)
    return multiplier, scaled, norm.reshape(1)


def solution(mesh):
    tile = P(("grp", "gx"), "gy")
    pair = P(None, ("grp", "gx"), "gy")
    return jax.shard_map(
        body,
        mesh=mesh,
        in_specs=(pair, pair, tile, tile, tile, tile, P("grp")),
        out_specs=(pair, tile, P("grp")),
        check_vma=False,
    )
```

```python
import functools

import jax
import jax.numpy as jnp
from jax import lax
from jax.experimental import pallas as pl
from jax.experimental.pallas import tpu as pltpu
from jax.sharding import PartitionSpec as P

DEG = 4
LANES = 128
SEGS = 8
RIM = 10
EDGE = 16
F32 = jnp.float32
AXES = ("gx", "gy")


def lane_ids():
    return lax.broadcasted_iota(jnp.int32, (8, LANES), 1)


def pack_kernel(
    bounds, misfit, visc, friction, ice, grounded,
    fields, coefficients, x_send, z_send, side_send, x_corner, z_corner,
    levels, visc_in, friction_in, ice_in, grounded_in, sems,
):
    copies = [
        pltpu.make_async_copy(source, target, sems.at[n])
        for n, (source, target) in enumerate((
            (misfit, fields.at[pl.ds(0, 2)]),
            (visc, visc_in),
            (ice, ice_in),
            (friction, friction_in),
            (grounded, grounded_in),
            (bounds, levels),
        ))
    ]
    for copy in copies:
        copy.start()
    rows, cols = visc.shape
    left = lax.axis_index("gy") == 0
    at, last_at = lax.axis_index("gx"), lax.axis_size("gx") - 1
    low_half = at % 2 == 0
    at_end = (at == 0) | (at == last_at)
    for copy in copies[:5]:
        copy.wait()
    fields[2] = visc_in[...] * ice_in[...].astype(F32)
    fields[3] = friction_in[...] * grounded_in[...].astype(F32)
    sublanes = lax.broadcasted_iota(jnp.int32, (8, cols), 0)
    down_tail = up_tail = jnp.zeros((8, cols), F32)
    for n in range(4):
        last, first = fields[n, rows - 8 :, :], fields[n, :8, :]
        x_send[8 * n : 8 * n + 8, :] = jnp.where(low_half, last, first)
        z_send[8 * n : 8 * n + 8, :] = jnp.where(at_end, 0.0, jnp.where(low_half, first, last))
        here = sublanes // 2 == n
        down_tail = jnp.where(here, pltpu.roll(fields[n, rows - 16 : rows - 8, :], (2 * n + 2) % 8, 0), down_tail)
        up_tail = jnp.where(here, pltpu.roll(fields[n, 8:16, :], 2 * n, 0), up_tail)
        side_send[rows * n : rows * n + rows, :] = jnp.where(
            left, fields[n, :, cols - LANES :], fields[n, :, :LANES]
        )
    x_send[32:, :] = jnp.where(low_half, down_tail, up_tail)
    z_send[32:, :] = jnp.where(at_end, 0.0, jnp.where(low_half, up_tail, down_tail))
    sublanes = sublanes[:, :LANES]
    own_columns_of = lane_ids() // EDGE == sublanes
    for source, target in ((x_send, x_corner), (z_send, z_corner)):
        packed = jnp.zeros((8, LANES), F32)
        for q in range(RIM // 2):
            last, first = source[8 * q : 8 * q + 8, cols - LANES :], source[8 * q : 8 * q + 8, :LANES]
            columns = jnp.where(
                left,
                pltpu.roll(last, EDGE, 1, stride=EDGE, stride_axis=0),
                pltpu.roll(first, 0, 1, stride=EDGE, stride_axis=0),
            )
            row = jnp.sum(jnp.where(own_columns_of, columns, 0.0), axis=0, keepdims=True)
            packed = jnp.where(sublanes == q, row, packed)
        target[...] = packed
    copies[5].wait()
    for sweep in range(2):
        lower = jnp.full((8, LANES), levels[2 * sweep])
        upper = jnp.full((8, LANES), levels[2 * sweep + 1])
        middle = 0.5 * (upper + lower)
        half = 0.5 * (upper - lower)
        spread = middle / half
        factor = 1.0 / spread
        values = [1.0 / middle]
        for step in range(DEG - 1):
            factor_next = 1.0 / (2.0 * spread - factor)
            values += [factor_next * factor, 2.0 * factor_next / half]
            factor = factor_next
        for n, value in enumerate(values):
            row = 8 * (sweep * (2 * DEG - 1) + n)
            coefficients[row : row + 8, :] = value


class Rows:
    def __init__(self, *pieces):
        self.pieces = pieces

    def place(self, row):
        for first, end, ref, start in self.pieces:
            if first <= row < end:
                return ref, slice(8 * (row - first + start), 8 * (row - first + start) + 8)
        raise IndexError(row)


def at(array, row):
    ref, place = array.place(row)
    return ref[place, :]


def put(array, row, value):
    ref, place = array.place(row)
    ref[place, :] = value


def to_left(value, shift):
    return pltpu.roll(value, LANES - shift, 1)


def to_right(value, shift):
    return pltpu.roll(value, shift, 1)


def spread(ref, base, height, left, side_block, target, first_row):
    blocks = [ref[base : base + height, LANES * j : LANES * j + LANES] for j in range(ref.shape[1] // LANES)]
    zero = jnp.zeros((height, LANES), F32)
    if side_block is None:
        blocks = [zero] + blocks + [zero]
    else:
        blocks = [jnp.where(left, zero, side_block)] + blocks + [jnp.where(left, side_block, zero)]
    lanes = lax.broadcasted_iota(jnp.int32, (height, LANES), 1)
    for s in range(SEGS):
        start = 96 * s - EDGE
        first = start // LANES
        offset = start - LANES * first
        merged = jnp.where(lanes >= offset, blocks[first + 1], blocks[first + 2])
        target[pl.ds(first_row * 8 + s, height, stride=8), :] = to_left(merged, offset)


def inside_columns(left, cols):
    column = 96 * lax.broadcasted_iota(jnp.int32, (8, LANES), 0) + lane_ids() - EDGE
    return jnp.where(left, (column >= 0).astype(F32), (column < cols).astype(F32))


def own_columns():
    lanes = lane_ids()
    return (lanes >= EDGE) & (lanes < LANES - EDGE)


def stiffness(visc, target, first, last, shift):
    paired = None
    for row in range(first, last + 1):
        k = at(visc, row)
        now = k + to_left(k, shift)
        if row > first:
            put(target, row - 1, 0.125 * (paired + now))
        paired = now


def edge_gradients(here, there):
    return here[0] + there[0], here[1] + there[1], there[0] - here[0], there[1] - here[1]


def cell_forces(s, one, two):
    a, b = two[0] - one[0], two[3] + one[3]
    c, d = two[2] + one[2], two[1] - one[1]
    both = a + b
    return s * (both + a), s * (both + b), (0.5 * s) * (c + d)


def forces(x, following, stiff, near, far, low, high, shift):
    def gradients(row):
        return edge_gradients([at(part, row) for part in x], [at(part, row) for part in following])

    here = gradients(low)
    before = cell_forces(at(stiff, low - 1), gradients(low - 1), here)
    for row in range(low, high):
        after = gradients(row + 1)
        now = cell_forces(at(stiff, row), here, after)
        shear, shear_step = before[2] + now[2], before[2] - now[2]
        normal_step, normal = before[0] - now[0], before[1] + now[1]
        put(near[0], row, normal_step - shear)
        put(near[1], row, shear_step - normal)
        put(far[0], row, to_right(normal_step + shear, shift))
        put(far[1], row, to_right(shear_step + normal, shift))
        here, before = after, now


def remaining(n, value, f, beta, near, far, row):
    return (at(f[n], row) - at(beta, row) * value) - (at(near[n], row) + at(far[n], row))


def begin(x, following, f, coefficients, rows, shift):
    inverse = coefficients[:8, :]
    for row in rows:
        for n in range(2):
            value = at(f[n], row) * inverse
            put(x[n], row, value)
            put(following[n], row, to_left(value, shift))


def advance(levels, followings, f, beta, stiff, near, far, coefficients, step, spans, mask_of):
    keep = coefficients[8 + 16 * step : 16 + 16 * step, :]
    gain = coefficients[16 + 16 * step : 24 + 16 * step, :]
    gains = {}
    x, new = levels[step], levels[step + 1]
    for low, high in spans:
        forces(x, followings[step], stiff, near, far, low, high, 1)
        for row in range(low, high):
            mask = mask_of(row)
            part = gains.setdefault(id(mask), gain * mask)
            for n in range(2):
                value = at(x[n], row)
                change = value if step == 0 else value - at(levels[step - 1][n], row)
                value = value + keep * change + part * remaining(n, value, f, beta, near, far, row)
                put(new[n], row, value)
                put(followings[step + 1][n], row, to_left(value, 1))


def restrict(source, i, lanes, scale=None):
    row = DEG + 2 * i
    pair = at(source, row) + at(source, row + 1)
    if scale is not None:
        pair = scale * pair
    even, odd = lanes != "odd", lanes != "even"
    if even and odd:
        return jnp.where(lane_ids() % 2 == 0, pair + to_left(pair, 1), pair + to_right(pair, 1))
    return pair + (to_left(pair, 1) if even else to_right(pair, 1))


def pairs_of(refs):
    return [tuple(refs[n : n + 2]) for n in range(0, len(refs), 2)]


def middle_kernel(coefficients, fields, side, *refs):
    rows, cols = fields.shape[1:]
    end = RIM + rows
    left = lax.axis_index("gy") == 0
    outs, scratch = refs[:-4], refs[-4:]
    own, cell_ref, squares_out = outs[:4], outs[4], outs[5]
    level_refs, following_refs = pairs_of(outs[6 : 6 + 2 * DEG]), pairs_of(outs[6 + 2 * DEG : 6 + 4 * DEG])
    residual_refs, coarse_refs = outs[6 + 4 * DEG : 8 + 4 * DEG], outs[8 + 4 * DEG :]
    for n in range(4):
        for h in range(0, rows, 8):
            spread(fields.at[n], h, 8, left, side[rows * n + h : rows * n + h + 8, :], own[n], h)

    def whole_rows(ref):
        return Rows((RIM, end, ref, 0))

    f_u, f_v, visc, beta = (whole_rows(ref) for ref in own)
    f = (f_u, f_v)
    cell = whole_rows(cell_ref)
    levels = [tuple(map(whole_rows, pair)) for pair in level_refs]
    followings = [tuple(map(whole_rows, pair)) for pair in following_refs]
    near, far = (tuple(map(whole_rows, pair)) for pair in pairs_of(scratch))
    inside = inside_columns(left, cols)
    stiffness(visc, cell, RIM, end - 1, 1)
    begin(levels[0], followings[0], f, coefficients, range(RIM, end), 1)
    for step in range(DEG - 1):
        span = (RIM + step + 1, end - step - 1)
        advance(levels, followings, f, beta, cell, near, far, coefficients, step, (span,), lambda row: inside)
    residual = tuple(map(whole_rows, residual_refs))
    low, high = RIM + DEG, end - DEG
    forces(levels[-1], followings[-1], cell, near, far, low, high, 1)
    squares = jnp.zeros((8, LANES), F32)
    for row in range(low, high):
        for n in range(2):
            value = inside * remaining(n, at(levels[-1][n], row), f, beta, near, far, row)
            put(residual[n], row, value)
            squares = squares + value * value
    squares_out[...] = squares
    rim = (RIM - DEG) // 2
    coarse = [Rows((rim, rim + rows // 2, ref, 0)) for ref in coarse_refs]
    for i in range(rim, rim + rows // 2):
        put(coarse[0], i, restrict(visc, i, "both", 0.25))
        put(coarse[1], i, restrict(beta, i, "both"))
        if low <= DEG + 2 * i < high:
            put(coarse[2], i, restrict(residual[0], i, "both"))
            put(coarse[3], i, restrict(residual[1], i, "both"))


def main_kernel(coefficients, fields, velocity, from_x, from_z, side_x, side_z, middle, outs, scratch):
    multiplier, gradient, sums = outs
    scratch = list(scratch)
    rows, cols = gradient.shape
    total, end = rows + 2 * RIM, RIM + rows
    gx_at, gx_size = lax.axis_index("gx"), lax.axis_size("gx")
    low_half = gx_at % 2 == 0
    left = lax.axis_index("gy") == 0
    own, cell_ref, squares_ref = middle[:4], middle[4], middle[5]
    level_refs, following_refs = pairs_of(middle[6 : 6 + 2 * DEG]), pairs_of(middle[6 + 2 * DEG : 6 + 4 * DEG])
    residual_refs, coarse_refs = middle[6 + 4 * DEG : 8 + 4 * DEG], middle[8 + 4 * DEG :]

    def take(count):
        taken = scratch[:count]
        del scratch[:count]
        return taken

    rims = take(4)
    tails = take(1)[0]
    joint = [Rows((0, rows, ref, 0)) for ref in take(2)]
    for received, partner, corner, is_above in (
        (from_x, side_x, take(1)[0], jnp.logical_not(low_half)),
        (from_z, side_z, take(1)[0], low_half),
    ):
        first_row = jnp.where(is_above, 0, 8)
        rolled = [to_left(partner[...], EDGE * i) if i else partner[...] for i in range(8)]
        for i in range(8):
            corner[pl.ds(i, 8, stride=8), :] = jnp.where(left, rolled[i], rolled[(i + 1) % 8])
        for n, target in enumerate((*rims, tails)):
            spread(received, 8 * n, 8, left, corner[8 * n : 8 * n + 8, :], target, first_row)

    def joined(full, ref, margin):
        return Rows(
            (0, RIM + margin, full, 0),
            (RIM + margin, end - margin, ref, margin),
            (end - margin, total, full, end - margin),
        )

    f_u, f_v, visc, beta = (
        Rows(
            (0, RIM - 8, tails, 2 * n),
            (RIM - 8, RIM, rims[n], 0),
            (RIM, end, own[n], 0),
            (end, end + 8, rims[n], 8),
            (end + 8, total, tails, 8 + 2 * n),
        )
        for n in range(4)
    )
    f = (f_u, f_v)
    cell_full = take(1)[0]
    cell = Rows((0, RIM, cell_full, 0), (RIM, end - 1, cell_ref, 0), (end - 1, total, cell_full, end - 1))
    levels = [tuple(joined(take(1)[0], ref, n) for ref in pair) for n, pair in enumerate(level_refs)]
    followings = [tuple(joined(take(1)[0], ref, n) for ref in pair) for n, pair in enumerate(following_refs)]
    residual = tuple(joined(take(1)[0], ref, DEG) for ref in residual_refs)
    near, far = (tuple(Rows((0, total, ref, 0)) for ref in take(2)) for _ in range(2))

    inside = inside_columns(left, cols)
    above = inside * jnp.where(gx_at > 0, 1.0, 0.0)
    below = inside * jnp.where(gx_at < gx_size - 1, 1.0, 0.0)

    def mask_of(row):
        return above if row < RIM else below if row >= end else inside

    stiffness(visc, cell, 0, RIM, 1)
    stiffness(visc, cell, end - 1, total - 1, 1)
    begin(levels[0], followings[0], f, coefficients, [*range(RIM), *range(end, total)], 1)
    for step in range(DEG - 1):
        spans = ((step + 1, RIM + step + 1), (end - step - 1, total - step - 1))
        advance(levels, followings, f, beta, cell, near, far, coefficients, step, spans, mask_of)
    x = levels[-1]
    squares = squares_ref[...]
    for low, high in ((DEG, RIM + DEG), (end - DEG, total - DEG)):
        forces(x, followings[-1], cell, near, far, low, high, 1)
        for row in range(low, high):
            for n in range(2):
                value = mask_of(row) * remaining(n, at(x[n], row), f, beta, near, far, row)
                put(residual[n], row, value)
                if RIM <= row < end:
                    squares = squares + value * value

    even = lane_ids() % 2 == 0
    coarse_rim = (RIM - DEG) // 2
    half = rows // 4
    count = half + 2 * coarse_rim

    def plain():
        return Rows((0, count, take(1)[0], 0))

    def packed(source, ref, margin, scale):
        first, last = coarse_rim + margin, coarse_rim + 2 * half - margin
        target = plain()
        for j in range(count):
            i, k = j, j + half
            one = at(Rows((first, last, ref, margin)), i) if first <= i < last else restrict(source, i, "even", scale)
            two = at(Rows((first, last, ref, margin)), k) if first <= k < last else restrict(source, k, "odd", scale)
            put(target, j, jnp.where(even, one, two))
        return target

    c_visc, c_beta, *c_f = (
        packed(source, ref, margin, scale)
        for source, ref, margin, scale in zip(
            (visc, beta, *residual), coarse_refs, (0, 0, DEG // 2, DEG // 2), (0.25, None, None, None)
        )
    )
    masks = [
        jnp.where(even, above if j < coarse_rim else inside, below if j >= count - coarse_rim else inside)
        for j in range(count)
    ]
    stiff, stiff_before = plain(), plain()
    stiffness(c_visc, stiff, 0, count - 1, 2)
    for row in range(count - 1):
        put(stiff_before, row, to_right(at(stiff, row), 2))
    table = 8 * (2 * DEG - 1)

    def gradients(here):
        after = [to_left(value, 2) for value in here]
        before = [to_right(value, 2) for value in here]
        return edge_gradients(here, after), edge_gradients(before, here)

    def cells(row, one, two):
        return [cell_forces(at(s, row), p, q) for s, p, q in zip((stiff, stiff_before), one, two)]

    inverse = coefficients[table : table + 8, :]
    c_x = [[at(part, row) * inverse for part in c_f] for row in range(count)]
    c_old = c_x
    for step in range(DEG - 1):
        keep = coefficients[table + 8 + 16 * step : table + 16 + 16 * step, :]
        gain = coefficients[table + 16 + 16 * step : table + 24 + 16 * step, :]
        low, high = step + 1, count - step - 1
        edges = {row: gradients(c_x[row]) for row in range(low - 1, high + 1)}
        forces_at = {row: cells(row, edges[row], edges[row + 1]) for row in range(low - 1, high)}
        c_new = list(c_x)
        for row in range(low, high):
            (xx0, yy0, xy0), (xx1, yy1, xy1) = (
                (p[0] - q[0], p[1] + q[1], (p[2] + q[2], p[2] - q[2]))
                for p, q in zip(forces_at[row - 1], forces_at[row])
            )
            applied = ((xx0 - xy0[0]) + (xx1 + xy1[0]), (xy0[1] - yy0) + (xy1[1] + yy1))
            part = gain * masks[row]
            c_new[row] = []
            for n in range(2):
                value = c_x[row][n]
                change = value if step == 0 else value - c_old[row][n]
                left_over = (at(c_f[n], row) - at(c_beta, row) * value) - applied[n]
                c_new[row].append(value + keep * change + part * left_over)
        c_x, c_old = c_new, c_x

    lanes = lane_ids()
    for i in range(half):
        for n in range(2):
            value = c_x[coarse_rim + i][n]
            corrections = jnp.where(even, value, to_right(value, 1)), jnp.where(even, to_left(value, 1), value)
            for first, correction in zip((2 * i, 2 * (i + half)), corrections):
                for row in (first, first + 1):
                    put(joint[n], row, at(x[n], RIM + row) + correction)

    gradient_squares = jnp.zeros((8, LANES), F32)
    for h in range(0, rows, 8):
        for j in range(cols // LANES):
            s = (LANES * j) // 96
            shift = LANES * j - 96 * s + EDGE
            border = 96 * (s + 1) - LANES * j
            columns = slice(LANES * j, LANES * j + LANES)
            product = None
            for n in range(2):
                source = joint[n].pieces[0][2]
                one = source[pl.ds(8 * h + s, 8, stride=8), :]
                two = source[pl.ds(8 * h + s + 1, 8, stride=8), :]
                value = jnp.where(lanes < border, to_left(one, shift), to_right(two, (96 - shift) % LANES))
                multiplier[n, h : h + 8, columns] = value
                term = velocity[n, h : h + 8, columns] * value
                product = term if product is None else product + term
            value = -fields[3, h : h + 8, columns] * product
            gradient[h : h + 8, columns] = value
            gradient_squares = gradient_squares + value * value
    pair = [jnp.sum(value, axis=0, keepdims=True) for value in (jnp.where(own_columns(), squares, 0.0), gradient_squares)]
    sums[...] = jnp.broadcast_to(jnp.concatenate(pair, axis=1), sums.shape)


def scale_kernel(nodes, gathered, gradient, held_multiplier, scaled, norm, multiplier, scaled_out, norm_out, sems):
    copies = [
        pltpu.make_async_copy(source, target, sems.at[n])
        for n, (source, target) in enumerate(((held_multiplier, multiplier), (norm_out, norm), (scaled_out, scaled)))
    ]
    copies[0].start()
    residual_total = jnp.sum(gathered[:, :LANES], keepdims=True)
    gradient_total = jnp.sum(gathered[:, LANES:], keepdims=True)
    norm_out[...] = jnp.sqrt(residual_total / (2 * nodes))
    copies[1].start()
    scaled_out[...] = gradient[...] / jnp.sqrt(gradient_total / nodes + 1e-06)
    copies[2].start()
    for copy in copies:
        copy.wait()


def body(misfit, velocity, viscosity, friction, ice, grounded, bounds):
    rows, cols = viscosity.shape
    gx_size, gy_size = lax.axis_size("gx"), lax.axis_size("gy")
    assert gy_size == 2 and gx_size % 2 == 0 and cols == 96 * SEGS and rows == 16
    peers = gx_size * gy_size
    nodes = rows * cols * peers
    total = rows + 2 * RIM
    shaped = jax.ShapeDtypeStruct
    whole = pl.BlockSpec(memory_space=pltpu.VMEM)
    params = pltpu.CompilerParams(vmem_limit_bytes=32 * 1024 * 1024)

    held = pl.BlockSpec(memory_space=pltpu.HBM)
    fields, coefficients, x_send, z_send, side_send, x_corner, z_corner = pl.pallas_call(
        pack_kernel,
        out_shape=(
            shaped((4, rows, cols), F32),
            shaped((16 * (2 * DEG - 1), LANES), F32),
            shaped((4 * RIM, cols), F32),
            shaped((4 * RIM, cols), F32),
            shaped((4 * rows, LANES), F32),
            shaped((8, LANES), F32),
            shaped((8, LANES), F32),
        ),
        in_specs=[held] * 6,
        out_specs=[whole] * 7,
        scratch_shapes=[
            pltpu.SMEM((4,), F32),
            pltpu.VMEM((rows, cols), F32),
            pltpu.VMEM((rows, cols), F32),
            pltpu.VMEM((rows, cols), jnp.int32),
            pltpu.VMEM((rows, cols), jnp.int32),
            pltpu.SemaphoreType.DMA((6,)),
        ],
        compiler_params=params,
        name="pack",
    )(*(pltpu.with_memory_space_constraint(x, pltpu.HBM) for x in (bounds, misfit, viscosity, friction, ice, grounded)))

    x_pairs = [(i, i ^ 1) for i in range(gx_size)]
    z_pairs = [(2 * i + c, 2 * j + c) for i in range(1, gx_size - 1) for j in (i + 1 if i % 2 else i - 1,) for c in (0, 1)]
    z_pairs += [(2 * i + c, 2 * i + 1 - c) for i in (0, gx_size - 1) for c in (0, 1)]
    swap = [(0, 1), (1, 0)]
    from_x = lax.ppermute(x_send, "gx", x_pairs)
    from_z = lax.ppermute(z_send, AXES, z_pairs)
    side = lax.ppermute(side_send, "gy", swap)
    side_x = lax.ppermute(x_corner, AXES, [(2 * i + c, 2 * j + 1 - c) for i, j in x_pairs for c in (0, 1)])
    side_z = lax.ppermute(z_corner, AXES, [(i, j ^ 1 if 1 < i < 2 * gx_size - 2 else j) for i, j in z_pairs])

    fine = pltpu.VMEM((8 * total, LANES), F32)
    coarse = pltpu.VMEM((4 * total, LANES), F32)
    owned = pltpu.VMEM((8 * rows, LANES), F32)
    halved = pltpu.VMEM((4 * rows, LANES), F32)
    middle = pl.pallas_call(
        middle_kernel,
        out_shape=[owned] * 5 + [pltpu.VMEM((8, LANES), F32)] + [owned] * (4 * DEG + 2) + [halved] * 4,
        in_specs=[whole] * 3,
        out_specs=[whole] * (12 + 4 * DEG),
        scratch_shapes=[owned] * 4,
        compiler_params=params,
        name="middle",
    )(coefficients, fields, side)

    def leg_kernel(coefficients, fields, velocity, from_x, from_z, side_x, side_z, *refs):
        done, refs = refs[: len(middle)], refs[len(middle) :]
        main_kernel(coefficients, fields, velocity, from_x, from_z, side_x, side_z, done, refs[:3], refs[3:])

    rim = pltpu.VMEM((8 * 16, LANES), F32)
    corner = pltpu.VMEM((8 * 8, LANES), F32)
    held_multiplier, gradient, sums = pl.pallas_call(
        leg_kernel,
        out_shape=(
            pltpu.VMEM((2, rows, cols), F32),
            pltpu.VMEM((rows, cols), F32),
            shaped((peers, 2 * LANES), F32),
        ),
        in_specs=[whole] * (7 + len(middle)),
        out_specs=[whole] * 3,
        scratch_shapes=[rim] * 5 + [owned] * 2 + [corner] * 2 + [fine] * (7 + 4 * DEG) + [coarse] * 14,
        compiler_params=params,
        name="leg",
    )(coefficients, fields, velocity, from_x, from_z, side_x, side_z, *middle)

    gathered = lax.all_to_all(sums, AXES, 0, 0, tiled=True)
    scaled, norm, multiplier = pl.pallas_call(
        functools.partial(scale_kernel, nodes),
        out_shape=(
            pltpu.HBM((rows, cols), F32),
            pltpu.HBM((1, 1), F32),
            pltpu.HBM((2, rows, cols), F32),
        ),
        in_specs=[whole] * 3,
        out_specs=[held] * 3,
        scratch_shapes=[
            pltpu.VMEM((rows, cols), F32),
            pltpu.VMEM((1, 1), F32),
            pltpu.SemaphoreType.DMA((3,)),
        ],
        compiler_params=params,
        name="scale",
    )(gathered, gradient, held_multiplier)
    return multiplier, scaled, norm.reshape(1)


def solution(mesh):
    tile = P(("grp", "gx"), "gy")
    pair = P(None, ("grp", "gx"), "gy")
    return jax.shard_map(
        body,
        mesh=mesh,
        in_specs=(pair, pair, tile, tile, tile, tile, P("grp")),
        out_specs=(pair, tile, P("grp")),
        check_vma=False,
    )
```

```python
import functools

import jax
import jax.numpy as jnp
from jax import lax
from jax.experimental import pallas as pl
from jax.experimental.pallas import tpu as pltpu
from jax.sharding import PartitionSpec as P

DEG = 4
LANES = 128
SEGS = 8
RIM = 10
EDGE = 16
F32 = jnp.float32
AXES = ("gx", "gy")


def lane_ids():
    return lax.broadcasted_iota(jnp.int32, (8, LANES), 1)


def rim_rows(fields, n, low_half):
    first, last = fields[n, :8, :], fields[n, 8:16, :]
    return jnp.where(low_half, last, first), jnp.where(low_half, first, last)


def rim_tail(fields, low_half):
    sublanes = lax.broadcasted_iota(jnp.int32, (8, fields.shape[2]), 0)
    down = up = jnp.zeros(sublanes.shape, F32)
    for n in range(4):
        here = sublanes // 2 == n
        down = jnp.where(here, pltpu.roll(fields[n, :8, :], (2 * n + 2) % 8, 0), down)
        up = jnp.where(here, pltpu.roll(fields[n, 8:16, :], 2 * n, 0), up)
    return jnp.where(low_half, down, up), jnp.where(low_half, up, down)


def first_pack_kernel(
    bounds, misfit, visc, friction, ice, grounded, fields, levels, x_send,
    levels_in, visc_in, friction_in, ice_in, grounded_in, sems,
):
    copies = [
        pltpu.make_async_copy(source, target, sems.at[n])
        for n, (source, target) in enumerate((
            (misfit, fields.at[pl.ds(0, 2)]),
            (visc, visc_in),
            (ice, ice_in),
            (friction, friction_in),
            (grounded, grounded_in),
            (bounds, levels_in),
        ))
    ]
    for copy in copies:
        copy.start()
    low_half = lax.axis_index("gx") % 2 == 0
    for copy in copies:
        copy.wait()
    fields[2] = visc_in[...] * ice_in[...].astype(F32)
    fields[3] = friction_in[...] * grounded_in[...].astype(F32)
    for n in range(4):
        x_send[8 * n : 8 * n + 8, :] = rim_rows(fields, n, low_half)[0]
        levels[8 * n : 8 * n + 8, :] = jnp.full((8, LANES), levels_in[n])
    x_send[32:, :] = rim_tail(fields, low_half)[0]


def second_pack_kernel(fields, levels, x_send, coefficients, z_send, side_send, x_corner, z_corner):
    rows, cols = fields.shape[1:]
    left = lax.axis_index("gy") == 0
    position, last_position = lax.axis_index("gx"), lax.axis_size("gx") - 1
    low_half = position % 2 == 0
    at_end = (position == 0) | (position == last_position)
    for n in range(4):
        z_send[8 * n : 8 * n + 8, :] = jnp.where(at_end, 0.0, rim_rows(fields, n, low_half)[1])
        side_send[rows * n : rows * n + rows, :] = jnp.where(
            left, fields[n, :, cols - LANES :], fields[n, :, :LANES]
        )
    z_send[32:, :] = jnp.where(at_end, 0.0, rim_tail(fields, low_half)[1])
    sublanes = lax.broadcasted_iota(jnp.int32, (8, LANES), 0)
    own_columns_of = lane_ids() // EDGE == sublanes
    for source, target in ((x_send, x_corner), (z_send, z_corner)):
        packed = jnp.zeros((8, LANES), F32)
        for q in range(RIM // 2):
            last, first = source[8 * q : 8 * q + 8, cols - LANES :], source[8 * q : 8 * q + 8, :LANES]
            columns = jnp.where(
                left,
                pltpu.roll(last, EDGE, 1, stride=EDGE, stride_axis=0),
                pltpu.roll(first, 0, 1, stride=EDGE, stride_axis=0),
            )
            row = jnp.sum(jnp.where(own_columns_of, columns, 0.0), axis=0, keepdims=True)
            packed = jnp.where(sublanes == q, row, packed)
        target[...] = packed
    for sweep in range(2):
        lower, upper = levels[16 * sweep : 16 * sweep + 8, :], levels[16 * sweep + 8 : 16 * sweep + 16, :]
        middle = 0.5 * (upper + lower)
        half = 0.5 * (upper - lower)
        ratio = middle / half
        factor = 1.0 / ratio
        values = [1.0 / middle]
        for step in range(DEG - 1):
            factor_next = 1.0 / (2.0 * ratio - factor)
            values += [factor_next * factor, 2.0 * factor_next / half]
            factor = factor_next
        for n, value in enumerate(values):
            row = 8 * (sweep * (2 * DEG - 1) + n)
            coefficients[row : row + 8, :] = value


class Rows:
    def __init__(self, *pieces):
        self.pieces = pieces

    def place(self, row):
        for first, end, ref, start in self.pieces:
            if first <= row < end:
                return ref, slice(8 * (row - first + start), 8 * (row - first + start) + 8)
        raise IndexError(row)


def at(array, row):
    ref, place = array.place(row)
    return ref[place, :]


def put(array, row, value):
    ref, place = array.place(row)
    ref[place, :] = value


def to_left(value, shift):
    return pltpu.roll(value, LANES - shift, 1)


def to_right(value, shift):
    return pltpu.roll(value, shift, 1)


def spread(ref, base, height, left, side_block, target, first_row):
    blocks = [ref[base : base + height, LANES * j : LANES * j + LANES] for j in range(ref.shape[1] // LANES)]
    zero = jnp.zeros((height, LANES), F32)
    if side_block is None:
        blocks = [zero] + blocks + [zero]
    else:
        blocks = [jnp.where(left, zero, side_block)] + blocks + [jnp.where(left, side_block, zero)]
    lanes = lax.broadcasted_iota(jnp.int32, (height, LANES), 1)
    for s in range(SEGS):
        start = 96 * s - EDGE
        first = start // LANES
        offset = start - LANES * first
        merged = jnp.where(lanes >= offset, blocks[first + 1], blocks[first + 2])
        target[pl.ds(first_row * 8 + s, height, stride=8), :] = to_left(merged, offset)


def inside_columns(left, cols):
    column = 96 * lax.broadcasted_iota(jnp.int32, (8, LANES), 0) + lane_ids() - EDGE
    return jnp.where(left, (column >= 0).astype(F32), (column < cols).astype(F32))


def own_columns():
    lanes = lane_ids()
    return (lanes >= EDGE) & (lanes < LANES - EDGE)


def stiffness(visc, target, first, last, shift):
    paired = None
    for row in range(first, last + 1):
        k = at(visc, row)
        now = k + to_left(k, shift)
        if row > first:
            put(target, row - 1, 0.125 * (paired + now))
        paired = now


def edge_gradients(here, there):
    return here[0] + there[0], here[1] + there[1], there[0] - here[0], there[1] - here[1]


def cell_forces(s, one, two):
    a, b = two[0] - one[0], two[3] + one[3]
    c, d = two[2] + one[2], two[1] - one[1]
    both = a + b
    return s * (both + a), s * (both + b), (0.5 * s) * (c + d)


def forces(x, following, stiff, low, high, shift):
    applied = {}
    def gradients(row):
        return edge_gradients([at(part, row) for part in x], [at(part, row) for part in following])

    here = gradients(low)
    before = cell_forces(at(stiff, low - 1), gradients(low - 1), here)
    for row in range(low, high):
        after = gradients(row + 1)
        now = cell_forces(at(stiff, row), here, after)
        shear, shear_step = before[2] + now[2], before[2] - now[2]
        normal_step, normal = before[0] - now[0], before[1] + now[1]
        applied[row] = (
            (normal_step - shear, to_right(normal_step + shear, shift)),
            (shear_step - normal, to_right(shear_step + normal, shift)),
        )
        here, before = after, now
    return applied


def remaining(n, value, f, beta, applied, row):
    return (at(f[n], row) - at(beta, row) * value) - (applied[row][n][0] + applied[row][n][1])


def begin(x, following, f, coefficients, rows, shift):
    inverse = coefficients[:8, :]
    for row in rows:
        for n in range(2):
            value = at(f[n], row) * inverse
            put(x[n], row, value)
            put(following[n], row, to_left(value, shift))


def advance(levels, followings, f, beta, stiff, coefficients, step, spans, mask_of):
    keep = coefficients[8 + 16 * step : 16 + 16 * step, :]
    gain = coefficients[16 + 16 * step : 24 + 16 * step, :]
    gains = {}
    x, new = levels[step], levels[step + 1]
    applied = {}
    for low, high in spans:
        applied.update(forces(x, followings[step], stiff, low, high, 1))
    for low, high in spans:
        for row in range(low, high):
            mask = mask_of(row)
            part = gains.setdefault(id(mask), gain * mask)
            for n in range(2):
                value = at(x[n], row)
                change = value if step == 0 else value - at(levels[step - 1][n], row)
                value = value + keep * change + part * remaining(n, value, f, beta, applied, row)
                put(new[n], row, value)
                put(followings[step + 1][n], row, to_left(value, 1))


def restrict(source, i, lanes, scale=None):
    row = DEG + 2 * i
    pair = at(source, row) + at(source, row + 1)
    if scale is not None:
        pair = scale * pair
    even, odd = lanes != "odd", lanes != "even"
    if even and odd:
        return jnp.where(lane_ids() % 2 == 0, pair + to_left(pair, 1), pair + to_right(pair, 1))
    return pair + (to_left(pair, 1) if even else to_right(pair, 1))


def pairs_of(refs):
    return [tuple(refs[n : n + 2]) for n in range(0, len(refs), 2)]


def middle_kernel(coefficients, fields, side, *refs):
    rows, cols = fields.shape[1:]
    end = RIM + rows
    left = lax.axis_index("gy") == 0
    outs = refs
    own, cell_ref, squares_out = outs[:4], outs[4], outs[5]
    level_refs, following_refs = pairs_of(outs[6 : 6 + 2 * DEG]), pairs_of(outs[6 + 2 * DEG : 6 + 4 * DEG])
    residual_refs, coarse_refs = outs[6 + 4 * DEG : 8 + 4 * DEG], outs[8 + 4 * DEG :]
    for n in range(4):
        for h in range(0, rows, 8):
            spread(fields.at[n], h, 8, left, side[rows * n + h : rows * n + h + 8, :], own[n], h)

    def whole_rows(ref):
        return Rows((RIM, end, ref, 0))

    f_u, f_v, visc, beta = (whole_rows(ref) for ref in own)
    f = (f_u, f_v)
    cell = whole_rows(cell_ref)
    levels = [tuple(map(whole_rows, pair)) for pair in level_refs]
    followings = [tuple(map(whole_rows, pair)) for pair in following_refs]
    inside = inside_columns(left, cols)
    stiffness(visc, cell, RIM, end - 1, 1)
    begin(levels[0], followings[0], f, coefficients, range(RIM, end), 1)
    for step in range(DEG - 1):
        span = (RIM + step + 1, end - step - 1)
        advance(levels, followings, f, beta, cell, coefficients, step, (span,), lambda row: inside)
    residual = tuple(map(whole_rows, residual_refs))
    low, high = RIM + DEG, end - DEG
    applied = forces(levels[-1], followings[-1], cell, low, high, 1)
    squares = jnp.zeros((8, LANES), F32)
    for row in range(low, high):
        for n in range(2):
            value = inside * remaining(n, at(levels[-1][n], row), f, beta, applied, row)
            put(residual[n], row, value)
            squares = squares + value * value
    squares_out[...] = squares
    rim = (RIM - DEG) // 2
    coarse = [Rows((rim, rim + rows // 2, ref, 0)) for ref in coarse_refs]
    for i in range(rim, rim + rows // 2):
        put(coarse[0], i, restrict(visc, i, "both", 0.25))
        put(coarse[1], i, restrict(beta, i, "both"))
        if low <= DEG + 2 * i < high:
            put(coarse[2], i, restrict(residual[0], i, "both"))
            put(coarse[3], i, restrict(residual[1], i, "both"))


def main_kernel(coefficients, fields, velocity, from_x, from_z, side_x, side_z, middle, outs, scratch):
    multiplier, gradient, sums = outs
    scratch = list(scratch)
    rows, cols = gradient.shape
    total, end = rows + 2 * RIM, RIM + rows
    gx_at, gx_size = lax.axis_index("gx"), lax.axis_size("gx")
    low_half = gx_at % 2 == 0
    left = lax.axis_index("gy") == 0
    own, cell_ref, squares_ref = middle[:4], middle[4], middle[5]
    level_refs, following_refs = pairs_of(middle[6 : 6 + 2 * DEG]), pairs_of(middle[6 + 2 * DEG : 6 + 4 * DEG])
    residual_refs, coarse_refs = middle[6 + 4 * DEG : 8 + 4 * DEG], middle[8 + 4 * DEG :]

    def take(count):
        taken = scratch[:count]
        del scratch[:count]
        return taken

    rims = take(4)
    tails = take(1)[0]
    joint = [Rows((0, rows, ref, 0)) for ref in take(2)]
    for received, partner, corner, is_above in (
        (from_x, side_x, take(1)[0], jnp.logical_not(low_half)),
        (from_z, side_z, take(1)[0], low_half),
    ):
        first_row = jnp.where(is_above, 0, 8)
        rolled = [to_left(partner[...], EDGE * i) if i else partner[...] for i in range(8)]
        for i in range(8):
            corner[pl.ds(i, 8, stride=8), :] = jnp.where(left, rolled[i], rolled[(i + 1) % 8])
        for n, target in enumerate((*rims, tails)):
            spread(received, 8 * n, 8, left, corner[8 * n : 8 * n + 8, :], target, first_row)

    def joined(full, ref, margin):
        return Rows(
            (0, RIM + margin, full, 0),
            (RIM + margin, end - margin, ref, margin),
            (end - margin, total, full, end - margin),
        )

    f_u, f_v, visc, beta = (
        Rows(
            (0, RIM - 8, tails, 2 * n),
            (RIM - 8, RIM, rims[n], 0),
            (RIM, end, own[n], 0),
            (end, end + 8, rims[n], 8),
            (end + 8, total, tails, 8 + 2 * n),
        )
        for n in range(4)
    )
    f = (f_u, f_v)
    cell_full = take(1)[0]
    cell = Rows((0, RIM, cell_full, 0), (RIM, end - 1, cell_ref, 0), (end - 1, total, cell_full, end - 1))
    levels = [tuple(joined(take(1)[0], ref, n) for ref in pair) for n, pair in enumerate(level_refs)]
    followings = [tuple(joined(take(1)[0], ref, n) for ref in pair) for n, pair in enumerate(following_refs)]
    residual = tuple(joined(take(1)[0], ref, DEG) for ref in residual_refs)

    inside = inside_columns(left, cols)
    above = inside * jnp.where(gx_at > 0, 1.0, 0.0)
    below = inside * jnp.where(gx_at < gx_size - 1, 1.0, 0.0)

    def mask_of(row):
        return above if row < RIM else below if row >= end else inside

    stiffness(visc, cell, 0, RIM, 1)
    stiffness(visc, cell, end - 1, total - 1, 1)
    begin(levels[0], followings[0], f, coefficients, [*range(RIM), *range(end, total)], 1)
    for step in range(DEG - 1):
        spans = ((step + 1, RIM + step + 1), (end - step - 1, total - step - 1))
        advance(levels, followings, f, beta, cell, coefficients, step, spans, mask_of)
    x = levels[-1]
    squares = squares_ref[...]
    for low, high in ((DEG, RIM + DEG), (end - DEG, total - DEG)):
        applied = forces(x, followings[-1], cell, low, high, 1)
        for row in range(low, high):
            for n in range(2):
                value = mask_of(row) * remaining(n, at(x[n], row), f, beta, applied, row)
                put(residual[n], row, value)
                if RIM <= row < end:
                    squares = squares + value * value

    even = lane_ids() % 2 == 0
    coarse_rim = (RIM - DEG) // 2
    half = rows // 4
    count = half + 2 * coarse_rim

    def plain():
        return Rows((0, count, take(1)[0], 0))

    def packed(source, ref, margin, scale):
        first, last = coarse_rim + margin, coarse_rim + 2 * half - margin
        target = plain()
        for j in range(count):
            i, k = j, j + half
            one = at(Rows((first, last, ref, margin)), i) if first <= i < last else restrict(source, i, "even", scale)
            two = at(Rows((first, last, ref, margin)), k) if first <= k < last else restrict(source, k, "odd", scale)
            put(target, j, jnp.where(even, one, two))
        return target

    c_visc, c_beta, *c_f = (
        packed(source, ref, margin, scale)
        for source, ref, margin, scale in zip(
            (visc, beta, *residual), coarse_refs, (0, 0, DEG // 2, DEG // 2), (0.25, None, None, None)
        )
    )
    masks = [
        jnp.where(even, above if j < coarse_rim else inside, below if j >= count - coarse_rim else inside)
        for j in range(count)
    ]
    stiff, stiff_before = plain(), plain()
    stiffness(c_visc, stiff, 0, count - 1, 2)
    for row in range(count - 1):
        put(stiff_before, row, to_right(at(stiff, row), 2))
    table = 8 * (2 * DEG - 1)

    def gradients(here):
        after = [to_left(value, 2) for value in here]
        before = [to_right(value, 2) for value in here]
        return edge_gradients(here, after), edge_gradients(before, here)

    def cells(row, one, two):
        return [cell_forces(at(s, row), p, q) for s, p, q in zip((stiff, stiff_before), one, two)]

    inverse = coefficients[table : table + 8, :]
    c_x = [[at(part, row) * inverse for part in c_f] for row in range(count)]
    c_old = c_x
    for step in range(DEG - 1):
        keep = coefficients[table + 8 + 16 * step : table + 16 + 16 * step, :]
        gain = coefficients[table + 16 + 16 * step : table + 24 + 16 * step, :]
        low, high = step + 1, count - step - 1
        edges = {row: gradients(c_x[row]) for row in range(low - 1, high + 1)}
        forces_at = {row: cells(row, edges[row], edges[row + 1]) for row in range(low - 1, high)}
        c_new = list(c_x)
        for row in range(low, high):
            (xx0, yy0, xy0), (xx1, yy1, xy1) = (
                (p[0] - q[0], p[1] + q[1], (p[2] + q[2], p[2] - q[2]))
                for p, q in zip(forces_at[row - 1], forces_at[row])
            )
            applied = ((xx0 - xy0[0]) + (xx1 + xy1[0]), (xy0[1] - yy0) + (xy1[1] + yy1))
            part = gain * masks[row]
            c_new[row] = []
            for n in range(2):
                value = c_x[row][n]
                change = value if step == 0 else value - c_old[row][n]
                left_over = (at(c_f[n], row) - at(c_beta, row) * value) - applied[n]
                c_new[row].append(value + keep * change + part * left_over)
        c_x, c_old = c_new, c_x

    lanes = lane_ids()
    for i in range(half):
        for n in range(2):
            value = c_x[coarse_rim + i][n]
            corrections = jnp.where(even, value, to_right(value, 1)), jnp.where(even, to_left(value, 1), value)
            for first, correction in zip((2 * i, 2 * (i + half)), corrections):
                for row in (first, first + 1):
                    put(joint[n], row, at(x[n], RIM + row) + correction)

    gradient_squares = jnp.zeros((8, LANES), F32)
    for h in range(0, rows, 8):
        for j in range(cols // LANES):
            s = (LANES * j) // 96
            shift = LANES * j - 96 * s + EDGE
            border = 96 * (s + 1) - LANES * j
            columns = slice(LANES * j, LANES * j + LANES)
            product = None
            for n in range(2):
                source = joint[n].pieces[0][2]
                one = source[pl.ds(8 * h + s, 8, stride=8), :]
                two = source[pl.ds(8 * h + s + 1, 8, stride=8), :]
                value = jnp.where(lanes < border, to_left(one, shift), to_right(two, (96 - shift) % LANES))
                multiplier[n, h : h + 8, columns] = value
                term = velocity[n, h : h + 8, columns] * value
                product = term if product is None else product + term
            value = -fields[3, h : h + 8, columns] * product
            gradient[h : h + 8, columns] = value
            gradient_squares = gradient_squares + value * value
    pair = [jnp.sum(value, axis=0, keepdims=True) for value in (jnp.where(own_columns(), squares, 0.0), gradient_squares)]
    sums[...] = jnp.broadcast_to(jnp.concatenate(pair, axis=1), sums.shape)


def scale_kernel(nodes, gathered, gradient, held_multiplier, scaled, norm, multiplier, scaled_out, norm_out, sems):
    copies = [
        pltpu.make_async_copy(source, target, sems.at[n])
        for n, (source, target) in enumerate(((held_multiplier, multiplier), (norm_out, norm), (scaled_out, scaled)))
    ]
    copies[0].start()
    residual_total = jnp.sum(gathered[:, :LANES], keepdims=True)
    gradient_total = jnp.sum(gathered[:, LANES:], keepdims=True)
    norm_out[...] = jnp.sqrt(residual_total / (2 * nodes))
    copies[1].start()
    scaled_out[...] = gradient[...] / jnp.sqrt(gradient_total / nodes + 1e-06)
    copies[2].start()
    for copy in copies:
        copy.wait()


def body(misfit, velocity, viscosity, friction, ice, grounded, bounds):
    rows, cols = viscosity.shape
    gx_size, gy_size = lax.axis_size("gx"), lax.axis_size("gy")
    assert gy_size == 2 and gx_size % 2 == 0 and cols == 96 * SEGS and rows == 16
    peers = gx_size * gy_size
    nodes = rows * cols * peers
    total = rows + 2 * RIM
    shaped = jax.ShapeDtypeStruct
    whole = pl.BlockSpec(memory_space=pltpu.VMEM)
    params = pltpu.CompilerParams(vmem_limit_bytes=32 * 1024 * 1024)

    held = pl.BlockSpec(memory_space=pltpu.HBM)
    inputs = (bounds, misfit, viscosity, friction, ice, grounded)
    fields, levels, x_send = pl.pallas_call(
        first_pack_kernel,
        out_shape=(shaped((4, rows, cols), F32), shaped((32, LANES), F32), shaped((4 * RIM, cols), F32)),
        in_specs=[held] * 6,
        out_specs=[whole] * 3,
        scratch_shapes=[
            pltpu.SMEM((4,), F32),
            pltpu.VMEM((rows, cols), F32),
            pltpu.VMEM((rows, cols), F32),
            pltpu.VMEM((rows, cols), jnp.int32),
            pltpu.VMEM((rows, cols), jnp.int32),
            pltpu.SemaphoreType.DMA((6,)),
        ],
        compiler_params=params,
        name="first_pack",
    )(*(pltpu.with_memory_space_constraint(x, pltpu.HBM) for x in inputs))
    coefficients, z_send, side_send, x_corner, z_corner = pl.pallas_call(
        second_pack_kernel,
        out_shape=(
            shaped((16 * (2 * DEG - 1), LANES), F32),
            shaped((4 * RIM, cols), F32),
            shaped((4 * rows, LANES), F32),
            shaped((8, LANES), F32),
            shaped((8, LANES), F32),
        ),
        in_specs=[whole] * 3,
        out_specs=[whole] * 5,
        compiler_params=params,
        name="second_pack",
    )(fields, levels, x_send)

    x_pairs = [(i, i ^ 1) for i in range(gx_size)]
    z_pairs = [(2 * i + c, 2 * j + c) for i in range(1, gx_size - 1) for j in (i + 1 if i % 2 else i - 1,) for c in (0, 1)]
    z_pairs += [(2 * i + c, 2 * i + 1 - c) for i in (0, gx_size - 1) for c in (0, 1)]
    swap = [(0, 1), (1, 0)]
    from_x = lax.ppermute(x_send, "gx", x_pairs)
    from_z = lax.ppermute(z_send, AXES, z_pairs)
    side = lax.ppermute(side_send, "gy", swap)
    side_x = lax.ppermute(x_corner, AXES, [(2 * i + c, 2 * j + 1 - c) for i, j in x_pairs for c in (0, 1)])
    side_z = lax.ppermute(z_corner, AXES, [(i, j ^ 1 if 1 < i < 2 * gx_size - 2 else j) for i, j in z_pairs])

    fine = pltpu.VMEM((8 * total, LANES), F32)
    coarse = pltpu.VMEM((4 * total, LANES), F32)
    owned = pltpu.VMEM((8 * rows, LANES), F32)
    halved = pltpu.VMEM((4 * rows, LANES), F32)
    middle = pl.pallas_call(
        middle_kernel,
        out_shape=[owned] * 5 + [pltpu.VMEM((8, LANES), F32)] + [owned] * (4 * DEG + 2) + [halved] * 4,
        in_specs=[whole] * 3,
        out_specs=[whole] * (12 + 4 * DEG),
        compiler_params=params,
        name="middle",
    )(coefficients, fields, side)

    def leg_kernel(coefficients, fields, velocity, from_x, from_z, side_x, side_z, *refs):
        done, refs = refs[: len(middle)], refs[len(middle) :]
        main_kernel(coefficients, fields, velocity, from_x, from_z, side_x, side_z, done, refs[:3], refs[3:])

    rim = pltpu.VMEM((8 * 16, LANES), F32)
    corner = pltpu.VMEM((8 * 8, LANES), F32)
    held_multiplier, gradient, sums = pl.pallas_call(
        leg_kernel,
        out_shape=(
            pltpu.VMEM((2, rows, cols), F32),
            pltpu.VMEM((rows, cols), F32),
            shaped((peers, 2 * LANES), F32),
        ),
        in_specs=[whole] * (7 + len(middle)),
        out_specs=[whole] * 3,
        scratch_shapes=[rim] * 5 + [owned] * 2 + [corner] * 2 + [fine] * (3 + 4 * DEG) + [coarse] * 14,
        compiler_params=params,
        name="leg",
    )(coefficients, fields, velocity, from_x, from_z, side_x, side_z, *middle)

    gathered = lax.all_to_all(sums, AXES, 0, 0, tiled=True)
    scaled, norm, multiplier = pl.pallas_call(
        functools.partial(scale_kernel, nodes),
        out_shape=(
            pltpu.HBM((rows, cols), F32),
            pltpu.HBM((1, 1), F32),
            pltpu.HBM((2, rows, cols), F32),
        ),
        in_specs=[whole] * 3,
        out_specs=[held] * 3,
        scratch_shapes=[
            pltpu.VMEM((rows, cols), F32),
            pltpu.VMEM((1, 1), F32),
            pltpu.SemaphoreType.DMA((3,)),
        ],
        compiler_params=params,
        name="scale",
    )(gathered, gradient, held_multiplier)
    return multiplier, scaled, norm.reshape(1)


def solution(mesh):
    tile = P(("grp", "gx"), "gy")
    pair = P(None, ("grp", "gx"), "gy")
    return jax.shard_map(
        body,
        mesh=mesh,
        in_specs=(pair, pair, tile, tile, tile, tile, P("grp")),
        out_specs=(pair, tile, P("grp")),
        check_vma=False,
    )
```

```python
import functools

import jax
import jax.numpy as jnp
from jax import lax
from jax.experimental import pallas as pl
from jax.experimental.pallas import tpu as pltpu
from jax.sharding import PartitionSpec as P

DEG = 4
LANES = 128
SEGS = 8
RIM = 10
EDGE = 16
F32 = jnp.float32
AXES = ("gx", "gy")


def lane_ids():
    return lax.broadcasted_iota(jnp.int32, (8, LANES), 1)


def rim_rows(fields, n, low_half):
    first, last = fields[n, :8, :], fields[n, 8:16, :]
    return jnp.where(low_half, last, first), jnp.where(low_half, first, last)


def rim_tail(fields, low_half):
    sublanes = lax.broadcasted_iota(jnp.int32, (8, fields.shape[2]), 0)
    down = up = jnp.zeros(sublanes.shape, F32)
    for n in range(4):
        here = sublanes // 2 == n
        down = jnp.where(here, pltpu.roll(fields[n, :8, :], (2 * n + 2) % 8, 0), down)
        up = jnp.where(here, pltpu.roll(fields[n, 8:16, :], 2 * n, 0), up)
    return jnp.where(low_half, down, up), jnp.where(low_half, up, down)


def first_pack_kernel(
    bounds, misfit, visc, friction, ice, grounded, fields, levels, x_send,
    levels_in, visc_in, friction_in, ice_in, grounded_in, sems,
):
    copies = [
        pltpu.make_async_copy(source, target, sems.at[n])
        for n, (source, target) in enumerate((
            (misfit, fields.at[pl.ds(0, 2)]),
            (visc, visc_in),
            (ice, ice_in),
            (friction, friction_in),
            (grounded, grounded_in),
            (bounds, levels_in),
        ))
    ]
    for copy in copies:
        copy.start()
    low_half = lax.axis_index("gx") % 2 == 0
    for copy in copies:
        copy.wait()
    fields[2] = visc_in[...] * ice_in[...].astype(F32)
    fields[3] = friction_in[...] * grounded_in[...].astype(F32)
    for n in range(4):
        x_send[8 * n : 8 * n + 8, :] = rim_rows(fields, n, low_half)[0]
        levels[8 * n : 8 * n + 8, :] = jnp.full((8, LANES), levels_in[n])
    x_send[32:, :] = rim_tail(fields, low_half)[0]


def second_pack_kernel(fields, levels, x_send, coefficients, z_send, side_send, x_corner, z_corner):
    rows, cols = fields.shape[1:]
    left = lax.axis_index("gy") == 0
    position, last_position = lax.axis_index("gx"), lax.axis_size("gx") - 1
    low_half = position % 2 == 0
    at_end = (position == 0) | (position == last_position)
    for n in range(4):
        z_send[8 * n : 8 * n + 8, :] = jnp.where(at_end, 0.0, rim_rows(fields, n, low_half)[1])
        side_send[rows * n : rows * n + rows, :] = jnp.where(
            left, fields[n, :, cols - LANES :], fields[n, :, :LANES]
        )
    z_send[32:, :] = jnp.where(at_end, 0.0, rim_tail(fields, low_half)[1])
    sublanes = lax.broadcasted_iota(jnp.int32, (8, LANES), 0)
    own_columns_of = lane_ids() // EDGE == sublanes
    for source, target in ((x_send, x_corner), (z_send, z_corner)):
        packed = jnp.zeros((8, LANES), F32)
        for q in range(RIM // 2):
            last, first = source[8 * q : 8 * q + 8, cols - LANES :], source[8 * q : 8 * q + 8, :LANES]
            columns = jnp.where(
                left,
                pltpu.roll(last, EDGE, 1, stride=EDGE, stride_axis=0),
                pltpu.roll(first, 0, 1, stride=EDGE, stride_axis=0),
            )
            row = jnp.sum(jnp.where(own_columns_of, columns, 0.0), axis=0, keepdims=True)
            packed = jnp.where(sublanes == q, row, packed)
        target[...] = packed
    for sweep in range(2):
        lower, upper = levels[16 * sweep : 16 * sweep + 8, :], levels[16 * sweep + 8 : 16 * sweep + 16, :]
        middle = 0.5 * (upper + lower)
        half = 0.5 * (upper - lower)
        ratio = middle / half
        factor = 1.0 / ratio
        values = [1.0 / middle]
        for step in range(DEG - 1):
            factor_next = 1.0 / (2.0 * ratio - factor)
            values += [factor_next * factor, 2.0 * factor_next / half]
            factor = factor_next
        for n, value in enumerate(values):
            row = 8 * (sweep * (2 * DEG - 1) + n)
            coefficients[row : row + 8, :] = value


class Rows:
    def __init__(self, *pieces):
        self.pieces = pieces

    def place(self, row):
        for first, end, ref, start in self.pieces:
            if first <= row < end:
                return ref, slice(8 * (row - first + start), 8 * (row - first + start) + 8)
        raise IndexError(row)


def at(array, row):
    ref, place = array.place(row)
    return ref[place, :]


def put(array, row, value):
    ref, place = array.place(row)
    ref[place, :] = value


def to_left(value, shift):
    return pltpu.roll(value, LANES - shift, 1)


def to_right(value, shift):
    return pltpu.roll(value, shift, 1)


def spread(ref, base, height, left, side_block, target, first_row):
    blocks = [ref[base : base + height, LANES * j : LANES * j + LANES] for j in range(ref.shape[1] // LANES)]
    zero = jnp.zeros((height, LANES), F32)
    if side_block is None:
        blocks = [zero] + blocks + [zero]
    else:
        blocks = [jnp.where(left, zero, side_block)] + blocks + [jnp.where(left, side_block, zero)]
    lanes = lax.broadcasted_iota(jnp.int32, (height, LANES), 1)
    for s in range(SEGS):
        start = 96 * s - EDGE
        first = start // LANES
        offset = start - LANES * first
        merged = jnp.where(lanes >= offset, blocks[first + 1], blocks[first + 2])
        target[pl.ds(first_row * 8 + s, height, stride=8), :] = to_left(merged, offset)


def inside_columns(left, cols):
    column = 96 * lax.broadcasted_iota(jnp.int32, (8, LANES), 0) + lane_ids() - EDGE
    return jnp.where(left, (column >= 0).astype(F32), (column < cols).astype(F32))


def own_columns():
    lanes = lane_ids()
    return (lanes >= EDGE) & (lanes < LANES - EDGE)


def stiffness(visc, target, first, last, shift):
    paired = None
    for row in range(first, last + 1):
        k = at(visc, row)
        now = k + to_left(k, shift)
        if row > first:
            put(target, row - 1, 0.125 * (paired + now))
        paired = now


def edge_gradients(here, there):
    return here[0] + there[0], here[1] + there[1], there[0] - here[0], there[1] - here[1]


def cell_forces(s, one, two):
    a, b = two[0] - one[0], two[3] + one[3]
    c, d = two[2] + one[2], two[1] - one[1]
    both = a + b
    return s * (both + a), s * (both + b), (0.5 * s) * (c + d)


def forces(x, following, stiff, low, high):
    applied = {}
    def gradients(row):
        return edge_gradients([at(part, row) for part in x], [at(part, row) for part in following])

    here = gradients(low)
    before = cell_forces(at(stiff, low - 1), gradients(low - 1), here)
    for row in range(low, high):
        after = gradients(row + 1)
        now = cell_forces(at(stiff, row), here, after)
        shear, shear_step = before[2] + now[2], before[2] - now[2]
        normal_step, normal = before[0] - now[0], before[1] + now[1]
        applied[row] = (
            (normal_step - shear, normal_step + shear),
            (shear_step - normal, shear_step + normal),
        )
        here, before = after, now
    return applied


def remaining(n, value, f, beta, applied, row):
    return (at(f[n], row) - at(beta, row) * value) - (applied[row][n][0] + to_right(applied[row][n][1], 1))


def begin(x, following, f, coefficients, rows, shift):
    inverse = coefficients[:8, :]
    for row in rows:
        for n in range(2):
            value = at(f[n], row) * inverse
            put(x[n], row, value)
            put(following[n], row, to_left(value, shift))


def advance(levels, followings, f, beta, stiff, coefficients, step, spans, mask_of):
    keep = coefficients[8 + 16 * step : 16 + 16 * step, :]
    gain = coefficients[16 + 16 * step : 24 + 16 * step, :]
    gains = {}
    x, new = levels[step], levels[step + 1]
    applied = {}
    for low, high in spans:
        applied.update(forces(x, followings[step], stiff, low, high))
    for low, high in spans:
        for row in range(low, high):
            mask = mask_of(row)
            part = gains.setdefault(id(mask), gain * mask)
            for n in range(2):
                value = at(x[n], row)
                change = value if step == 0 else value - at(levels[step - 1][n], row)
                value = value + keep * change + part * remaining(n, value, f, beta, applied, row)
                put(new[n], row, value)
                put(followings[step + 1][n], row, to_left(value, 1))


def restrict(source, i, lanes, scale=None):
    row = DEG + 2 * i
    pair = at(source, row) + at(source, row + 1)
    if scale is not None:
        pair = scale * pair
    even, odd = lanes != "odd", lanes != "even"
    if even and odd:
        return jnp.where(lane_ids() % 2 == 0, pair + to_left(pair, 1), pair + to_right(pair, 1))
    return pair + (to_left(pair, 1) if even else to_right(pair, 1))


def pairs_of(refs):
    return [tuple(refs[n : n + 2]) for n in range(0, len(refs), 2)]


def middle_kernel(coefficients, fields, side, *refs):
    rows, cols = fields.shape[1:]
    end = RIM + rows
    left = lax.axis_index("gy") == 0
    outs = refs
    own, cell_ref, squares_out = outs[:4], outs[4], outs[5]
    level_refs, following_refs = pairs_of(outs[6 : 6 + 2 * DEG]), pairs_of(outs[6 + 2 * DEG : 6 + 4 * DEG])
    residual_refs, coarse_refs = outs[6 + 4 * DEG : 8 + 4 * DEG], outs[8 + 4 * DEG :]
    for n in range(4):
        for h in range(0, rows, 8):
            spread(fields.at[n], h, 8, left, side[rows * n + h : rows * n + h + 8, :], own[n], h)

    def whole_rows(ref):
        return Rows((RIM, end, ref, 0))

    f_u, f_v, visc, beta = (whole_rows(ref) for ref in own)
    f = (f_u, f_v)
    cell = whole_rows(cell_ref)
    levels = [tuple(map(whole_rows, pair)) for pair in level_refs]
    followings = [tuple(map(whole_rows, pair)) for pair in following_refs]
    inside = inside_columns(left, cols)
    stiffness(visc, cell, RIM, end - 1, 1)
    begin(levels[0], followings[0], f, coefficients, range(RIM, end), 1)
    for step in range(DEG - 1):
        span = (RIM + step + 1, end - step - 1)
        advance(levels, followings, f, beta, cell, coefficients, step, (span,), lambda row: inside)
    residual = tuple(map(whole_rows, residual_refs))
    low, high = RIM + DEG, end - DEG
    applied = forces(levels[-1], followings[-1], cell, low, high)
    squares = jnp.zeros((8, LANES), F32)
    for row in range(low, high):
        for n in range(2):
            value = inside * remaining(n, at(levels[-1][n], row), f, beta, applied, row)
            put(residual[n], row, value)
            squares = squares + value * value
    squares_out[...] = squares
    rim = (RIM - DEG) // 2
    coarse = [Rows((rim, rim + rows // 2, ref, 0)) for ref in coarse_refs]
    for i in range(rim, rim + rows // 2):
        put(coarse[0], i, restrict(visc, i, "both", 0.25))
        put(coarse[1], i, restrict(beta, i, "both"))
        if low <= DEG + 2 * i < high:
            put(coarse[2], i, restrict(residual[0], i, "both"))
            put(coarse[3], i, restrict(residual[1], i, "both"))


def main_kernel(coefficients, fields, velocity, from_x, from_z, side_x, side_z, middle, outs, scratch):
    multiplier, gradient, sums = outs
    scratch = list(scratch)
    rows, cols = gradient.shape
    total, end = rows + 2 * RIM, RIM + rows
    gx_at, gx_size = lax.axis_index("gx"), lax.axis_size("gx")
    low_half = gx_at % 2 == 0
    left = lax.axis_index("gy") == 0
    own, cell_ref, squares_ref = middle[:4], middle[4], middle[5]
    level_refs, following_refs = pairs_of(middle[6 : 6 + 2 * DEG]), pairs_of(middle[6 + 2 * DEG : 6 + 4 * DEG])
    residual_refs, coarse_refs = middle[6 + 4 * DEG : 8 + 4 * DEG], middle[8 + 4 * DEG :]

    def take(count):
        taken = scratch[:count]
        del scratch[:count]
        return taken

    rims = take(4)
    tails = take(1)[0]
    joint = [Rows((0, rows, ref, 0)) for ref in take(2)]
    for received, partner, corner, is_above in (
        (from_x, side_x, take(1)[0], jnp.logical_not(low_half)),
        (from_z, side_z, take(1)[0], low_half),
    ):
        first_row = jnp.where(is_above, 0, 8)
        rolled = [to_left(partner[...], EDGE * i) if i else partner[...] for i in range(8)]
        for i in range(8):
            corner[pl.ds(i, 8, stride=8), :] = jnp.where(left, rolled[i], rolled[(i + 1) % 8])
        for n, target in enumerate((*rims, tails)):
            spread(received, 8 * n, 8, left, corner[8 * n : 8 * n + 8, :], target, first_row)

    def joined(full, ref, margin):
        return Rows(
            (0, RIM + margin, full, 0),
            (RIM + margin, end - margin, ref, margin),
            (end - margin, total, full, end - margin),
        )

    f_u, f_v, visc, beta = (
        Rows(
            (0, RIM - 8, tails, 2 * n),
            (RIM - 8, RIM, rims[n], 0),
            (RIM, end, own[n], 0),
            (end, end + 8, rims[n], 8),
            (end + 8, total, tails, 8 + 2 * n),
        )
        for n in range(4)
    )
    f = (f_u, f_v)
    cell_full = take(1)[0]
    cell = Rows((0, RIM, cell_full, 0), (RIM, end - 1, cell_ref, 0), (end - 1, total, cell_full, end - 1))
    levels = [tuple(joined(take(1)[0], ref, n) for ref in pair) for n, pair in enumerate(level_refs)]
    followings = [tuple(joined(take(1)[0], ref, n) for ref in pair) for n, pair in enumerate(following_refs)]

    inside = inside_columns(left, cols)
    above = inside * jnp.where(gx_at > 0, 1.0, 0.0)
    below = inside * jnp.where(gx_at < gx_size - 1, 1.0, 0.0)

    def mask_of(row):
        return above if row < RIM else below if row >= end else inside

    stiffness(visc, cell, 0, RIM, 1)
    stiffness(visc, cell, end - 1, total - 1, 1)
    begin(levels[0], followings[0], f, coefficients, [*range(RIM), *range(end, total)], 1)
    for step in range(DEG - 1):
        spans = ((step + 1, RIM + step + 1), (end - step - 1, total - step - 1))
        advance(levels, followings, f, beta, cell, coefficients, step, spans, mask_of)
    x = levels[-1]
    squares = squares_ref[...]
    bases, others = {}, {}
    for low, high in ((DEG, RIM + DEG), (end - DEG, total - DEG)):
        applied = forces(x, followings[-1], cell, low, high)
        for row in range(low, high):
            for n in range(2):
                here, other = applied[row][n]
                bases[n, row] = (at(f[n], row) - at(beta, row) * at(x[n], row)) - here
                others[n, row] = other
                if RIM <= row < end:
                    value = inside * (bases[n, row] - to_right(other, 1))
                    squares = squares + value * value

    def restrict_residual(n, i, lanes):
        row = DEG + 2 * i
        base, other = (part[n, row] + part[n, row + 1] for part in (bases, others))
        if lanes == "even":
            value = (base - other) + (to_left(base, 1) - to_right(other, 1))
        else:
            value = base + (to_right(base - other, 1) - to_right(other, 2))
        return mask_of(row) * value

    even = lane_ids() % 2 == 0
    coarse_rim = (RIM - DEG) // 2
    half = rows // 4
    count = half + 2 * coarse_rim

    def plain():
        return Rows((0, count, take(1)[0], 0))

    def packed(make, ref, margin):
        first, last = coarse_rim + margin, coarse_rim + 2 * half - margin
        target = plain()
        for j in range(count):
            i, k = j, j + half
            one = at(Rows((first, last, ref, margin)), i) if first <= i < last else make(i, "even")
            two = at(Rows((first, last, ref, margin)), k) if first <= k < last else make(k, "odd")
            put(target, j, jnp.where(even, one, two))
        return target

    c_visc, c_beta, *c_f = (
        packed(make, ref, margin)
        for make, ref, margin in zip(
            (
                lambda i, lanes: restrict(visc, i, lanes, 0.25),
                lambda i, lanes: restrict(beta, i, lanes),
                functools.partial(restrict_residual, 0),
                functools.partial(restrict_residual, 1),
            ),
            coarse_refs,
            (0, 0, DEG // 2, DEG // 2),
        )
    )
    masks = [
        jnp.where(even, above if j < coarse_rim else inside, below if j >= count - coarse_rim else inside)
        for j in range(count)
    ]
    stiff, stiff_before = plain(), plain()
    stiffness(c_visc, stiff, 0, count - 1, 2)
    for row in range(count - 1):
        put(stiff_before, row, to_right(at(stiff, row), 2))
    table = 8 * (2 * DEG - 1)

    def gradients(here):
        after = [to_left(value, 2) for value in here]
        before = [to_right(value, 2) for value in here]
        return edge_gradients(here, after), edge_gradients(before, here)

    def cells(row, one, two):
        return [cell_forces(at(s, row), p, q) for s, p, q in zip((stiff, stiff_before), one, two)]

    inverse = coefficients[table : table + 8, :]
    c_x = [[at(part, row) * inverse for part in c_f] for row in range(count)]
    c_old = c_x
    for step in range(DEG - 1):
        keep = coefficients[table + 8 + 16 * step : table + 16 + 16 * step, :]
        gain = coefficients[table + 16 + 16 * step : table + 24 + 16 * step, :]
        low, high = step + 1, count - step - 1
        edges = {row: gradients(c_x[row]) for row in range(low - 1, high + 1)}
        forces_at = {row: cells(row, edges[row], edges[row + 1]) for row in range(low - 1, high)}
        c_new = list(c_x)
        for row in range(low, high):
            (xx0, yy0, xy0), (xx1, yy1, xy1) = (
                (p[0] - q[0], p[1] + q[1], (p[2] + q[2], p[2] - q[2]))
                for p, q in zip(forces_at[row - 1], forces_at[row])
            )
            applied = ((xx0 - xy0[0]) + (xx1 + xy1[0]), (xy0[1] - yy0) + (xy1[1] + yy1))
            part = gain * masks[row]
            c_new[row] = []
            for n in range(2):
                value = c_x[row][n]
                change = value if step == 0 else value - c_old[row][n]
                left_over = (at(c_f[n], row) - at(c_beta, row) * value) - applied[n]
                c_new[row].append(value + keep * change + part * left_over)
        c_x, c_old = c_new, c_x

    lanes = lane_ids()
    for i in range(half):
        for n in range(2):
            value = c_x[coarse_rim + i][n]
            corrections = jnp.where(even, value, to_right(value, 1)), jnp.where(even, to_left(value, 1), value)
            for first, correction in zip((2 * i, 2 * (i + half)), corrections):
                for row in (first, first + 1):
                    put(joint[n], row, at(x[n], RIM + row) + correction)

    gradient_squares = jnp.zeros((8, LANES), F32)
    for h in range(0, rows, 8):
        for j in range(cols // LANES):
            s = (LANES * j) // 96
            shift = LANES * j - 96 * s + EDGE
            border = 96 * (s + 1) - LANES * j
            columns = slice(LANES * j, LANES * j + LANES)
            product = None
            for n in range(2):
                source = joint[n].pieces[0][2]
                one = source[pl.ds(8 * h + s, 8, stride=8), :]
                two = source[pl.ds(8 * h + s + 1, 8, stride=8), :]
                value = jnp.where(lanes < border, to_left(one, shift), to_right(two, (96 - shift) % LANES))
                multiplier[n, h : h + 8, columns] = value
                term = velocity[n, h : h + 8, columns] * value
                product = term if product is None else product + term
            value = -fields[3, h : h + 8, columns] * product
            gradient[h : h + 8, columns] = value
            gradient_squares = gradient_squares + value * value
    pair = [jnp.sum(value, axis=0, keepdims=True) for value in (jnp.where(own_columns(), squares, 0.0), gradient_squares)]
    sums[...] = jnp.broadcast_to(jnp.concatenate(pair, axis=1), sums.shape)


def scale_kernel(nodes, gathered, gradient, held_multiplier, scaled, norm, multiplier, scaled_out, norm_out, sems):
    copies = [
        pltpu.make_async_copy(source, target, sems.at[n])
        for n, (source, target) in enumerate(((held_multiplier, multiplier), (norm_out, norm), (scaled_out, scaled)))
    ]
    copies[0].start()
    residual_total = jnp.sum(gathered[:, :LANES], keepdims=True)
    gradient_total = jnp.sum(gathered[:, LANES:], keepdims=True)
    norm_out[...] = jnp.sqrt(residual_total / (2 * nodes))
    copies[1].start()
    scaled_out[...] = gradient[...] / jnp.sqrt(gradient_total / nodes + 1e-06)
    copies[2].start()
    for copy in copies:
        copy.wait()


def body(misfit, velocity, viscosity, friction, ice, grounded, bounds):
    rows, cols = viscosity.shape
    gx_size, gy_size = lax.axis_size("gx"), lax.axis_size("gy")
    assert gy_size == 2 and gx_size % 2 == 0 and cols == 96 * SEGS and rows == 16
    peers = gx_size * gy_size
    nodes = rows * cols * peers
    total = rows + 2 * RIM
    shaped = jax.ShapeDtypeStruct
    whole = pl.BlockSpec(memory_space=pltpu.VMEM)
    params = pltpu.CompilerParams(vmem_limit_bytes=32 * 1024 * 1024)

    held = pl.BlockSpec(memory_space=pltpu.HBM)
    inputs = (bounds, misfit, viscosity, friction, ice, grounded)
    fields, levels, x_send = pl.pallas_call(
        first_pack_kernel,
        out_shape=(shaped((4, rows, cols), F32), shaped((32, LANES), F32), shaped((4 * RIM, cols), F32)),
        in_specs=[held] * 6,
        out_specs=[whole] * 3,
        scratch_shapes=[
            pltpu.SMEM((4,), F32),
            pltpu.VMEM((rows, cols), F32),
            pltpu.VMEM((rows, cols), F32),
            pltpu.VMEM((rows, cols), jnp.int32),
            pltpu.VMEM((rows, cols), jnp.int32),
            pltpu.SemaphoreType.DMA((6,)),
        ],
        compiler_params=params,
        name="first_pack",
    )(*(pltpu.with_memory_space_constraint(x, pltpu.HBM) for x in inputs))
    coefficients, z_send, side_send, x_corner, z_corner = pl.pallas_call(
        second_pack_kernel,
        out_shape=(
            shaped((16 * (2 * DEG - 1), LANES), F32),
            shaped((4 * RIM, cols), F32),
            shaped((4 * rows, LANES), F32),
            shaped((8, LANES), F32),
            shaped((8, LANES), F32),
        ),
        in_specs=[whole] * 3,
        out_specs=[whole] * 5,
        compiler_params=params,
        name="second_pack",
    )(fields, levels, x_send)

    x_pairs = [(i, i ^ 1) for i in range(gx_size)]
    z_pairs = [(2 * i + c, 2 * j + c) for i in range(1, gx_size - 1) for j in (i + 1 if i % 2 else i - 1,) for c in (0, 1)]
    z_pairs += [(2 * i + c, 2 * i + 1 - c) for i in (0, gx_size - 1) for c in (0, 1)]
    swap = [(0, 1), (1, 0)]
    from_x = lax.ppermute(x_send, "gx", x_pairs)
    from_z = lax.ppermute(z_send, AXES, z_pairs)
    side = lax.ppermute(side_send, "gy", swap)
    side_x = lax.ppermute(x_corner, AXES, [(2 * i + c, 2 * j + 1 - c) for i, j in x_pairs for c in (0, 1)])
    side_z = lax.ppermute(z_corner, AXES, [(i, j ^ 1 if 1 < i < 2 * gx_size - 2 else j) for i, j in z_pairs])

    fine = pltpu.VMEM((8 * total, LANES), F32)
    coarse = pltpu.VMEM((4 * total, LANES), F32)
    owned = pltpu.VMEM((8 * rows, LANES), F32)
    halved = pltpu.VMEM((4 * rows, LANES), F32)
    middle = pl.pallas_call(
        middle_kernel,
        out_shape=[owned] * 5 + [pltpu.VMEM((8, LANES), F32)] + [owned] * (4 * DEG + 2) + [halved] * 4,
        in_specs=[whole] * 3,
        out_specs=[whole] * (12 + 4 * DEG),
        compiler_params=params,
        name="middle",
    )(coefficients, fields, side)

    def leg_kernel(coefficients, fields, velocity, from_x, from_z, side_x, side_z, *refs):
        done, refs = refs[: len(middle)], refs[len(middle) :]
        main_kernel(coefficients, fields, velocity, from_x, from_z, side_x, side_z, done, refs[:3], refs[3:])

    rim = pltpu.VMEM((8 * 16, LANES), F32)
    corner = pltpu.VMEM((8 * 8, LANES), F32)
    held_multiplier, gradient, sums = pl.pallas_call(
        leg_kernel,
        out_shape=(
            pltpu.VMEM((2, rows, cols), F32),
            pltpu.VMEM((rows, cols), F32),
            shaped((peers, 2 * LANES), F32),
        ),
        in_specs=[whole] * (7 + len(middle)),
        out_specs=[whole] * 3,
        scratch_shapes=[rim] * 5 + [owned] * 2 + [corner] * 2 + [fine] * (1 + 4 * DEG) + [coarse] * 14,
        compiler_params=params,
        name="leg",
    )(coefficients, fields, velocity, from_x, from_z, side_x, side_z, *middle)

    gathered = lax.all_to_all(sums, AXES, 0, 0, tiled=True)
    scaled, norm, multiplier = pl.pallas_call(
        functools.partial(scale_kernel, nodes),
        out_shape=(
            pltpu.HBM((rows, cols), F32),
            pltpu.HBM((1, 1), F32),
            pltpu.HBM((2, rows, cols), F32),
        ),
        in_specs=[whole] * 3,
        out_specs=[held] * 3,
        scratch_shapes=[
            pltpu.VMEM((rows, cols), F32),
            pltpu.VMEM((1, 1), F32),
            pltpu.SemaphoreType.DMA((3,)),
        ],
        compiler_params=params,
        name="scale",
    )(gathered, gradient, held_multiplier)
    return multiplier, scaled, norm.reshape(1)


def solution(mesh):
    tile = P(("grp", "gx"), "gy")
    pair = P(None, ("grp", "gx"), "gy")
    return jax.shard_map(
        body,
        mesh=mesh,
        in_specs=(pair, pair, tile, tile, tile, tile, P("grp")),
        out_specs=(pair, tile, P("grp")),
        check_vma=False,
    )
```

```python
import functools

import jax
import jax.numpy as jnp
from jax import lax
from jax.experimental import pallas as pl
from jax.experimental.pallas import tpu as pltpu
from jax.sharding import PartitionSpec as P

DEG = 4
LANES = 128
SEGS = 8
RIM = 10
EDGE = 16
F32 = jnp.float32
AXES = ("gx", "gy")


def lane_ids():
    return lax.broadcasted_iota(jnp.int32, (8, LANES), 1)


def rim_rows(fields, n, low_half):
    first, last = fields[n, :8, :], fields[n, 8:16, :]
    return jnp.where(low_half, last, first), jnp.where(low_half, first, last)


def rim_tail(fields, low_half):
    sublanes = lax.broadcasted_iota(jnp.int32, (8, fields.shape[2]), 0)
    down = up = jnp.zeros(sublanes.shape, F32)
    for n in range(4):
        here = sublanes // 2 == n
        down = jnp.where(here, pltpu.roll(fields[n, :8, :], (2 * n + 2) % 8, 0), down)
        up = jnp.where(here, pltpu.roll(fields[n, 8:16, :], 2 * n, 0), up)
    return jnp.where(low_half, down, up), jnp.where(low_half, up, down)


def first_pack_kernel(
    misfit, visc, friction, ice, grounded, fields, x_send, visc_in, friction_in, ice_in, grounded_in, sems
):
    copies = [
        pltpu.make_async_copy(source, target, sems.at[n])
        for n, (source, target) in enumerate((
            (misfit, fields.at[pl.ds(0, 2)]),
            (visc, visc_in),
            (ice, ice_in),
            (friction, friction_in),
            (grounded, grounded_in),
        ))
    ]
    for copy in copies:
        copy.start()
    low_half = lax.axis_index("gx") % 2 == 0
    for copy in copies:
        copy.wait()
    fields[2] = visc_in[...] * ice_in[...].astype(F32)
    fields[3] = friction_in[...] * grounded_in[...].astype(F32)
    for n in range(4):
        x_send[8 * n : 8 * n + 8, :] = rim_rows(fields, n, low_half)[0]
    x_send[32:, :] = rim_tail(fields, low_half)[0]


def second_pack_kernel(fields, x_send, z_send, side_send, x_corner, z_corner):
    rows, cols = fields.shape[1:]
    left = lax.axis_index("gy") == 0
    position, last_position = lax.axis_index("gx"), lax.axis_size("gx") - 1
    low_half = position % 2 == 0
    at_end = (position == 0) | (position == last_position)
    for n in range(4):
        z_send[8 * n : 8 * n + 8, :] = jnp.where(at_end, 0.0, rim_rows(fields, n, low_half)[1])
        side_send[rows * n : rows * n + rows, :] = jnp.where(
            left, fields[n, :, cols - LANES :], fields[n, :, :LANES]
        )
    z_send[32:, :] = jnp.where(at_end, 0.0, rim_tail(fields, low_half)[1])
    sublanes = lax.broadcasted_iota(jnp.int32, (8, LANES), 0)
    own_columns_of = lane_ids() // EDGE == sublanes
    for source, target in ((x_send, x_corner), (z_send, z_corner)):
        packed = jnp.zeros((8, LANES), F32)
        for q in range(RIM // 2):
            last, first = source[8 * q : 8 * q + 8, cols - LANES :], source[8 * q : 8 * q + 8, :LANES]
            columns = jnp.where(
                left,
                pltpu.roll(last, EDGE, 1, stride=EDGE, stride_axis=0),
                pltpu.roll(first, 0, 1, stride=EDGE, stride_axis=0),
            )
            row = jnp.sum(jnp.where(own_columns_of, columns, 0.0), axis=0, keepdims=True)
            packed = jnp.where(sublanes == q, row, packed)
        target[...] = packed


def coefficient_kernel(bounds, coefficients):
    for sweep in range(2):
        lower, upper = jnp.full((8, LANES), bounds[2 * sweep]), jnp.full((8, LANES), bounds[2 * sweep + 1])
        middle = 0.5 * (upper + lower)
        half = 0.5 * (upper - lower)
        ratio = middle / half
        factor = 1.0 / ratio
        values = [1.0 / middle]
        for step in range(DEG - 1):
            factor_next = 1.0 / (2.0 * ratio - factor)
            values += [factor_next * factor, 2.0 * factor_next / half]
            factor = factor_next
        for n, value in enumerate(values):
            row = 8 * (sweep * (2 * DEG - 1) + n)
            coefficients[row : row + 8, :] = value


class Rows:
    def __init__(self, *pieces):
        self.pieces = pieces

    def place(self, row):
        for first, end, ref, start in self.pieces:
            if first <= row < end:
                return ref, slice(8 * (row - first + start), 8 * (row - first + start) + 8)
        raise IndexError(row)


def at(array, row):
    ref, place = array.place(row)
    return ref[place, :]


def put(array, row, value):
    ref, place = array.place(row)
    ref[place, :] = value


def to_left(value, shift):
    return pltpu.roll(value, LANES - shift, 1)


def to_right(value, shift):
    return pltpu.roll(value, shift, 1)


def spread(ref, base, height, left, side_block, target, first_row):
    blocks = [ref[base : base + height, LANES * j : LANES * j + LANES] for j in range(ref.shape[1] // LANES)]
    zero = jnp.zeros((height, LANES), F32)
    if side_block is None:
        blocks = [zero] + blocks + [zero]
    else:
        blocks = [jnp.where(left, zero, side_block)] + blocks + [jnp.where(left, side_block, zero)]
    lanes = lax.broadcasted_iota(jnp.int32, (height, LANES), 1)
    for s in range(SEGS):
        start = 96 * s - EDGE
        first = start // LANES
        offset = start - LANES * first
        merged = jnp.where(lanes >= offset, blocks[first + 1], blocks[first + 2])
        target[pl.ds(first_row * 8 + s, height, stride=8), :] = to_left(merged, offset)


def inside_columns(left, cols):
    column = 96 * lax.broadcasted_iota(jnp.int32, (8, LANES), 0) + lane_ids() - EDGE
    return jnp.where(left, (column >= 0).astype(F32), (column < cols).astype(F32))


def own_columns():
    lanes = lane_ids()
    return (lanes >= EDGE) & (lanes < LANES - EDGE)


def stiffness(visc, target, first, last, shift):
    paired = None
    for row in range(first, last + 1):
        k = at(visc, row)
        now = k + to_left(k, shift)
        if row > first:
            put(target, row - 1, 0.125 * (paired + now))
        paired = now


def edge_gradients(here, there):
    return here[0] + there[0], here[1] + there[1], there[0] - here[0], there[1] - here[1]


def cell_forces(s, one, two):
    a, b = two[0] - one[0], two[3] + one[3]
    c, d = two[2] + one[2], two[1] - one[1]
    both = a + b
    return s * (both + a), s * (both + b), (0.5 * s) * (c + d)


def forces(x, following, stiff, low, high):
    applied = {}
    def gradients(row):
        return edge_gradients([at(part, row) for part in x], [at(part, row) for part in following])

    here = gradients(low)
    before = cell_forces(at(stiff, low - 1), gradients(low - 1), here)
    for row in range(low, high):
        after = gradients(row + 1)
        now = cell_forces(at(stiff, row), here, after)
        shear, shear_step = before[2] + now[2], before[2] - now[2]
        normal_step, normal = before[0] - now[0], before[1] + now[1]
        applied[row] = (
            (normal_step - shear, normal_step + shear),
            (shear_step - normal, shear_step + normal),
        )
        here, before = after, now
    return applied


def remaining(n, value, f, beta, applied, row):
    return (at(f[n], row) - at(beta, row) * value) - (applied[row][n][0] + to_right(applied[row][n][1], 1))


def begin(x, following, f, coefficients, rows, shift):
    inverse = coefficients[:8, :]
    for row in rows:
        for n in range(2):
            value = at(f[n], row) * inverse
            put(x[n], row, value)
            put(following[n], row, to_left(value, shift))


def advance(levels, followings, f, beta, stiff, coefficients, step, spans, mask_of):
    keep = coefficients[8 + 16 * step : 16 + 16 * step, :]
    gain = coefficients[16 + 16 * step : 24 + 16 * step, :]
    gains = {}
    x, new = levels[step], levels[step + 1]
    applied = {}
    for low, high in spans:
        applied.update(forces(x, followings[step], stiff, low, high))
    for low, high in spans:
        for row in range(low, high):
            mask = mask_of(row)
            part = gains.setdefault(id(mask), gain * mask)
            for n in range(2):
                value = at(x[n], row)
                change = value if step == 0 else value - at(levels[step - 1][n], row)
                value = value + keep * change + part * remaining(n, value, f, beta, applied, row)
                put(new[n], row, value)
                put(followings[step + 1][n], row, to_left(value, 1))


def restrict(source, i, lanes, scale=None):
    row = DEG + 2 * i
    pair = at(source, row) + at(source, row + 1)
    if scale is not None:
        pair = scale * pair
    even, odd = lanes != "odd", lanes != "even"
    if even and odd:
        return jnp.where(lane_ids() % 2 == 0, pair + to_left(pair, 1), pair + to_right(pair, 1))
    return pair + (to_left(pair, 1) if even else to_right(pair, 1))


def pairs_of(refs):
    return [tuple(refs[n : n + 2]) for n in range(0, len(refs), 2)]


def middle_kernel(coefficients, fields, side, *refs):
    rows, cols = fields.shape[1:]
    end = RIM + rows
    left = lax.axis_index("gy") == 0
    outs = refs
    own, cell_ref, squares_out = outs[:4], outs[4], outs[5]
    level_refs, following_refs = pairs_of(outs[6 : 6 + 2 * DEG]), pairs_of(outs[6 + 2 * DEG : 6 + 4 * DEG])
    residual_refs, coarse_refs = outs[6 + 4 * DEG : 8 + 4 * DEG], outs[8 + 4 * DEG :]
    for n in range(4):
        for h in range(0, rows, 8):
            spread(fields.at[n], h, 8, left, side[rows * n + h : rows * n + h + 8, :], own[n], h)

    def whole_rows(ref):
        return Rows((RIM, end, ref, 0))

    f_u, f_v, visc, beta = (whole_rows(ref) for ref in own)
    f = (f_u, f_v)
    cell = whole_rows(cell_ref)
    levels = [tuple(map(whole_rows, pair)) for pair in level_refs]
    followings = [tuple(map(whole_rows, pair)) for pair in following_refs]
    inside = inside_columns(left, cols)
    stiffness(visc, cell, RIM, end - 1, 1)
    begin(levels[0], followings[0], f, coefficients, range(RIM, end), 1)
    for step in range(DEG - 1):
        span = (RIM + step + 1, end - step - 1)
        advance(levels, followings, f, beta, cell, coefficients, step, (span,), lambda row: inside)
    residual = tuple(map(whole_rows, residual_refs))
    low, high = RIM + DEG, end - DEG
    applied = forces(levels[-1], followings[-1], cell, low, high)
    squares = jnp.zeros((8, LANES), F32)
    for row in range(low, high):
        for n in range(2):
            value = inside * remaining(n, at(levels[-1][n], row), f, beta, applied, row)
            put(residual[n], row, value)
            squares = squares + value * value
    squares_out[...] = squares
    rim = (RIM - DEG) // 2
    coarse = [Rows((rim, rim + rows // 2, ref, 0)) for ref in coarse_refs]
    for i in range(rim, rim + rows // 2):
        put(coarse[0], i, restrict(visc, i, "both", 0.25))
        put(coarse[1], i, restrict(beta, i, "both"))
        if low <= DEG + 2 * i < high:
            put(coarse[2], i, restrict(residual[0], i, "both"))
            put(coarse[3], i, restrict(residual[1], i, "both"))


def main_kernel(coefficients, fields, velocity, from_x, from_z, side_x, side_z, middle, outs, scratch):
    multiplier, gradient, sums = outs
    scratch = list(scratch)
    rows, cols = gradient.shape
    total, end = rows + 2 * RIM, RIM + rows
    gx_at, gx_size = lax.axis_index("gx"), lax.axis_size("gx")
    low_half = gx_at % 2 == 0
    left = lax.axis_index("gy") == 0
    own, cell_ref, squares_ref = middle[:4], middle[4], middle[5]
    level_refs, following_refs = pairs_of(middle[6 : 6 + 2 * DEG]), pairs_of(middle[6 + 2 * DEG : 6 + 4 * DEG])
    residual_refs, coarse_refs = middle[6 + 4 * DEG : 8 + 4 * DEG], middle[8 + 4 * DEG :]

    def take(count):
        taken = scratch[:count]
        del scratch[:count]
        return taken

    rims = take(4)
    tails = take(1)[0]
    joint = [Rows((0, rows, ref, 0)) for ref in take(2)]
    for received, partner, corner, is_above in (
        (from_x, side_x, take(1)[0], jnp.logical_not(low_half)),
        (from_z, side_z, take(1)[0], low_half),
    ):
        first_row = jnp.where(is_above, 0, 8)
        rolled = [to_left(partner[...], EDGE * i) if i else partner[...] for i in range(8)]
        for i in range(8):
            corner[pl.ds(i, 8, stride=8), :] = jnp.where(left, rolled[i], rolled[(i + 1) % 8])
        for n, target in enumerate((*rims, tails)):
            spread(received, 8 * n, 8, left, corner[8 * n : 8 * n + 8, :], target, first_row)

    def joined(full, ref, margin):
        return Rows(
            (0, RIM + margin, full, 0),
            (RIM + margin, end - margin, ref, margin),
            (end - margin, total, full, end - margin),
        )

    f_u, f_v, visc, beta = (
        Rows(
            (0, RIM - 8, tails, 2 * n),
            (RIM - 8, RIM, rims[n], 0),
            (RIM, end, own[n], 0),
            (end, end + 8, rims[n], 8),
            (end + 8, total, tails, 8 + 2 * n),
        )
        for n in range(4)
    )
    f = (f_u, f_v)
    cell_full = take(1)[0]
    cell = Rows((0, RIM, cell_full, 0), (RIM, end - 1, cell_ref, 0), (end - 1, total, cell_full, end - 1))
    levels = [tuple(joined(take(1)[0], ref, n) for ref in pair) for n, pair in enumerate(level_refs)]
    followings = [tuple(joined(take(1)[0], ref, n) for ref in pair) for n, pair in enumerate(following_refs)]

    inside = inside_columns(left, cols)
    above = inside * jnp.where(gx_at > 0, 1.0, 0.0)
    below = inside * jnp.where(gx_at < gx_size - 1, 1.0, 0.0)

    def mask_of(row):
        return above if row < RIM else below if row >= end else inside

    stiffness(visc, cell, 0, RIM, 1)
    stiffness(visc, cell, end - 1, total - 1, 1)
    begin(levels[0], followings[0], f, coefficients, [*range(RIM), *range(end, total)], 1)
    for step in range(DEG - 1):
        spans = ((step + 1, RIM + step + 1), (end - step - 1, total - step - 1))
        advance(levels, followings, f, beta, cell, coefficients, step, spans, mask_of)
    x = levels[-1]
    squares = squares_ref[...]
    bases, others = {}, {}
    for low, high in ((DEG, RIM + DEG), (end - DEG, total - DEG)):
        applied = forces(x, followings[-1], cell, low, high)
        for row in range(low, high):
            for n in range(2):
                here, other = applied[row][n]
                bases[n, row] = (at(f[n], row) - at(beta, row) * at(x[n], row)) - here
                others[n, row] = other
                if RIM <= row < end:
                    value = inside * (bases[n, row] - to_right(other, 1))
                    squares = squares + value * value

    def restrict_residual(n, i, lanes):
        row = DEG + 2 * i
        base, other = (part[n, row] + part[n, row + 1] for part in (bases, others))
        if lanes == "even":
            value = (base - other) + (to_left(base, 1) - to_right(other, 1))
        else:
            value = base + (to_right(base - other, 1) - to_right(other, 2))
        return mask_of(row) * value

    even = lane_ids() % 2 == 0
    coarse_rim = (RIM - DEG) // 2
    half = rows // 4
    count = half + 2 * coarse_rim

    def plain():
        return Rows((0, count, take(1)[0], 0))

    def packed(make, ref, margin):
        first, last = coarse_rim + margin, coarse_rim + 2 * half - margin
        target = plain()
        for j in range(count):
            i, k = j, j + half
            one = at(Rows((first, last, ref, margin)), i) if first <= i < last else make(i, "even")
            two = at(Rows((first, last, ref, margin)), k) if first <= k < last else make(k, "odd")
            put(target, j, jnp.where(even, one, two))
        return target

    c_visc, c_beta, *c_f = (
        packed(make, ref, margin)
        for make, ref, margin in zip(
            (
                lambda i, lanes: restrict(visc, i, lanes, 0.25),
                lambda i, lanes: restrict(beta, i, lanes),
                functools.partial(restrict_residual, 0),
                functools.partial(restrict_residual, 1),
            ),
            coarse_refs,
            (0, 0, DEG // 2, DEG // 2),
        )
    )
    masks = [
        jnp.where(even, above if j < coarse_rim else inside, below if j >= count - coarse_rim else inside)
        for j in range(count)
    ]
    stiff, stiff_before = plain(), plain()
    stiffness(c_visc, stiff, 0, count - 1, 2)
    for row in range(count - 1):
        put(stiff_before, row, to_right(at(stiff, row), 2))
    table = 8 * (2 * DEG - 1)

    def gradients(here):
        after = [to_left(value, 2) for value in here]
        before = [to_right(value, 2) for value in here]
        return edge_gradients(here, after), edge_gradients(before, here)

    def cells(row, one, two):
        return [cell_forces(at(s, row), p, q) for s, p, q in zip((stiff, stiff_before), one, two)]

    inverse = coefficients[table : table + 8, :]
    c_x = [[at(part, row) * inverse for part in c_f] for row in range(count)]
    c_old = c_x
    for step in range(DEG - 1):
        keep = coefficients[table + 8 + 16 * step : table + 16 + 16 * step, :]
        gain = coefficients[table + 16 + 16 * step : table + 24 + 16 * step, :]
        low, high = step + 1, count - step - 1
        edges = {row: gradients(c_x[row]) for row in range(low - 1, high + 1)}
        forces_at = {row: cells(row, edges[row], edges[row + 1]) for row in range(low - 1, high)}
        c_new = list(c_x)
        for row in range(low, high):
            (xx0, yy0, xy0), (xx1, yy1, xy1) = (
                (p[0] - q[0], p[1] + q[1], (p[2] + q[2], p[2] - q[2]))
                for p, q in zip(forces_at[row - 1], forces_at[row])
            )
            applied = ((xx0 - xy0[0]) + (xx1 + xy1[0]), (xy0[1] - yy0) + (xy1[1] + yy1))
            part = gain * masks[row]
            c_new[row] = []
            for n in range(2):
                value = c_x[row][n]
                change = value if step == 0 else value - c_old[row][n]
                left_over = (at(c_f[n], row) - at(c_beta, row) * value) - applied[n]
                c_new[row].append(value + keep * change + part * left_over)
        c_x, c_old = c_new, c_x

    lanes = lane_ids()
    for i in range(half):
        for n in range(2):
            value = c_x[coarse_rim + i][n]
            corrections = jnp.where(even, value, to_right(value, 1)), jnp.where(even, to_left(value, 1), value)
            for first, correction in zip((2 * i, 2 * (i + half)), corrections):
                for row in (first, first + 1):
                    put(joint[n], row, at(x[n], RIM + row) + correction)

    gradient_squares = jnp.zeros((8, LANES), F32)
    for h in range(0, rows, 8):
        for j in range(cols // LANES):
            s = (LANES * j) // 96
            shift = LANES * j - 96 * s + EDGE
            border = 96 * (s + 1) - LANES * j
            columns = slice(LANES * j, LANES * j + LANES)
            product = None
            for n in range(2):
                source = joint[n].pieces[0][2]
                one = source[pl.ds(8 * h + s, 8, stride=8), :]
                two = source[pl.ds(8 * h + s + 1, 8, stride=8), :]
                value = jnp.where(lanes < border, to_left(one, shift), to_right(two, (96 - shift) % LANES))
                multiplier[n, h : h + 8, columns] = value
                term = velocity[n, h : h + 8, columns] * value
                product = term if product is None else product + term
            value = -fields[3, h : h + 8, columns] * product
            gradient[h : h + 8, columns] = value
            gradient_squares = gradient_squares + value * value
    pair = [jnp.sum(value, axis=0, keepdims=True) for value in (jnp.where(own_columns(), squares, 0.0), gradient_squares)]
    sums[...] = jnp.broadcast_to(jnp.concatenate(pair, axis=1), sums.shape)


def scale_kernel(nodes, gathered, gradient, held_multiplier, scaled, norm, multiplier, scaled_out, norm_out, sems):
    copies = [
        pltpu.make_async_copy(source, target, sems.at[n])
        for n, (source, target) in enumerate(((held_multiplier, multiplier), (norm_out, norm), (scaled_out, scaled)))
    ]
    copies[0].start()
    residual_total = jnp.sum(gathered[:, :LANES], keepdims=True)
    gradient_total = jnp.sum(gathered[:, LANES:], keepdims=True)
    norm_out[...] = jnp.sqrt(residual_total / (2 * nodes))
    copies[1].start()
    scaled_out[...] = gradient[...] / jnp.sqrt(gradient_total / nodes + 1e-06)
    copies[2].start()
    for copy in copies:
        copy.wait()


def body(misfit, velocity, viscosity, friction, ice, grounded, bounds):
    rows, cols = viscosity.shape
    gx_size, gy_size = lax.axis_size("gx"), lax.axis_size("gy")
    assert gy_size == 2 and gx_size % 2 == 0 and cols == 96 * SEGS and rows == 16
    peers = gx_size * gy_size
    nodes = rows * cols * peers
    total = rows + 2 * RIM
    shaped = jax.ShapeDtypeStruct
    whole = pl.BlockSpec(memory_space=pltpu.VMEM)
    params = pltpu.CompilerParams(vmem_limit_bytes=32 * 1024 * 1024)

    held = pl.BlockSpec(memory_space=pltpu.HBM)
    inputs = (misfit, viscosity, friction, ice, grounded)
    fields, x_send = pl.pallas_call(
        first_pack_kernel,
        out_shape=(shaped((4, rows, cols), F32), shaped((4 * RIM, cols), F32)),
        in_specs=[held] * 5,
        out_specs=[whole] * 2,
        scratch_shapes=[
            pltpu.VMEM((rows, cols), F32),
            pltpu.VMEM((rows, cols), F32),
            pltpu.VMEM((rows, cols), jnp.int32),
            pltpu.VMEM((rows, cols), jnp.int32),
            pltpu.SemaphoreType.DMA((5,)),
        ],
        compiler_params=params,
        name="first_pack",
    )(*(pltpu.with_memory_space_constraint(x, pltpu.HBM) for x in inputs))
    z_send, side_send, x_corner, z_corner = pl.pallas_call(
        second_pack_kernel,
        out_shape=(
            shaped((4 * RIM, cols), F32),
            shaped((4 * rows, LANES), F32),
            shaped((8, LANES), F32),
            shaped((8, LANES), F32),
        ),
        in_specs=[whole] * 2,
        out_specs=[whole] * 4,
        compiler_params=params,
        name="second_pack",
    )(fields, x_send)
    coefficients = pl.pallas_call(
        coefficient_kernel,
        out_shape=shaped((16 * (2 * DEG - 1), LANES), F32),
        in_specs=[pl.BlockSpec(memory_space=pltpu.SMEM)],
        out_specs=whole,
        compiler_params=params,
        name="coefficients",
    )(bounds)

    x_pairs = [(i, i ^ 1) for i in range(gx_size)]
    z_pairs = [(2 * i + c, 2 * j + c) for i in range(1, gx_size - 1) for j in (i + 1 if i % 2 else i - 1,) for c in (0, 1)]
    z_pairs += [(2 * i + c, 2 * i + 1 - c) for i in (0, gx_size - 1) for c in (0, 1)]
    swap = [(0, 1), (1, 0)]
    from_x = lax.ppermute(x_send, "gx", x_pairs)
    from_z = lax.ppermute(z_send, AXES, z_pairs)
    side = lax.ppermute(side_send, "gy", swap)
    side_x = lax.ppermute(x_corner, AXES, [(2 * i + c, 2 * j + 1 - c) for i, j in x_pairs for c in (0, 1)])
    side_z = lax.ppermute(z_corner, AXES, [(i, j ^ 1 if 1 < i < 2 * gx_size - 2 else j) for i, j in z_pairs])

    fine = pltpu.VMEM((8 * total, LANES), F32)
    coarse = pltpu.VMEM((4 * total, LANES), F32)
    owned = pltpu.VMEM((8 * rows, LANES), F32)
    halved = pltpu.VMEM((4 * rows, LANES), F32)
    middle = pl.pallas_call(
        middle_kernel,
        out_shape=[owned] * 5 + [pltpu.VMEM((8, LANES), F32)] + [owned] * (4 * DEG + 2) + [halved] * 4,
        in_specs=[whole] * 3,
        out_specs=[whole] * (12 + 4 * DEG),
        compiler_params=params,
        name="middle",
    )(coefficients, fields, side)

    def leg_kernel(coefficients, fields, velocity, from_x, from_z, side_x, side_z, *refs):
        done, refs = refs[: len(middle)], refs[len(middle) :]
        main_kernel(coefficients, fields, velocity, from_x, from_z, side_x, side_z, done, refs[:3], refs[3:])

    rim = pltpu.VMEM((8 * 16, LANES), F32)
    corner = pltpu.VMEM((8 * 8, LANES), F32)
    held_multiplier, gradient, sums = pl.pallas_call(
        leg_kernel,
        out_shape=(
            pltpu.VMEM((2, rows, cols), F32),
            pltpu.VMEM((rows, cols), F32),
            shaped((peers, 2 * LANES), F32),
        ),
        in_specs=[whole] * (7 + len(middle)),
        out_specs=[whole] * 3,
        scratch_shapes=[rim] * 5 + [owned] * 2 + [corner] * 2 + [fine] * (1 + 4 * DEG) + [coarse] * 14,
        compiler_params=params,
        name="leg",
    )(coefficients, fields, velocity, from_x, from_z, side_x, side_z, *middle)

    gathered = lax.all_to_all(sums, AXES, 0, 0, tiled=True)
    scaled, norm, multiplier = pl.pallas_call(
        functools.partial(scale_kernel, nodes),
        out_shape=(
            pltpu.HBM((rows, cols), F32),
            pltpu.HBM((1, 1), F32),
            pltpu.HBM((2, rows, cols), F32),
        ),
        in_specs=[whole] * 3,
        out_specs=[held] * 3,
        scratch_shapes=[
            pltpu.VMEM((rows, cols), F32),
            pltpu.VMEM((1, 1), F32),
            pltpu.SemaphoreType.DMA((3,)),
        ],
        compiler_params=params,
        name="scale",
    )(gathered, gradient, held_multiplier)
    return multiplier, scaled, norm.reshape(1)


def solution(mesh):
    tile = P(("grp", "gx"), "gy")
    pair = P(None, ("grp", "gx"), "gy")
    return jax.shard_map(
        body,
        mesh=mesh,
        in_specs=(pair, pair, tile, tile, tile, tile, P("grp")),
        out_specs=(pair, tile, P("grp")),
        check_vma=False,
    )
```

```python
import functools

import jax
import jax.numpy as jnp
from jax import lax
from jax.experimental import pallas as pl
from jax.experimental.pallas import tpu as pltpu
from jax.sharding import PartitionSpec as P

DEG = 4
LANES = 128
SEGS = 8
RIM = 10
EDGE = 16
F32 = jnp.float32
AXES = ("gx", "gy")


def lane_ids():
    return lax.broadcasted_iota(jnp.int32, (8, LANES), 1)


def rim_rows(fields, n, low_half):
    first, last = fields[n, :8, :], fields[n, 8:16, :]
    return jnp.where(low_half, last, first), jnp.where(low_half, first, last)


def rim_tail(fields, low_half):
    sublanes = lax.broadcasted_iota(jnp.int32, (8, fields.shape[2]), 0)
    down = up = jnp.zeros(sublanes.shape, F32)
    for n in range(4):
        here = sublanes // 2 == n
        down = jnp.where(here, pltpu.roll(fields[n, :8, :], (2 * n + 2) % 8, 0), down)
        up = jnp.where(here, pltpu.roll(fields[n, 8:16, :], 2 * n, 0), up)
    return jnp.where(low_half, down, up), jnp.where(low_half, up, down)


def first_pack_kernel(
    bounds, misfit, visc, friction, ice, grounded, fields, levels, x_send,
    levels_in, visc_in, friction_in, ice_in, grounded_in, sems,
):
    copies = [
        pltpu.make_async_copy(source, target, sems.at[n])
        for n, (source, target) in enumerate((
            (misfit, fields.at[pl.ds(0, 2)]),
            (visc, visc_in),
            (ice, ice_in),
            (friction, friction_in),
            (grounded, grounded_in),
            (bounds, levels_in),
        ))
    ]
    for copy in copies:
        copy.start()
    low_half = lax.axis_index("gx") % 2 == 0
    for n in range(4):
        if n == 0:
            copies[0].wait()
        if n == 2:
            copies[1].wait()
            copies[2].wait()
            fields[2] = visc_in[...] * ice_in[...].astype(F32)
        if n == 3:
            copies[3].wait()
            copies[4].wait()
            fields[3] = friction_in[...] * grounded_in[...].astype(F32)
        x_send[8 * n : 8 * n + 8, :] = rim_rows(fields, n, low_half)[0]
    x_send[32:, :] = rim_tail(fields, low_half)[0]
    copies[5].wait()
    for n in range(4):
        levels[8 * n : 8 * n + 8, :] = jnp.full((8, LANES), levels_in[n])


def second_pack_kernel(fields, levels, x_send, coefficients, z_send, side_send, x_corner, z_corner):
    rows, cols = fields.shape[1:]
    left = lax.axis_index("gy") == 0
    position, last_position = lax.axis_index("gx"), lax.axis_size("gx") - 1
    low_half = position % 2 == 0
    at_end = (position == 0) | (position == last_position)
    for n in range(4):
        z_send[8 * n : 8 * n + 8, :] = jnp.where(at_end, 0.0, rim_rows(fields, n, low_half)[1])
        side_send[rows * n : rows * n + rows, :] = jnp.where(
            left, fields[n, :, cols - LANES :], fields[n, :, :LANES]
        )
    z_send[32:, :] = jnp.where(at_end, 0.0, rim_tail(fields, low_half)[1])
    sublanes = lax.broadcasted_iota(jnp.int32, (8, LANES), 0)
    own_columns_of = lane_ids() // EDGE == sublanes
    for source, target in ((x_send, x_corner), (z_send, z_corner)):
        packed = jnp.zeros((8, LANES), F32)
        for q in range(RIM // 2):
            last, first = source[8 * q : 8 * q + 8, cols - LANES :], source[8 * q : 8 * q + 8, :LANES]
            columns = jnp.where(
                left,
                pltpu.roll(last, EDGE, 1, stride=EDGE, stride_axis=0),
                pltpu.roll(first, 0, 1, stride=EDGE, stride_axis=0),
            )
            row = jnp.sum(jnp.where(own_columns_of, columns, 0.0), axis=0, keepdims=True)
            packed = jnp.where(sublanes == q, row, packed)
        target[...] = packed
    for sweep in range(2):
        lower, upper = levels[16 * sweep : 16 * sweep + 8, :], levels[16 * sweep + 8 : 16 * sweep + 16, :]
        middle = 0.5 * (upper + lower)
        half = 0.5 * (upper - lower)
        ratio = middle / half
        factor = 1.0 / ratio
        values = [1.0 / middle]
        for step in range(DEG - 1):
            factor_next = 1.0 / (2.0 * ratio - factor)
            values += [factor_next * factor, 2.0 * factor_next / half]
            factor = factor_next
        for n, value in enumerate(values):
            row = 8 * (sweep * (2 * DEG - 1) + n)
            coefficients[row : row + 8, :] = value


class Rows:
    def __init__(self, *pieces):
        self.pieces = pieces

    def place(self, row):
        for first, end, ref, start in self.pieces:
            if first <= row < end:
                return ref, slice(8 * (row - first + start), 8 * (row - first + start) + 8)
        raise IndexError(row)


def at(array, row):
    ref, place = array.place(row)
    return ref[place, :]


def put(array, row, value):
    ref, place = array.place(row)
    ref[place, :] = value


def to_left(value, shift):
    return pltpu.roll(value, LANES - shift, 1)


def to_right(value, shift):
    return pltpu.roll(value, shift, 1)


def spread(ref, base, height, left, side_block, target, first_row):
    blocks = [ref[base : base + height, LANES * j : LANES * j + LANES] for j in range(ref.shape[1] // LANES)]
    zero = jnp.zeros((height, LANES), F32)
    if side_block is None:
        blocks = [zero] + blocks + [zero]
    else:
        blocks = [jnp.where(left, zero, side_block)] + blocks + [jnp.where(left, side_block, zero)]
    lanes = lax.broadcasted_iota(jnp.int32, (height, LANES), 1)
    for s in range(SEGS):
        start = 96 * s - EDGE
        first = start // LANES
        offset = start - LANES * first
        merged = jnp.where(lanes >= offset, blocks[first + 1], blocks[first + 2])
        target[pl.ds(first_row * 8 + s, height, stride=8), :] = to_left(merged, offset)


def inside_columns(left, cols):
    column = 96 * lax.broadcasted_iota(jnp.int32, (8, LANES), 0) + lane_ids() - EDGE
    return jnp.where(left, (column >= 0).astype(F32), (column < cols).astype(F32))


def own_columns():
    lanes = lane_ids()
    return (lanes >= EDGE) & (lanes < LANES - EDGE)


def stiffness(visc, target, first, last, shift):
    paired = None
    for row in range(first, last + 1):
        k = at(visc, row)
        now = k + to_left(k, shift)
        if row > first:
            put(target, row - 1, 0.125 * (paired + now))
        paired = now


def edge_gradients(here, there):
    return here[0] + there[0], here[1] + there[1], there[0] - here[0], there[1] - here[1]


def cell_forces(s, one, two):
    a, b = two[0] - one[0], two[3] + one[3]
    c, d = two[2] + one[2], two[1] - one[1]
    both = a + b
    return s * (both + a), s * (both + b), (0.5 * s) * (c + d)


def forces(x, following, stiff, low, high):
    applied = {}
    def gradients(row):
        return edge_gradients([at(part, row) for part in x], [at(part, row) for part in following])

    here = gradients(low)
    before = cell_forces(at(stiff, low - 1), gradients(low - 1), here)
    for row in range(low, high):
        after = gradients(row + 1)
        now = cell_forces(at(stiff, row), here, after)
        shear, shear_step = before[2] + now[2], before[2] - now[2]
        normal_step, normal = before[0] - now[0], before[1] + now[1]
        applied[row] = (
            (normal_step - shear, normal_step + shear),
            (shear_step - normal, shear_step + normal),
        )
        here, before = after, now
    return applied


def remaining(n, value, f, beta, applied, row):
    return (at(f[n], row) - at(beta, row) * value) - (applied[row][n][0] + to_right(applied[row][n][1], 1))


def begin(x, following, f, coefficients, rows, shift):
    inverse = coefficients[:8, :]
    for row in rows:
        for n in range(2):
            value = at(f[n], row) * inverse
            put(x[n], row, value)
            put(following[n], row, to_left(value, shift))


def advance(levels, followings, f, beta, stiff, coefficients, step, spans, mask_of):
    keep = coefficients[8 + 16 * step : 16 + 16 * step, :]
    gain = coefficients[16 + 16 * step : 24 + 16 * step, :]
    gains = {}
    x, new = levels[step], levels[step + 1]
    applied = {}
    for low, high in spans:
        applied.update(forces(x, followings[step], stiff, low, high))
    for low, high in spans:
        for row in range(low, high):
            mask = mask_of(row)
            part = gains.setdefault(id(mask), gain * mask)
            for n in range(2):
                value = at(x[n], row)
                change = value if step == 0 else value - at(levels[step - 1][n], row)
                value = value + keep * change + part * remaining(n, value, f, beta, applied, row)
                put(new[n], row, value)
                put(followings[step + 1][n], row, to_left(value, 1))


def restrict(source, i, lanes, scale=None):
    row = DEG + 2 * i
    pair = at(source, row) + at(source, row + 1)
    if scale is not None:
        pair = scale * pair
    even, odd = lanes != "odd", lanes != "even"
    if even and odd:
        return jnp.where(lane_ids() % 2 == 0, pair + to_left(pair, 1), pair + to_right(pair, 1))
    return pair + (to_left(pair, 1) if even else to_right(pair, 1))


def pairs_of(refs):
    return [tuple(refs[n : n + 2]) for n in range(0, len(refs), 2)]


def middle_kernel(coefficients, fields, side, *refs):
    rows, cols = fields.shape[1:]
    end = RIM + rows
    left = lax.axis_index("gy") == 0
    outs = refs
    own, cell_ref, squares_out = outs[:4], outs[4], outs[5]
    level_refs, following_refs = pairs_of(outs[6 : 6 + 2 * DEG]), pairs_of(outs[6 + 2 * DEG : 6 + 4 * DEG])
    residual_refs, coarse_refs = outs[6 + 4 * DEG : 8 + 4 * DEG], outs[8 + 4 * DEG :]
    for n in range(4):
        for h in range(0, rows, 8):
            spread(fields.at[n], h, 8, left, side[rows * n + h : rows * n + h + 8, :], own[n], h)

    def whole_rows(ref):
        return Rows((RIM, end, ref, 0))

    f_u, f_v, visc, beta = (whole_rows(ref) for ref in own)
    f = (f_u, f_v)
    cell = whole_rows(cell_ref)
    levels = [tuple(map(whole_rows, pair)) for pair in level_refs]
    followings = [tuple(map(whole_rows, pair)) for pair in following_refs]
    inside = inside_columns(left, cols)
    stiffness(visc, cell, RIM, end - 1, 1)
    begin(levels[0], followings[0], f, coefficients, range(RIM, end), 1)
    for step in range(DEG - 1):
        span = (RIM + step + 1, end - step - 1)
        advance(levels, followings, f, beta, cell, coefficients, step, (span,), lambda row: inside)
    residual = tuple(map(whole_rows, residual_refs))
    low, high = RIM + DEG, end - DEG
    applied = forces(levels[-1], followings[-1], cell, low, high)
    squares = jnp.zeros((8, LANES), F32)
    for row in range(low, high):
        for n in range(2):
            value = inside * remaining(n, at(levels[-1][n], row), f, beta, applied, row)
            put(residual[n], row, value)
            squares = squares + value * value
    squares_out[...] = squares
    rim = (RIM - DEG) // 2
    coarse = [Rows((rim, rim + rows // 2, ref, 0)) for ref in coarse_refs]
    for i in range(rim, rim + rows // 2):
        put(coarse[0], i, restrict(visc, i, "both", 0.25))
        put(coarse[1], i, restrict(beta, i, "both"))
        if low <= DEG + 2 * i < high:
            put(coarse[2], i, restrict(residual[0], i, "both"))
            put(coarse[3], i, restrict(residual[1], i, "both"))


def main_kernel(coefficients, fields, velocity, from_x, from_z, side_x, side_z, middle, outs, scratch):
    multiplier, gradient, sums = outs
    scratch = list(scratch)
    rows, cols = gradient.shape
    total, end = rows + 2 * RIM, RIM + rows
    gx_at, gx_size = lax.axis_index("gx"), lax.axis_size("gx")
    low_half = gx_at % 2 == 0
    left = lax.axis_index("gy") == 0
    own, cell_ref, squares_ref = middle[:4], middle[4], middle[5]
    level_refs, following_refs = pairs_of(middle[6 : 6 + 2 * DEG]), pairs_of(middle[6 + 2 * DEG : 6 + 4 * DEG])
    residual_refs, coarse_refs = middle[6 + 4 * DEG : 8 + 4 * DEG], middle[8 + 4 * DEG :]

    def take(count):
        taken = scratch[:count]
        del scratch[:count]
        return taken

    rims = take(4)
    tails = take(1)[0]
    joint = [Rows((0, rows, ref, 0)) for ref in take(2)]
    for received, partner, corner, is_above in (
        (from_x, side_x, take(1)[0], jnp.logical_not(low_half)),
        (from_z, side_z, take(1)[0], low_half),
    ):
        first_row = jnp.where(is_above, 0, 8)
        rolled = [to_left(partner[...], EDGE * i) if i else partner[...] for i in range(8)]
        for i in range(8):
            corner[pl.ds(i, 8, stride=8), :] = jnp.where(left, rolled[i], rolled[(i + 1) % 8])
        for n, target in enumerate((*rims, tails)):
            spread(received, 8 * n, 8, left, corner[8 * n : 8 * n + 8, :], target, first_row)

    def joined(full, ref, margin):
        return Rows(
            (0, RIM + margin, full, 0),
            (RIM + margin, end - margin, ref, margin),
            (end - margin, total, full, end - margin),
        )

    f_u, f_v, visc, beta = (
        Rows(
            (0, RIM - 8, tails, 2 * n),
            (RIM - 8, RIM, rims[n], 0),
            (RIM, end, own[n], 0),
            (end, end + 8, rims[n], 8),
            (end + 8, total, tails, 8 + 2 * n),
        )
        for n in range(4)
    )
    f = (f_u, f_v)
    cell_full = take(1)[0]
    cell = Rows((0, RIM, cell_full, 0), (RIM, end - 1, cell_ref, 0), (end - 1, total, cell_full, end - 1))
    levels = [tuple(joined(take(1)[0], ref, n) for ref in pair) for n, pair in enumerate(level_refs)]
    followings = [tuple(joined(take(1)[0], ref, n) for ref in pair) for n, pair in enumerate(following_refs)]

    inside = inside_columns(left, cols)
    above = inside * jnp.where(gx_at > 0, 1.0, 0.0)
    below = inside * jnp.where(gx_at < gx_size - 1, 1.0, 0.0)

    def mask_of(row):
        return above if row < RIM else below if row >= end else inside

    stiffness(visc, cell, 0, RIM, 1)
    stiffness(visc, cell, end - 1, total - 1, 1)
    begin(levels[0], followings[0], f, coefficients, [*range(RIM), *range(end, total)], 1)
    even = lane_ids() % 2 == 0
    coarse_rim = (RIM - DEG) // 2
    half = rows // 4
    count = half + 2 * coarse_rim

    def plain():
        return Rows((0, count, take(1)[0], 0))

    def packed(make, ref, margin):
        first, last = coarse_rim + margin, coarse_rim + 2 * half - margin
        target = plain()
        for j in range(count):
            i, k = j, j + half
            one = at(Rows((first, last, ref, margin)), i) if first <= i < last else make(i, "even")
            two = at(Rows((first, last, ref, margin)), k) if first <= k < last else make(k, "odd")
            put(target, j, jnp.where(even, one, two))
        return target

    c_visc = packed(lambda i, lanes: restrict(visc, i, lanes, 0.25), coarse_refs[0], 0)
    c_beta = packed(lambda i, lanes: restrict(beta, i, lanes), coarse_refs[1], 0)
    masks = [
        jnp.where(even, above if j < coarse_rim else inside, below if j >= count - coarse_rim else inside)
        for j in range(count)
    ]
    stiff, stiff_before = plain(), plain()
    stiffness(c_visc, stiff, 0, count - 1, 2)
    for row in range(count - 1):
        put(stiff_before, row, to_right(at(stiff, row), 2))
    for step in range(DEG - 1):
        spans = ((step + 1, RIM + step + 1), (end - step - 1, total - step - 1))
        advance(levels, followings, f, beta, cell, coefficients, step, spans, mask_of)
    x = levels[-1]
    squares = squares_ref[...]
    bases, others = {}, {}
    for low, high in ((DEG, RIM + DEG), (end - DEG, total - DEG)):
        applied = forces(x, followings[-1], cell, low, high)
        for row in range(low, high):
            for n in range(2):
                here, other = applied[row][n]
                bases[n, row] = (at(f[n], row) - at(beta, row) * at(x[n], row)) - here
                others[n, row] = other
                if RIM <= row < end:
                    value = inside * (bases[n, row] - to_right(other, 1))
                    squares = squares + value * value

    def restrict_residual(n, i, lanes):
        row = DEG + 2 * i
        base, other = (part[n, row] + part[n, row + 1] for part in (bases, others))
        if lanes == "even":
            value = (base - other) + (to_left(base, 1) - to_right(other, 1))
        else:
            value = base + (to_right(base - other, 1) - to_right(other, 2))
        return mask_of(row) * value

    c_f = [packed(functools.partial(restrict_residual, n), coarse_refs[n + 2], DEG // 2) for n in range(2)]
    table = 8 * (2 * DEG - 1)

    def gradients(here):
        after = [to_left(value, 2) for value in here]
        before = [to_right(value, 2) for value in here]
        return edge_gradients(here, after), edge_gradients(before, here)

    def cells(row, one, two):
        return [cell_forces(at(s, row), p, q) for s, p, q in zip((stiff, stiff_before), one, two)]

    inverse = coefficients[table : table + 8, :]
    c_x = [[at(part, row) * inverse for part in c_f] for row in range(count)]
    c_old = c_x
    for step in range(DEG - 1):
        keep = coefficients[table + 8 + 16 * step : table + 16 + 16 * step, :]
        gain = coefficients[table + 16 + 16 * step : table + 24 + 16 * step, :]
        low, high = step + 1, count - step - 1
        edges = {row: gradients(c_x[row]) for row in range(low - 1, high + 1)}
        forces_at = {row: cells(row, edges[row], edges[row + 1]) for row in range(low - 1, high)}
        c_new = list(c_x)
        for row in range(low, high):
            (xx0, yy0, xy0), (xx1, yy1, xy1) = (
                (p[0] - q[0], p[1] + q[1], (p[2] + q[2], p[2] - q[2]))
                for p, q in zip(forces_at[row - 1], forces_at[row])
            )
            applied = ((xx0 - xy0[0]) + (xx1 + xy1[0]), (xy0[1] - yy0) + (xy1[1] + yy1))
            part = gain * masks[row]
            c_new[row] = []
            for n in range(2):
                value = c_x[row][n]
                change = value if step == 0 else value - c_old[row][n]
                left_over = (at(c_f[n], row) - at(c_beta, row) * value) - applied[n]
                c_new[row].append(value + keep * change + part * left_over)
        c_x, c_old = c_new, c_x

    lanes = lane_ids()
    for i in range(half):
        for n in range(2):
            value = c_x[coarse_rim + i][n]
            corrections = jnp.where(even, value, to_right(value, 1)), jnp.where(even, to_left(value, 1), value)
            for first, correction in zip((2 * i, 2 * (i + half)), corrections):
                for row in (first, first + 1):
                    put(joint[n], row, at(x[n], RIM + row) + correction)

    gradient_squares = jnp.zeros((8, LANES), F32)
    for h in range(0, rows, 8):
        for j in range(cols // LANES):
            s = (LANES * j) // 96
            shift = LANES * j - 96 * s + EDGE
            border = 96 * (s + 1) - LANES * j
            columns = slice(LANES * j, LANES * j + LANES)
            product = None
            for n in range(2):
                source = joint[n].pieces[0][2]
                one = source[pl.ds(8 * h + s, 8, stride=8), :]
                two = source[pl.ds(8 * h + s + 1, 8, stride=8), :]
                value = jnp.where(lanes < border, to_left(one, shift), to_right(two, (96 - shift) % LANES))
                multiplier[n, h : h + 8, columns] = value
                term = velocity[n, h : h + 8, columns] * value
                product = term if product is None else product + term
            value = -fields[3, h : h + 8, columns] * product
            gradient[h : h + 8, columns] = value
            gradient_squares = gradient_squares + value * value
    pair = [jnp.sum(value, axis=0, keepdims=True) for value in (jnp.where(own_columns(), squares, 0.0), gradient_squares)]
    sums[...] = jnp.broadcast_to(jnp.concatenate(pair, axis=1), sums.shape)


def scale_kernel(nodes, gathered, gradient, held_multiplier, scaled, norm, multiplier, scaled_out, norm_out, sems):
    copies = [
        pltpu.make_async_copy(source, target, sems.at[n])
        for n, (source, target) in enumerate(((held_multiplier, multiplier), (norm_out, norm), (scaled_out, scaled)))
    ]
    copies[0].start()
    residual_total = jnp.sum(gathered[:, :LANES], keepdims=True)
    gradient_total = jnp.sum(gathered[:, LANES:], keepdims=True)
    norm_out[...] = jnp.sqrt(residual_total / (2 * nodes))
    copies[1].start()
    scaled_out[...] = gradient[...] / jnp.sqrt(gradient_total / nodes + 1e-06)
    copies[2].start()
    for copy in copies:
        copy.wait()


def body(misfit, velocity, viscosity, friction, ice, grounded, bounds):
    rows, cols = viscosity.shape
    gx_size, gy_size = lax.axis_size("gx"), lax.axis_size("gy")
    assert gy_size == 2 and gx_size % 2 == 0 and cols == 96 * SEGS and rows == 16
    peers = gx_size * gy_size
    nodes = rows * cols * peers
    total = rows + 2 * RIM
    shaped = jax.ShapeDtypeStruct
    whole = pl.BlockSpec(memory_space=pltpu.VMEM)
    params = pltpu.CompilerParams(vmem_limit_bytes=32 * 1024 * 1024)

    held = pl.BlockSpec(memory_space=pltpu.HBM)
    inputs = (bounds, misfit, viscosity, friction, ice, grounded)
    fields, levels, x_send = pl.pallas_call(
        first_pack_kernel,
        out_shape=(shaped((4, rows, cols), F32), shaped((32, LANES), F32), shaped((4 * RIM, cols), F32)),
        in_specs=[held] * 6,
        out_specs=[whole] * 3,
        scratch_shapes=[
            pltpu.SMEM((4,), F32),
            pltpu.VMEM((rows, cols), F32),
            pltpu.VMEM((rows, cols), F32),
            pltpu.VMEM((rows, cols), jnp.int32),
            pltpu.VMEM((rows, cols), jnp.int32),
            pltpu.SemaphoreType.DMA((6,)),
        ],
        compiler_params=params,
        name="first_pack",
    )(*(pltpu.with_memory_space_constraint(x, pltpu.HBM) for x in inputs))
    coefficients, z_send, side_send, x_corner, z_corner = pl.pallas_call(
        second_pack_kernel,
        out_shape=(
            shaped((16 * (2 * DEG - 1), LANES), F32),
            shaped((4 * RIM, cols), F32),
            shaped((4 * rows, LANES), F32),
            shaped((8, LANES), F32),
            shaped((8, LANES), F32),
        ),
        in_specs=[whole] * 3,
        out_specs=[whole] * 5,
        compiler_params=params,
        name="second_pack",
    )(fields, levels, x_send)

    x_pairs = [(i, i ^ 1) for i in range(gx_size)]
    z_pairs = [(2 * i + c, 2 * j + c) for i in range(1, gx_size - 1) for j in (i + 1 if i % 2 else i - 1,) for c in (0, 1)]
    z_pairs += [(2 * i + c, 2 * i + 1 - c) for i in (0, gx_size - 1) for c in (0, 1)]
    swap = [(0, 1), (1, 0)]
    from_x = lax.ppermute(x_send, "gx", x_pairs)
    from_z = lax.ppermute(z_send, AXES, z_pairs)
    side = lax.ppermute(side_send, "gy", swap)
    side_x = lax.ppermute(x_corner, AXES, [(2 * i + c, 2 * j + 1 - c) for i, j in x_pairs for c in (0, 1)])
    side_z = lax.ppermute(z_corner, AXES, [(i, j ^ 1 if 1 < i < 2 * gx_size - 2 else j) for i, j in z_pairs])

    fine = pltpu.VMEM((8 * total, LANES), F32)
    coarse = pltpu.VMEM((4 * total, LANES), F32)
    owned = pltpu.VMEM((8 * rows, LANES), F32)
    halved = pltpu.VMEM((4 * rows, LANES), F32)
    middle = pl.pallas_call(
        middle_kernel,
        out_shape=[owned] * 5 + [pltpu.VMEM((8, LANES), F32)] + [owned] * (4 * DEG + 2) + [halved] * 4,
        in_specs=[whole] * 3,
        out_specs=[whole] * (12 + 4 * DEG),
        compiler_params=params,
        name="middle",
    )(coefficients, fields, side)

    def leg_kernel(coefficients, fields, velocity, from_x, from_z, side_x, side_z, *refs):
        done, refs = refs[: len(middle)], refs[len(middle) :]
        main_kernel(coefficients, fields, velocity, from_x, from_z, side_x, side_z, done, refs[:3], refs[3:])

    rim = pltpu.VMEM((8 * 16, LANES), F32)
    corner = pltpu.VMEM((8 * 8, LANES), F32)
    held_multiplier, gradient, sums = pl.pallas_call(
        leg_kernel,
        out_shape=(
            pltpu.VMEM((2, rows, cols), F32),
            pltpu.VMEM((rows, cols), F32),
            shaped((peers, 2 * LANES), F32),
        ),
        in_specs=[whole] * (7 + len(middle)),
        out_specs=[whole] * 3,
        scratch_shapes=[rim] * 5 + [owned] * 2 + [corner] * 2 + [fine] * (1 + 4 * DEG) + [coarse] * 14,
        compiler_params=params,
        name="leg",
    )(coefficients, fields, velocity, from_x, from_z, side_x, side_z, *middle)

    gathered = lax.all_to_all(sums, AXES, 0, 0, tiled=True)
    scaled, norm, multiplier = pl.pallas_call(
        functools.partial(scale_kernel, nodes),
        out_shape=(
            pltpu.HBM((rows, cols), F32),
            pltpu.HBM((1, 1), F32),
            pltpu.HBM((2, rows, cols), F32),
        ),
        in_specs=[whole] * 3,
        out_specs=[held] * 3,
        scratch_shapes=[
            pltpu.VMEM((rows, cols), F32),
            pltpu.VMEM((1, 1), F32),
            pltpu.SemaphoreType.DMA((3,)),
        ],
        compiler_params=params,
        name="scale",
    )(gathered, gradient, held_multiplier)
    return multiplier, scaled, norm.reshape(1)


def solution(mesh):
    tile = P(("grp", "gx"), "gy")
    pair = P(None, ("grp", "gx"), "gy")
    return jax.shard_map(
        body,
        mesh=mesh,
        in_specs=(pair, pair, tile, tile, tile, tile, P("grp")),
        out_specs=(pair, tile, P("grp")),
        check_vma=False,
    )
```
